32 devices in a mesh: ep: 16 (over z, y, x), dp: 2 (over core).
Axes of the slice: x: 2, y: 2, z: 4, core: 2. Of those that a mesh axis runs over, the one named last changes fastest.
Arguments:
- patches: bfloat16 [32768, 768], P(('ep', 'dp')), may hold values from -6 to 6
- labels: int32 [32768, 256], P(('ep', 'dp')), may hold values from 0 to 39
- pixel_mask: int32 [32768, 256], P(('ep', 'dp')), may hold values from 0 to 1
- patch_valid: int32 [32768], P(('ep', 'dp')), may hold values from 0 to 1, as said below
- tasks: int32 [32], P(('ep', 'dp')), may hold values from 0 to 3
- routes: int32 [32768, 4], P(('ep', 'dp')), may hold values from 0 to 15, all different within a row; in each aligned block of 1024 rows (0 to 1023, 1024 to 2047, ...) at most 384 rows name the same one
- dense_weight: float32 [4468992], P('ep'), may hold values from -2 to 2
- dense_first: float32 [4468992], P('ep'), may hold values from -5.722046e-06 to 5.722046e-06
- dense_second: float32 [4468992], P('ep'), may hold values from 1.7135494e-13 to 6.8541977e-13
- dense_average: float32 [4468992], P('ep'), may hold values from -2 to 2
- expert_in: float32 [16, 384, 1536], P('ep', None, 'dp'), may hold values from -0.3125 to 0.3125
- in_first: float32 [16, 384, 1536], P('ep', None, 'dp'), may hold values from -5.722046e-06 to 5.722046e-06
- in_second: float32 [16, 384, 1536], P('ep', None, 'dp'), may hold values from 1.0709684e-14 to 4.2838735e-14
- in_average: float32 [16, 384, 1536], P('ep', None, 'dp'), may hold values from -0.3125 to 0.3125
- expert_out: float32 [16, 1536, 384], P('ep', 'dp'), may hold values from -0.15625 to 0.15625
- out_first: float32 [16, 1536, 384], P('ep', 'dp'), may hold values from -5.722046e-06 to 5.722046e-06
- out_second: float32 [16, 1536, 384], P('ep', 'dp'), may hold values from 1.7135494e-13 to 6.8541977e-13
- out_average: float32 [16, 1536, 384], P('ep', 'dp'), may hold values from -0.15625 to 0.15625
Outputs:
- loss: float32 [1], replicated
- grad_norm: float32 [1], replicated
- block_norms: float32 [46, 2], replicated
- dense_new: float32 [4468992], P('ep')
- dense_first_new: float32 [4468992], P('ep')
- dense_second_new: float32 [4468992], P('ep')
- dense_average_new: float32 [4468992], P('ep')
- dense_low: bfloat16 [4468992], P('ep')
- in_new: float32 [16, 384, 1536], P('ep', None, 'dp')
- in_first_new: float32 [16, 384, 1536], P('ep', None, 'dp')
- in_second_new: float32 [16, 384, 1536], P('ep', None, 'dp')
- in_average_new: float32 [16, 384, 1536], P('ep', None, 'dp')
- in_low: bfloat16 [16, 384, 1536], P('ep', None, 'dp')
- out_new: float32 [16, 1536, 384], P('ep', 'dp')
- out_first_new: float32 [16, 1536, 384], P('ep', 'dp')
- out_second_new: float32 [16, 1536, 384], P('ep', 'dp')
- out_average_new: float32 [16, 1536, 384], P('ep', 'dp')
- out_low: bfloat16 [16, 1536, 384], P('ep', 'dp')
The draws below stay inside these ranges and needn't reach their ends.
Inputs may be any that keep to these rules, and one draw needn't show every extreme that they name: `routes`: in the rows of one device each expert is named by at most 384 choices, a bound that some block reaches. `patch_valid`: the valid slots of an image are its first 392 or all 1024; both kinds occur.
All inputs are finite; a program needn't handle non-finite values.
Results may differ from the reference program's by a relative error of at most 0.0055.
The reference program's roundings to bfloat16 on the way count: a program that leaves them out, or rounds other values in their place, can miss the bound.
Values may be sent and summed in bfloat16 or wider, within the bound.
No kernel may reach another device: no remote copies, remote signals or barrier semaphores. Data moves between devices by JAX's collectives and lax.ppermute only.
A program may use at most 384 MiB of HBM per device.

```python
import math
import jax
import jax.numpy as jnp
import numpy as np
from jax import lax

D = 384
HEADS = 6
HD = 64
FF = 1536
EH = 1536
TOP = 4
C = 40
PIX = 768
PP = 256
TASKS = 4
SEQ = 1024
SHORT = 392
EXPERTS = 16
REPL = 1
PIECE = 1536
CAP = 384
TOKENS = 32768
IMAGES = 32
NDENSE = 4468992
N_EP = 16
N_DP = 2


def dense_law(key):
    sizes = [PIX * D] + [3 * D * D] * 3 + [D * D] * 3 + [D * FF] * 2 + [FF * D] * 2 + [TASKS * D * EXPERTS, D * C, 7 * D, 7 * D]
    spreads = [PIX ** (-0.5)] + [D ** (-0.5)] * 3 + [4.0 * D ** (-0.5)] * 3 + [D ** (-0.5)] * 2 + [FF ** (-0.5)] * 2 + [0.5 * D ** (-0.5), 2.0 * D ** (-0.5), 0.1, 0.1]
    centers = [0.0] * 13 + [1.0, 0.0]
    index = jnp.arange(NDENSE, dtype=jnp.int32)
    spread = jnp.zeros((NDENSE,), jnp.float32)
    center = jnp.zeros((NDENSE,), jnp.float32)
    start = 0
    for size, width, middle in zip(sizes, spreads, centers):
        inside = (index >= start) & (index < start + size)
        spread = jnp.where(inside, width, spread)
        center = jnp.where(inside, middle, center)
        start += size
    noise = jnp.clip(jax.random.normal(key, (NDENSE,), jnp.float32), -6.0, 6.0)
    return (center + spread * noise).astype(jnp.float32)


def draw_dense_weight(key, part):
    return dense_law(jax.random.fold_in(key, 11))


def draw_dense_average(key, part):
    return dense_law(jax.random.fold_in(key, 12))


def draw_pixel_mask(key, part):
    rows = jnp.arange(TOKENS, dtype=jnp.int32)[:, None]
    level = 250 + 500 * rows // TOKENS
    return (jax.random.randint(jax.random.fold_in(key, 13), (TOKENS, PP), 0, 1000) < level).astype(jnp.int32)


def draw_patch_valid(key, part):
    images = TOKENS // SEQ
    kind = jax.random.randint(jax.random.fold_in(key, 1), (images,), 0, 2)
    full = jax.random.randint(jax.random.fold_in(key, 2), (), 0, images)
    short = (full + 1 + jax.random.randint(jax.random.fold_in(key, 3), (), 0, images - 1)) % images
    kind = kind.at[full].set(1).at[short].set(0)
    length = jnp.where(kind > 0, SEQ, SHORT)
    position = jnp.arange(SEQ, dtype=jnp.int32)
    return (position[None, :] < length[:, None]).astype(jnp.int32).reshape(TOKENS)


def place_ends(drawn, key, least, largest):
    place = [jax.random.randint(jax.random.fold_in(key, axis), (), 0, length) for axis, length in enumerate(drawn.shape)]
    widest = drawn.shape.index(max(drawn.shape))
    beside = place[:widest] + [(place[widest] + 1) % drawn.shape[widest]] + place[widest + 1:]
    return drawn.at[tuple(place)].set(least).at[tuple(beside)].set(largest)


def level_of(stream_key, extent, cuts, smallest, high):
    def one(dim, blocks):
        steps = jax.random.uniform(jax.random.fold_in(jax.random.fold_in(stream_key, 6), dim), (blocks,), jnp.float32, smallest / len(cuts), high / len(cuts))
        return jnp.repeat(jnp.exp(steps), extent[dim] // blocks).reshape((-1,) + (1,) * (len(extent) - dim - 1))

    loudness = one(*cuts[0])
    for cut in cuts[1:]:
        loudness = loudness * one(*cut)
    return loudness


def routed_block(rng, own, number, rows, amount, top, bound, lean):
    order = jax.random.permutation(rng, amount)
    heavy_load, ordinary = load_shares(amount, rows * top, bound, lean, True), load_shares(amount, rows * top, bound, lean, False)
    places = jnp.arange(amount)

    def named(tallies, turn):
        used = int((tallies > 0).sum())
        fixed = max(1, used // 4)
        moved = fixed + (places - fixed + turn * (used - fixed)) % max(1, amount - fixed)
        return jnp.zeros((amount,), jnp.int32).at[order[jnp.where(places < fixed, places, moved)]].set(jnp.asarray(tallies, jnp.int32))

    tallies = jnp.where(number % 4 == 0, named(heavy_load, number // 4), named(ordinary, number - number // 4 - 1))
    mixed = jax.random.permutation(jax.random.fold_in(own, 3), amount)
    giver, sink = mixed[0:amount // 2 * 2:2], mixed[1:amount // 2 * 2:2]
    room = jnp.minimum(tallies[giver] - 1, bound - tallies[sink]) // 2
    room = jnp.where((giver == order[0]) | (sink == order[0]) | (tallies[sink] == 0), 0, jnp.maximum(room, 0))
    moved = jax.random.randint(jax.random.fold_in(own, 4), (amount // 2,), 0, 1 << 20) % (room + 1)
    tallies = tallies.at[giver].add(-moved).at[sink].add(moved)
    items = jnp.searchsorted(jnp.cumsum(tallies), jnp.arange(rows * top), side="right").astype(jnp.int32)
    table = items.reshape(top, rows).T
    table = table[jax.random.permutation(jax.random.fold_in(own, 1), rows)]
    turn = jax.random.randint(jax.random.fold_in(own, 2), (rows, 1), 0, top)
    return jnp.take_along_axis(table, (jnp.arange(top)[None, :] + turn) % top, axis=1)


def load_shares(amount, total, bound, skew, full):
    loads = [(1 << 20) // math.isqrt(grade ** skew) + 1 for grade in range(1, amount + 1)]
    largest = bound if full else min(bound, max(-(-total // amount), total * loads[0] // sum(loads)))
    least = 1 if total - largest >= amount - 1 else 0
    holding, spare = [largest] + [least] * (amount - 1), total - largest - least * (amount - 1)
    while spare > 0:
        movable = [i for i in range(1, amount) if holding[i] < largest] or [i for i in range(1, amount) if holding[i] < bound]
        mass, budget = sum([loads[i] for i in movable]), spare
        for i in movable:
            more = min(bound - holding[i], max(1, budget * loads[i] // mass), spare)
            holding[i] = holding[i] + more
            spare = spare - more
    return np.array(holding)


def gaussian(own_key, shape, scale, reach, cuts=(), held_as=jnp.bfloat16):
    entries = scale * jax.random.normal(own_key, shape, jnp.float32)
    if cuts:
        entries = entries * level_of(own_key, shape, cuts, -0.22, 0.18)
    return jnp.clip(entries, -reach, reach).astype(held_as)


def setup_inputs(seed: int = 0) -> dict:
    arg_keys = jax.random.split(jax.random.key(seed), 19)
    patches = gaussian(arg_keys[0], (TOKENS, PIX), 1.0, 6.0, ((0, 32),))
    labels = place_ends(jax.random.randint(arg_keys[1], (TOKENS, PP), 0, C), jax.random.fold_in(arg_keys[1], 1), 0, C - 1).astype(jnp.int32)
    pixel_mask = draw_pixel_mask(jax.random.fold_in(arg_keys[18], 71), 0)
    patch_valid = draw_patch_valid(jax.random.fold_in(arg_keys[18], 71), 0)
    tasks = place_ends(jax.random.randint(arg_keys[4], (IMAGES,), 0, TASKS), jax.random.fold_in(arg_keys[4], 1), 0, TASKS - 1).astype(jnp.int32)
    routes_keys = jax.random.split(jax.random.fold_in(arg_keys[5], 1), TOKENS // SEQ)
    routes_turns = jax.random.permutation(jax.random.fold_in(arg_keys[5], 3), TOKENS // SEQ)
    routes = jax.vmap(lambda own, number: routed_block(jax.random.fold_in(arg_keys[5], 2), own, number, SEQ, EXPERTS, TOP, CAP, 2))(routes_keys, routes_turns).reshape((TOKENS, TOP))
    dense_weight = draw_dense_weight(jax.random.fold_in(arg_keys[18], 71), 0)
    dense_first = gaussian(arg_keys[7], (NDENSE,), (0.002 * (NDENSE + 2 * EXPERTS * D * EH) ** -0.5), 5.7220458984375e-06, ((0, 16),), jnp.float32)
    dense_second = jnp.clip(jnp.exp(math.log(6.85419765649592e-13) - 1.3862944 * jax.random.uniform(arg_keys[8], (NDENSE,), jnp.float32) ** level_of(arg_keys[8], (NDENSE,), ((0, 16),), -0.2, 0.2)), 1.71354941412398e-13, 6.85419765649592e-13)
    dense_average = draw_dense_average(jax.random.fold_in(arg_keys[18], 71), 0)
    expert_in = gaussian(arg_keys[10], (N_EP, D, PIECE), D ** -0.5, 0.3125, ((0, 16), (2, 2)), jnp.float32)
    in_first = gaussian(arg_keys[11], (N_EP, D, PIECE), (0.002 * (NDENSE + 2 * EXPERTS * D * EH) ** -0.5), 5.7220458984375e-06, ((0, 16), (2, 2)), jnp.float32)
    in_second = jnp.clip(jnp.exp(math.log(4.28387353530995e-14) - 1.3862944 * jax.random.uniform(arg_keys[12], (N_EP, D, PIECE), jnp.float32) ** level_of(arg_keys[12], (N_EP, D, PIECE), ((0, 16), (2, 2)), -0.2, 0.2)), 1.0709683838274874e-14, 4.28387353530995e-14)
    in_average = gaussian(arg_keys[13], (N_EP, D, PIECE), D ** -0.5, 0.3125, ((0, 16), (2, 2)), jnp.float32)
    expert_out = gaussian(arg_keys[14], (N_EP, PIECE, D), EH ** -0.5, 0.15625, ((0, 16), (1, 2)), jnp.float32)
    out_first = gaussian(arg_keys[15], (N_EP, PIECE, D), (0.002 * (NDENSE + 2 * EXPERTS * D * EH) ** -0.5), 5.7220458984375e-06, ((0, 16), (1, 2)), jnp.float32)
    out_second = jnp.clip(jnp.exp(math.log(6.85419765649592e-13) - 1.3862944 * jax.random.uniform(arg_keys[16], (N_EP, PIECE, D), jnp.float32) ** level_of(arg_keys[16], (N_EP, PIECE, D), ((0, 16), (1, 2)), -0.2, 0.2)), 1.71354941412398e-13, 6.85419765649592e-13)
    out_average = gaussian(arg_keys[17], (N_EP, PIECE, D), EH ** -0.5, 0.15625, ((0, 16), (1, 2)), jnp.float32)
    return dict(patches=patches, labels=labels, pixel_mask=pixel_mask, patch_valid=patch_valid, tasks=tasks, routes=routes, dense_weight=dense_weight, dense_first=dense_first, dense_second=dense_second, dense_average=dense_average, expert_in=expert_in, in_first=in_first, in_second=in_second, in_average=in_average, expert_out=expert_out, out_first=out_first, out_second=out_second, out_average=out_average)


@jax.custom_vjp
def low(v):
    return lax.optimization_barrier(v.astype(jnp.bfloat16)).astype(jnp.float32)

@jax.custom_vjp
def low_back(v):
    return v

def low_keep(v):
    return (low(v), None)

def low_pass(kept, grad):
    return (grad,)

def back_keep(v):
    return (v, None)

def back_low(kept, grad):
    return (low(grad),)
low.defvjp(low_keep, low_pass)
low_back.defvjp(back_keep, back_low)
HIGH = lax.Precision.HIGHEST
EPS_NORM = 1e-05
CLIP_NORM = 0.002
RATE = 0.3
DECAY_ONE = 0.5
DECAY_TWO = 0.5
WEIGHT_DECAY = 0.01
EPS_ADAM = 1e-09
AVERAGE = 0.9
SCALE = 0.125

def product(left, right):
    return jnp.dot(left, right, precision=HIGH)

def shapes():
    return [(PIX, D), (3, D, 3 * D), (3, D, D), (2, D, FF), (2, FF, D), (TASKS, D, EXPERTS), (D, C), (2, 7, D)]

def unpack(flat):
    pieces = []
    start = 0
    for shape in shapes():
        count = math.prod(shape)
        pieces.append(flat[start:start + count].reshape(shape))
        start += count
    return pieces

def blocks_of(flat, first, second):
    parts = unpack(flat)
    listed = [parts[0]] + [parts[1][i] for i in range(3)] + [parts[2][i] for i in range(3)]
    listed = listed + [parts[3][i] for i in range(2)] + [parts[4][i] for i in range(2)] + [parts[5], parts[6], parts[7]]
    first_rows = first.reshape(EXPERTS, -1)
    second_rows = second.reshape(EXPERTS, -1)
    return listed + [first_rows[e] for e in range(EXPERTS)] + [second_rows[e] for e in range(EXPERTS)]

def segment_sizes():
    return [PIX * D] + [3 * D * D] * 3 + [D * D] * 3 + [D * FF] * 2 + [FF * D] * 2 + [TASKS * D * EXPERTS, D * C, 14 * D]

def layer_norm(x, gain, bias):
    mean = lax.optimization_barrier(jnp.mean(x, -1, keepdims=True))
    cent = x - mean
    var = lax.optimization_barrier(jnp.mean(cent * cent, -1, keepdims=True))
    return cent * lax.rsqrt(var + EPS_NORM) * gain + bias

def gelu(h):
    return jax.nn.gelu(h, approximate=False)

def attend(item):
    qkv, valid = item
    parts = qkv.reshape(SEQ, 3, HEADS, HD)
    scores = jnp.einsum('qhd,khd->hqk', parts[:, 0], parts[:, 1], precision=HIGH) * SCALE
    scores = jnp.where(valid[None, None, :] > 0, low_back(scores), -1e+30)
    probs = low(jax.nn.softmax(scores, axis=-1))
    return jnp.einsum('hqk,khd->qhd', probs, parts[:, 2], precision=HIGH).reshape(SEQ, D)

def mixture(c, w_router, ein, eout, task_tok, routes):
    every = jnp.einsum('td,sde->tse', c, w_router, precision=HIGH)
    logits = low_back(jnp.take_along_axis(every, task_tok[:, None, None], axis=1)[:, 0])
    picked = jnp.take_along_axis(logits, routes, axis=1)
    gates = jax.nn.softmax(picked, axis=-1).reshape(-1)
    flat = routes.reshape(-1)
    most = N_EP * N_DP * CAP

    def step(total, expert):
        chosen = flat == expert
        index = jnp.nonzero(chosen, size=most, fill_value=0)[0]
        live = (jnp.arange(most) < jnp.sum(chosen)).astype(jnp.float32)
        token = index // TOP
        rows = low_back(c[token])
        hidden = low_back(product(rows, ein[expert]))
        out = low(low_back(product(low(gelu(hidden)), eout[expert])))
        return (total.at[token].add((gates[index] * live)[:, None] * out), None)
    total, _ = lax.scan(jax.checkpoint(step), jnp.zeros_like(c), jnp.arange(EXPERTS))
    return total

def forward(dense_flat, expert_in, expert_out, patches, valid, task_tok, routes, count_tok, counts, total):
    w_patch, w_qkv, w_attn, w_up, w_down, w_router, w_head, norms = unpack(low(dense_flat))
    ein = low(expert_in).reshape(EXPERTS, REPL, D, PIECE).transpose(0, 2, 1, 3).reshape(EXPERTS, D, EH)
    eout = low(expert_out).reshape(EXPERTS, EH, D)
    x = low_back(product(patches, w_patch))
    for layer in range(3):
        a = low(layer_norm(x, norms[0, 2 * layer], norms[1, 2 * layer]))
        qkv = low(low_back(product(a, w_qkv[layer])))
        out = lax.map(jax.checkpoint(attend), (qkv.reshape(-1, SEQ, 3 * D), valid.reshape(-1, SEQ)))
        out = low(low_back(out.reshape(TOKENS, D)))
        x = x + low_back(product(out, w_attn[layer]))
        c = low(layer_norm(x, norms[0, 2 * layer + 1], norms[1, 2 * layer + 1]))
        if layer == 1:
            x = x + mixture(c, w_router, ein, eout, task_tok, routes)
        else:
            hidden = low_back(product(c, w_up[layer // 2]))
            x = x + low_back(product(low(gelu(hidden)), w_down[layer // 2]))
    f = low(layer_norm(x, norms[0, 6], norms[1, 6]))
    logits = low_back(product(f, w_head))
    lse = jax.scipy.special.logsumexp(logits, axis=-1)
    return (jnp.sum(count_tok * lse) - jnp.sum(counts * logits)) / total

def reference(patches, labels, pixel_mask, patch_valid, tasks, routes, dense_weight, dense_first, dense_second, dense_average, expert_in, in_first, in_second, in_average, expert_out, out_first, out_second, out_average):
    images = TOKENS // SEQ
    weight_pix = (pixel_mask * patch_valid[:, None]).astype(jnp.float32)
    count_tok = lax.optimization_barrier(jnp.sum(weight_pix, 1))

    def class_counts(item):
        lab, wts = item
        hot = lab[:, :, None] == jnp.arange(C, dtype=jnp.int32)[None, None, :]
        return lax.optimization_barrier(jnp.sum(jnp.where(hot, wts[:, :, None], 0.0), 1))
    counts = lax.map(class_counts, (labels.reshape(images, SEQ, PP), weight_pix.reshape(images, SEQ, PP))).reshape(TOKENS, C)
    total = jnp.sum(count_tok)
    task_tok = jnp.repeat(tasks, SEQ)
    data = (patches.astype(jnp.float32), patch_valid, task_tok, routes, count_tok, counts, total)
    loss, pull = jax.vjp(lambda a, b, c: forward(a, b, c, *data), dense_weight, expert_in, expert_out)
    g_dense, g_in, g_out = pull(jnp.ones_like(loss))
    grad_norm = jnp.sqrt(jnp.sum(g_dense * g_dense) + jnp.sum(g_in * g_in) + jnp.sum(g_out * g_out))
    clip = CLIP_NORM / jnp.maximum(grad_norm, CLIP_NORM)

    def moments(weight, first, second, grad):
        grad = grad * clip
        first_new = DECAY_ONE * first + (1.0 - DECAY_ONE) * grad
        second_new = DECAY_TWO * second + (1.0 - DECAY_TWO) * grad * grad
        return (first_new, second_new, first_new / (jnp.sqrt(second_new) + EPS_ADAM) + WEIGHT_DECAY * weight)
    dm, dv, dstep = moments(dense_weight, dense_first, dense_second, g_dense)
    im, iv, istep = moments(expert_in, in_first, in_second, g_in)
    om, ov, ostep = moments(expert_out, out_first, out_second, g_out)
    weight_norms = jnp.stack([jnp.sqrt(jnp.sum(b * b)) for b in blocks_of(dense_weight, expert_in, expert_out)])
    step_norms = jnp.stack([jnp.sqrt(jnp.sum(b * b)) for b in blocks_of(dstep, istep, ostep)])
    ratio = weight_norms / (step_norms + EPS_NORM)
    dense_ratio = jnp.repeat(ratio[:14], np.array(segment_sizes()), total_repeat_length=NDENSE)
    in_rate = jnp.repeat(ratio[14:14 + EXPERTS], REPL)[:, None, None]
    out_rate = jnp.repeat(ratio[14 + EXPERTS:], REPL)[:, None, None]

    def finish(weight, average, step, rate):
        new = weight - RATE * rate * step
        return (new, AVERAGE * average + (1.0 - AVERAGE) * new, new.astype(jnp.bfloat16))
    dn, da, dl = finish(dense_weight, dense_average, dstep, dense_ratio)
    inn, ina, inl = finish(expert_in, in_average, istep, in_rate)
    on, oa, ol = finish(expert_out, out_average, ostep, out_rate)
    block_norms = jnp.stack([weight_norms, step_norms], 1)
    return (loss.reshape(1), grad_norm.reshape(1), block_norms, dn, dm, dv, da, dl, inn, im, iv, ina, inl, on, om, ov, oa, ol)
```

```python
import functools
import math

import jax
import jax.numpy as jnp
from jax import lax
from jax.experimental import pallas as pl
from jax.experimental.pallas import tpu as pltpu
from jax.sharding import PartitionSpec as P

D = 384
HEADS = 6
HD = 64
FF = 1536
TOP = 4
C = 40
PIX = 768
TASKS = 4


EPS_NORM = 1e-05
CLIP_NORM = 0.002
RATE = 0.3
DECAY_ONE = 0.5
DECAY_TWO = 0.5
WEIGHT_DECAY = 0.01
EPS_ADAM = 1e-09
AVERAGE = 0.9
SCALE = 0.125
LOWTYPE = jnp.bfloat16
FULLTYPE = jnp.float32


def plain(left, right):
    return jnp.dot(left, right, preferred_element_type=FULLTYPE)


def left_t(left, right):
    return lax.dot_general(left, right, (((0,), (0,)), ((), ())), preferred_element_type=FULLTYPE)


def right_t(left, right):
    return lax.dot_general(left, right, (((1,), (1,)), ((), ())), preferred_element_type=FULLTYPE)


def segment_sizes(experts):
    return (
        [PIX * D]
        + [3 * D * D] * 3
        + [D * D] * 3
        + [D * FF] * 2
        + [FF * D] * 2
        + [TASKS * D * experts, D * C, 14 * D]
    )


def unpack(flat, experts):
    shapes = [
        (PIX, D),
        (3, D, 3 * D),
        (3, D, D),
        (2, D, FF),
        (2, FF, D),
        (TASKS, D, experts),
        (D, C),
        (2, 7, D),
    ]
    pieces = []
    start = 0
    for shape in shapes:
        count = math.prod(shape)
        pieces.append(flat[start : start + count].reshape(shape))
        start += count
    return pieces


def segment_onehot(start, count, experts):
    index = start + jnp.arange(count, dtype=jnp.int32)
    sizes = segment_sizes(experts)
    label = jnp.zeros((count,), jnp.int32)
    edge = 0
    for size in sizes[:-1]:
        edge += size
        label = label + (index >= edge).astype(jnp.int32)
    return label[:, None] == jnp.arange(len(sizes), dtype=jnp.int32)[None, :]


def layer_norm(x, gain, bias):
    mean = jnp.mean(x, -1, keepdims=True)
    cent = x - mean
    var = jnp.mean(cent * cent, -1, keepdims=True)
    return cent * lax.rsqrt(var + EPS_NORM) * gain + bias


def norm_back(x, gain, bias, grad):
    return jax.vjp(layer_norm, x, gain, bias)[1](grad)


def gelu(hidden):
    return jax.nn.gelu(hidden, approximate=False)


VMEM_LIMIT = 56 * 2**20
ROWS = 256
NEG = -1e30


def rows_of(index, size=ROWS):
    return pl.ds(pl.multiple_of(index * size, size), size)


def norm_parts(x):
    cent = x - jnp.mean(x, -1, keepdims=True)
    scale = lax.rsqrt(jnp.mean(cent * cent, -1, keepdims=True) + EPS_NORM)
    return (cent * scale, scale)


def norm_low(x, gain, bias):
    return (norm_parts(x)[0] * gain + bias).astype(LOWTYPE)


def norm_pull(x, gain, grad):
    unit, scale = norm_parts(x)
    inner = grad * gain
    d_x = scale * (
        inner
        - jnp.mean(inner, -1, keepdims=True)
        - unit * jnp.mean(inner * unit, -1, keepdims=True)
    )
    return (d_x, jnp.sum(grad * unit, 0, keepdims=True), jnp.sum(grad, 0, keepdims=True))


def gelu_pair(h):
    z = jnp.abs(h) * 0.7071067811865476
    t = 1.0 / (1.0 + 0.3275911 * z)
    poly = t * (
        0.127414796
        + t * (-0.142248368 + t * (0.7107068705 + t * (-0.7265760135 + t * 0.5307027145)))
    )
    e = jnp.exp(-(z * z))
    tail = poly * e
    cdf = jnp.where(h < 0, tail, 1.0 - tail)
    return (h * cdf, cdf + h * (e * 0.3989422804014327))


def half_masks(scale):
    lane = lax.broadcasted_iota(jnp.int32, (1, 128), 1)
    return [jnp.where((lane < HD) == (h == 0), scale, 0.0).astype(LOWTYPE) for h in (0, 1)]


def attend_rows(qkv_ref, bias_ref, o_ref, lse_ref):
    seq = qkv_ref.shape[0]
    masks = half_masks(SCALE)
    lane = lax.broadcasted_iota(jnp.int32, (ROWS, 128), 1)

    for pair in range(HEADS // 2):
        cols = pl.ds(pair * 128, 128)

        def body(i, carry, pair=pair, cols=cols):
            rows = rows_of(i)
            query = qkv_ref[rows, cols]
            keys = qkv_ref[:, pl.ds(D + pair * 128, 128)]
            values = qkv_ref[:, pl.ds(2 * D + pair * 128, 128)]
            outs = []
            for h in (0, 1):
                s = right_t(query * masks[h], keys) + bias_ref[...]
                top = jnp.max(s, -1, keepdims=True)
                e = jnp.exp(s - top)
                total = jnp.sum(e, -1, keepdims=True)
                probs = (e * (1.0 / total)).astype(LOWTYPE)
                outs.append(plain(probs, values))
                lse = jnp.broadcast_to(top + jnp.log(total), (ROWS, 128)).T
                lse_ref[pl.ds(2 * pair + h, 1), rows] = lse[0:1, :]
            o_ref[rows, cols] = jnp.where(lane < HD, outs[0], outs[1]).astype(LOWTYPE)
            return carry

        lax.fori_loop(0, seq // ROWS, body, 0)


def forward_kernel(has_patch, has_ff, *refs):
    refs = list(refs)
    x_in = refs.pop(0)
    if has_patch:
        w_patch = refs.pop(0)
    w_qkv, w_attn, norms, bias = refs[:4]
    refs = refs[4:]
    if has_ff:
        w_up, w_down = refs[:2]
        refs = refs[2:]
    if has_patch:
        x_ref = refs.pop(0)
    else:
        x_ref = x_in
    mid_ref, c_ref, qkv_ref, o_ref, lse_ref = refs[:5]
    refs = refs[5:]
    if has_ff:
        next_ref, act_ref, slope_ref = refs
    seq = x_ref.shape[0]

    def project(i, carry):
        rows = rows_of(i)
        if has_patch:
            x_ref[rows, :] = plain(x_in[rows, :], w_patch[...])
        a16 = norm_low(x_ref[rows, :], norms[0:1, :], norms[1:2, :])
        qkv_ref[rows, :] = plain(a16, w_qkv[...]).astype(LOWTYPE)
        return carry

    lax.fori_loop(0, seq // ROWS, project, 0)
    lse_ref[...] = jnp.zeros_like(lse_ref)
    attend_rows(qkv_ref, bias, o_ref, lse_ref)

    def finish(i, carry):
        rows = rows_of(i)
        mid = x_ref[rows, :] + plain(o_ref[rows, :], w_attn[...])
        mid_ref[rows, :] = mid
        c16 = norm_low(mid, norms[2:3, :], norms[3:4, :])
        c_ref[rows, :] = c16
        if has_ff:
            act, slope = gelu_pair(plain(c16, w_up[...]))
            act16 = act.astype(LOWTYPE)
            act_ref[rows, :] = act16
            slope_ref[rows, :] = slope
            next_ref[rows, :] = mid + plain(act16, w_down[...])
        return carry

    lax.fori_loop(0, seq // ROWS, finish, 0)


def in_vmem(count):
    return [pl.BlockSpec(memory_space=pltpu.VMEM)] * count


def local_call(kernel, outs, args, flops, scratch=()):
    moved = sum(math.prod(a.shape) * a.dtype.itemsize for a in (*args, *outs))
    return pl.pallas_call(
        kernel,
        out_shape=outs,
        in_specs=in_vmem(len(args)),
        out_specs=in_vmem(len(outs)),
        scratch_shapes=scratch,
        compiler_params=pltpu.CompilerParams(vmem_limit_bytes=VMEM_LIMIT),
        cost_estimate=pl.CostEstimate(flops=flops, bytes_accessed=moved, transcendentals=0),
    )(*args)


def shaped(shape, dtype):
    return jax.ShapeDtypeStruct(shape, dtype)


def layer_forward(x, w_patch, w_qkv, w_attn, norms, bias, w_up, w_down):
    seq = x.shape[0]
    has_patch, has_ff = (w_patch is not None, w_up is not None)
    args = [x] + [w_patch] * has_patch + [w_qkv, w_attn, norms, bias] + [w_up, w_down] * has_ff
    outs = [shaped((seq, D), FULLTYPE)] * has_patch
    outs += [
        shaped((seq, D), FULLTYPE),
        shaped((seq, D), LOWTYPE),
        shaped((seq, 3 * D), LOWTYPE),
        shaped((seq, D), LOWTYPE),
        shaped((8, seq), FULLTYPE),
    ]
    if has_ff:
        outs += [
            shaped((seq, D), FULLTYPE),
            shaped((seq, FF), LOWTYPE),
            shaped((seq, FF), FULLTYPE),
        ]
    flops = 2 * seq * D * (4 * D + 4 * seq + 2 * FF * has_ff)
    return local_call(functools.partial(forward_kernel, has_patch, has_ff), outs, args, flops)


def attend_pull(qkv_ref, do_ref, lse_ref, valid_ref, dqkv_ref, dk_ref, dv_ref):
    seq = qkv_ref.shape[0]
    scaled, ones = (half_masks(SCALE), half_masks(1.0))
    lane = lax.broadcasted_iota(jnp.int32, (ROWS, 128), 1)

    for pair in range(HEADS // 2):
        cols = pl.ds(pair * 128, 128)
        dk_ref[...] = jnp.zeros_like(dk_ref)
        dv_ref[...] = jnp.zeros_like(dv_ref)

        def body(i, carry, pair=pair, cols=cols):
            rows = rows_of(i)
            query = qkv_ref[rows, cols]
            keys = qkv_ref[:, pl.ds(D + pair * 128, 128)]
            values = qkv_ref[:, pl.ds(2 * D + pair * 128, 128)]
            d_out = do_ref[rows, cols]
            d_query = []
            for h in (0, 1):
                own_q = query * scaled[h]
                own_d = d_out * ones[h]
                s = right_t(keys, own_q) + valid_ref[...]
                probs = jnp.exp(s - lse_ref[pl.ds(2 * pair + h, 1), rows])
                dv_ref[...] += plain(probs.astype(LOWTYPE), own_d)
                d_probs = right_t(values, own_d)
                delta = jnp.sum(probs * d_probs, 0, keepdims=True)
                d_s = (probs * (d_probs - delta)).astype(LOWTYPE)
                dk_ref[...] += plain(d_s, own_q)
                d_query.append(left_t(d_s, keys))
            picked = jnp.where(lane < HD, d_query[0], d_query[1]) * SCALE
            dqkv_ref[rows, cols] = picked.astype(LOWTYPE)
            return carry

        lax.fori_loop(0, seq // ROWS, body, 0)
        dqkv_ref[:, pl.ds(D + pair * 128, 128)] = dk_ref[...].astype(LOWTYPE)
        dqkv_ref[:, pl.ds(2 * D + pair * 128, 128)] = dv_ref[...].astype(LOWTYPE)


def weight_pull(left_ref, right_ref, out_ref, tile=128):
    def body(j, carry):
        cols = rows_of(j, tile)
        out_ref[cols, :] = left_t(left_ref[:, cols], right_ref[...])
        return carry

    lax.fori_loop(0, left_ref.shape[1] // tile, body, 0)


def backward_kernel(has_patch, has_ff, *refs):
    refs = list(refs)
    grad, x_ref, mid_ref, qkv, o_ref, lse, w_qkv, w_attn, norms, valid = refs[:10]
    refs = refs[10:]
    if has_ff:
        c_ref, act, slope, w_up, w_down = refs[:5]
        refs = refs[5:]
    else:
        d_c_ref = refs.pop(0)
    if has_patch:
        patches = refs.pop(0)
    d_qkvw, d_attn, d_norms = refs[:3]
    refs = refs[3:]
    if has_ff:
        d_up, d_down = refs[:2]
        refs = refs[2:]
    if has_patch:
        d_patch = refs.pop(0)
    else:
        dx_ref = refs.pop(0)
    gmid, low, do_ref, dqkv, dk, dv = refs[:6]
    refs = refs[6:]
    if has_ff:
        dh_ref = refs.pop(0)
    seq = grad.shape[0]
    blocks_count = seq // ROWS
    d_norms[...] = jnp.zeros_like(d_norms)

    def feed(i, carry):
        rows = rows_of(i)
        g = grad[rows, :]
        if has_ff:
            g16 = g.astype(LOWTYPE)
            low[rows, :] = g16
            dh16 = (right_t(g16, w_down[...]) * slope[rows, :]).astype(LOWTYPE)
            dh_ref[rows, :] = dh16
            d_c = right_t(dh16, w_up[...])
        else:
            d_c = d_c_ref[rows, :]
        d_x, d_gain, d_bias = norm_pull(mid_ref[rows, :], norms[2:3, :], d_c)
        gmid[rows, :] = g + d_x
        d_norms[2:3, :] += d_gain
        d_norms[3:4, :] += d_bias
        return carry

    lax.fori_loop(0, blocks_count, feed, 0)
    if has_ff:
        weight_pull(act, low, d_down)
        weight_pull(c_ref, dh_ref, d_up)

    def out_pull(i, carry):
        rows = rows_of(i)
        g16 = gmid[rows, :].astype(LOWTYPE)
        low[rows, :] = g16
        do_ref[rows, :] = right_t(g16, w_attn[...]).astype(LOWTYPE)
        return carry

    lax.fori_loop(0, blocks_count, out_pull, 0)
    weight_pull(o_ref, low, d_attn)
    attend_pull(qkv, do_ref, lse, valid, dqkv, dk, dv)

    def in_pull(i, carry):
        rows = rows_of(i)
        d_a = right_t(dqkv[rows, :], w_qkv[...])
        x = x_ref[rows, :]
        d_x, d_gain, d_bias = norm_pull(x, norms[0:1, :], d_a)
        total = gmid[rows, :] + d_x
        if has_patch:
            gmid[rows, :] = total
        else:
            dx_ref[rows, :] = total
        low[rows, :] = norm_low(x, norms[0:1, :], norms[1:2, :])
        d_norms[0:1, :] += d_gain
        d_norms[1:2, :] += d_bias
        return carry

    lax.fori_loop(0, blocks_count, in_pull, 0)
    weight_pull(low, dqkv, d_qkvw)
    if has_patch:

        def lower(i, carry):
            rows = rows_of(i)
            low[rows, :] = gmid[rows, :].astype(LOWTYPE)
            return carry

        lax.fori_loop(0, blocks_count, lower, 0)
        weight_pull(patches, low, d_patch)


def layer_backward(grad, x, kept, w_qkv, w_attn, norms, valid, ff, d_c, patches):
    seq = grad.shape[0]
    mid, c16, qkv16, o16, lse = kept[:5]
    has_ff, has_patch = (ff is not None, patches is not None)
    args = [grad, x, mid, qkv16, o16, lse, w_qkv, w_attn, norms, valid]
    args += [c16, *kept[5:], *ff] if has_ff else [d_c]
    args += [patches] * has_patch
    outs = [
        shaped((D, 3 * D), FULLTYPE),
        shaped((D, D), FULLTYPE),
        shaped((8, D), FULLTYPE),
    ]
    if has_ff:
        outs += [shaped((D, FF), FULLTYPE), shaped((FF, D), FULLTYPE)]
    outs += [shaped((PIX, D), FULLTYPE) if has_patch else shaped((seq, D), FULLTYPE)]
    scratch = [
        pltpu.VMEM((seq, D), FULLTYPE),
        pltpu.VMEM((seq, D), LOWTYPE),
        pltpu.VMEM((seq, D), LOWTYPE),
        pltpu.VMEM((seq, 3 * D), LOWTYPE),
        pltpu.VMEM((seq, 128), FULLTYPE),
        pltpu.VMEM((seq, 128), FULLTYPE),
    ] + [pltpu.VMEM((seq, FF), LOWTYPE)] * has_ff
    flops = 2 * seq * D * (8 * D + 10 * seq + 4 * FF * has_ff + PIX * has_patch)
    return local_call(
        functools.partial(backward_kernel, has_patch, has_ff), outs, args, flops, scratch
    )


def head_kernel(x_ref, norms, w_head, counts, count, total, loss, d_head, d_norms, grad, f_ref, dl_ref):
    seq = x_ref.shape[0]
    d_norms[...] = jnp.zeros_like(d_norms)
    loss[...] = jnp.zeros_like(loss)
    real = lax.broadcasted_iota(jnp.int32, (1, 128), 1) < C

    def body(i, carry):
        rows = rows_of(i)
        x = x_ref[rows, :]
        f16 = norm_low(x, norms[0:1, :], norms[1:2, :])
        f_ref[rows, :] = f16
        logits = plain(f16, w_head[...])
        shown = jnp.where(real, logits, NEG)
        top = jnp.max(shown, -1, keepdims=True)
        e = jnp.exp(shown - top)
        under = jnp.sum(e, -1, keepdims=True)
        weight = count[rows, :]
        classes = counts[rows, :]
        part = weight * (top + jnp.log(under)) - jnp.sum(classes * logits, -1, keepdims=True)
        loss[...] += jnp.broadcast_to(jnp.sum(part, 0, keepdims=True), loss.shape)
        d_logits = ((weight * (e * (1.0 / under)) - classes) / total[...]).astype(LOWTYPE)
        dl_ref[rows, :] = d_logits
        d_x, d_gain, d_bias = norm_pull(x, norms[0:1, :], right_t(d_logits, w_head[...]))
        grad[rows, :] = d_x
        d_norms[0:1, :] += d_gain
        d_norms[1:2, :] += d_bias
        return carry

    lax.fori_loop(0, seq // ROWS, body, 0)
    weight_pull(f_ref, dl_ref, d_head)


def head_call(x, norms, w_head, counts, count, total):
    seq = x.shape[0]
    outs = [
        shaped((1, 128), FULLTYPE),
        shaped((D, 128), FULLTYPE),
        shaped((8, D), FULLTYPE),
        shaped((seq, D), FULLTYPE),
    ]
    args = [
        x,
        norms,
        jnp.pad(w_head, ((0, 0), (0, 128 - C))),
        jnp.pad(counts, ((0, 0), (0, 128 - C))),
        count.reshape(seq, 1),
        total.reshape(1, 1),
    ]
    scratch = [pltpu.VMEM((seq, D), LOWTYPE), pltpu.VMEM((seq, 128), LOWTYPE)]
    return local_call(head_kernel, outs, args, 6 * seq * D * 128, scratch)


def feed_forward(rows16, w_up, w_back):
    hidden = plain(rows16, w_up)
    return (plain(gelu(hidden).astype(LOWTYPE), w_back), hidden)


def feed_backward(rows16, hidden, grad16, w_up, w_back):
    act16 = gelu(hidden).astype(LOWTYPE)
    d_back = left_t(act16, grad16)
    d_act = right_t(grad16, w_back)
    d_hidden = jax.vjp(gelu, hidden)[1](d_act)[0].astype(LOWTYPE)
    return (right_t(d_hidden, w_up), (left_t(rows16, d_hidden), d_back))


def make_slots(routes, experts, capacity):
    flat = routes.reshape(-1)
    seq = routes.shape[0]
    named = (routes[:, :, None] == jnp.arange(experts, dtype=jnp.int32)[None, None, :]).astype(LOWTYPE)
    earlier = jnp.arange(seq)[:, None] > jnp.arange(seq)[None, :]
    before = plain(earlier.astype(LOWTYPE), jnp.sum(named, 1))
    rank = jnp.sum(before[:, None, :] * named, 2).astype(jnp.int32).reshape(-1)
    slot = flat * capacity + rank
    assign = (
        jnp.zeros((experts * capacity,), jnp.int32)
        .at[slot]
        .set(jnp.arange(flat.shape[0], dtype=jnp.int32))
    )
    used = jnp.zeros((experts * capacity,), jnp.int32).at[slot].set(1)
    return (slot, assign, used)


def swap_dp(value):
    return lax.ppermute(value, "dp", [(0, 1), (1, 0)])


def join_dp(value, place):
    groups = lax.axis_size("dp")
    if groups != 2:
        return lax.all_gather(value, "dp")
    other = swap_dp(value)
    first = place == 0
    return jnp.stack([jnp.where(first, value, other), jnp.where(first, other, value)])


def sum_scatter_dp(parts, place):
    groups = lax.axis_size("dp")
    if groups != 2:
        return lax.psum_scatter(parts, "dp", scatter_dimension=0, tiled=True)[0]
    first = place == 0
    mine = jnp.where(first, parts[0], parts[1])
    return mine + swap_dp(jnp.where(first, parts[1], parts[0]))


def sum_all(value):
    for axis in ("dp", "ep"):
        count = lax.axis_size(axis)
        step = 1
        while step < count:
            value = value + lax.ppermute(value, axis, [(i, i ^ step) for i in range(count)])
            step *= 2
    return value


def to_experts(buffer):
    return lax.all_to_all(buffer, "ep", split_axis=0, concat_axis=0, tiled=True)


def from_experts(buffer):
    return lax.all_to_all(
        buffer.astype(jnp.bfloat16), "ep", split_axis=0, concat_axis=0, tiled=True
    ).astype(buffer.dtype)


def per_device(
    patches,
    labels,
    pixel_mask,
    patch_valid,
    tasks,
    routes,
    dense_weight,
    dense_first,
    dense_second,
    dense_average,
    expert_in,
    in_first,
    in_second,
    in_average,
    expert_out,
    out_first,
    out_second,
    out_average,
):
    ep_count = lax.axis_size("ep")
    experts = min(16, ep_count)
    copies = ep_count // experts
    groups = lax.axis_size("dp")
    ep_place = lax.axis_index("ep")
    dp_place = lax.axis_index("dp")
    own_expert = ep_place // copies
    seq = patches.shape[0]
    capacity = 3 * seq * TOP // (2 * experts)
    shard = dense_weight.shape[0]
    part_rows = -(-shard // (groups * 1024)) * 8
    padded = part_rows * 128 * groups
    low_parts = jnp.pad(dense_weight.astype(LOWTYPE), (0, padded - shard)).reshape(
        groups, part_rows, 128
    )
    own_part = lax.dynamic_index_in_dim(low_parts, dp_place, 0, keepdims=False)
    parts = join_dp(lax.all_gather(own_part, "ep"), dp_place)
    gathered = jnp.swapaxes(parts, 0, 1).reshape(ep_count, padded)[:, :shard].reshape(-1)
    w_patch, w_qkv, w_attn, w_up, w_down, w_router, w_head, norms16 = unpack(gathered, experts)
    norms = norms16.astype(FULLTYPE)
    own_in, own_out = (
        lax.all_gather(expert_in.astype(LOWTYPE), "dp", axis=2, tiled=True),
        lax.all_gather(expert_out.astype(LOWTYPE), "dp", axis=1, tiled=True),
    )
    own_in = own_in[0]
    own_out = own_out[0]
    task = tasks[0]
    router = lax.dynamic_index_in_dim(w_router, task, 0, keepdims=False)
    slot, assign, used = make_slots(routes, experts, capacity)
    route_hot = (routes[:, :, None] == jnp.arange(experts, dtype=jnp.int32)[None, None, :]).astype(
        FULLTYPE
    )

    def dispatch(send):
        buffer = jnp.repeat(send.reshape(experts, capacity, D), copies, axis=0)
        return to_experts(buffer)

    def combine(partial_value):
        back = from_experts(partial_value).reshape(experts, copies, capacity, D)
        summed = jnp.sum(back, 1).astype(LOWTYPE).reshape(experts * capacity, D)
        return summed[slot].reshape(seq, TOP, D).astype(FULLTYPE)

    def expert_backward(arrived, rows, hidden):
        d_rows, (d_in, d_out) = feed_backward(rows, hidden, arrived.reshape(-1, D), own_in, own_out)
        d_in_own, d_out_own = (
            lax.psum_scatter(
                d_in[None].astype(jnp.bfloat16), "dp", scatter_dimension=2, tiled=True
            ).astype(jnp.float32),
            lax.psum_scatter(
                d_out[None].astype(jnp.bfloat16), "dp", scatter_dimension=1, tiled=True
            ).astype(jnp.float32),
        )
        return (d_rows.reshape(arrived.shape), d_in_own, d_out_own)

    def norm_rows(layer):
        rows = [norms[0, 2 * layer], norms[1, 2 * layer]]
        if layer < 3:
            rows += [norms[0, 2 * layer + 1], norms[1, 2 * layer + 1]]
        return jnp.pad(jnp.stack(rows), ((0, 8 - len(rows)), (0, 0)))

    bias = jnp.where(patch_valid > 0, 0.0, NEG).astype(FULLTYPE)
    across, down = (bias.reshape(1, seq), bias.reshape(seq, 1))
    weight_pix = (pixel_mask * patch_valid[:, None]).astype(FULLTYPE)
    count_tok = jnp.sum(weight_pix, 1)
    class_hot = labels[:, :, None] == jnp.arange(C, dtype=jnp.int32)[None, None, :]
    counts = jnp.sum(jnp.where(class_hot, weight_pix[:, :, None], 0.0), 1)
    total = sum_all(jnp.sum(count_tok).reshape(1))[0]

    x0, *kept0, x1, act0, slope0 = layer_forward(
        patches, w_patch, w_qkv[0], w_attn[0], norm_rows(0), across, w_up[0], w_down[0]
    )
    mid1, c16, *kept1 = layer_forward(
        x1, None, w_qkv[1], w_attn[1], norm_rows(1), across, None, None
    )
    logits = plain(c16, router)
    gates = jax.nn.softmax(jnp.sum(route_hot * logits[:, None, :], -1), -1)
    send = jnp.where(used[:, None] > 0, c16[assign // TOP], jnp.zeros((), LOWTYPE))
    arrived = dispatch(send)
    rows = arrived.reshape(-1, D)
    out, hidden = feed_forward(rows, own_in, own_out)
    picks = combine(out.reshape(arrived.shape))
    x2 = mid1 + jnp.sum(gates[:, :, None] * picks, 1)
    *kept2, x3, act2, slope2 = layer_forward(
        x2, None, w_qkv[2], w_attn[2], norm_rows(2), across, w_up[1], w_down[1]
    )
    loss_lanes, d_head, d_normf, grad = head_call(
        x3, norm_rows(3), w_head, counts, count_tok, total
    )
    local = loss_lanes[0, 0]
    d_qkv2, d_attn2, d_norm2, d_up1, d_down1, grad = layer_backward(
        grad, x2, (*kept2, act2, slope2), w_qkv[2], w_attn[2], norm_rows(2), down,
        (w_up[1], w_down[1]), None, None,
    )
    d_gates = jnp.sum(grad[:, None, :] * picks, -1)
    d_picked = gates * (d_gates - jnp.sum(gates * d_gates, -1, keepdims=True))
    d_logits = jnp.sum(route_hot * d_picked[:, :, None], 1).astype(LOWTYPE)
    task_hot = (jnp.arange(TASKS, dtype=jnp.int32) == task)[:, None, None]
    d_router = jnp.where(task_hot, left_t(c16, d_logits)[None], 0.0)
    d_picks = (gates[:, :, None] * grad[:, None, :]).astype(LOWTYPE).reshape(seq * TOP, D)
    send = jnp.where(used[:, None] > 0, d_picks[assign], jnp.zeros((), LOWTYPE))
    d_rows, d_in, d_out = expert_backward(dispatch(send), rows, hidden)
    d_c = right_t(d_logits, router) + jnp.sum(combine(d_rows), 1)
    d_qkv1, d_attn1, d_norm1, grad = layer_backward(
        grad, x1, (mid1, c16, *kept1), w_qkv[1], w_attn[1], norm_rows(1), down, None, d_c, None
    )
    d_qkv0, d_attn0, d_norm0, d_up0, d_down0, d_patch = layer_backward(
        grad, x0, (*kept0, act0, slope0), w_qkv[0], w_attn[0], norm_rows(0), down,
        (w_up[0], w_down[0]), None, patches,
    )
    d_head = d_head[:, :C]
    each = [d_norm0, d_norm1, d_norm2]
    gain_list = [n[k] for n in each for k in (0, 2)] + [d_normf[0]]
    bias_list = [n[k] for n in each for k in (1, 3)] + [d_normf[1]]
    d_qkv_list = [d_qkv0, d_qkv1, d_qkv2]
    d_attn_list = [d_attn0, d_attn1, d_attn2]
    d_up_list = [d_up0, d_up1]
    d_down_list = [d_down0, d_down1]
    d_norms = jnp.stack([jnp.stack(gain_list), jnp.stack(bias_list)])
    listed = [
        d_patch,
        jnp.stack(d_qkv_list),
        jnp.stack(d_attn_list),
        jnp.stack(d_up_list),
        jnp.stack(d_down_list),
        d_router,
        d_head,
        d_norms,
    ]
    flat_grad = jnp.concatenate([piece.reshape(-1) for piece in listed])
    by_owner = jnp.pad(flat_grad.reshape(ep_count, shard), ((0, 0), (0, padded - shard)))
    by_part = jnp.swapaxes(by_owner.reshape(ep_count, groups, part_rows, 128), 0, 1)
    own_sum = lax.psum_scatter(
        sum_scatter_dp(by_part, dp_place), "ep", scatter_dimension=0, tiled=True
    )[0]
    dense_grad = join_dp(own_sum, dp_place).reshape(padded)[:shard]
    piece = shard // groups
    part_hot = segment_onehot(ep_place * shard + dp_place * piece, piece, experts)
    expert_hot = (jnp.arange(experts, dtype=jnp.int32) == own_expert).astype(FULLTYPE)

    def block_sums(dense_vals, in_vals, out_vals):
        part = lax.dynamic_slice_in_dim(dense_vals, dp_place * piece, piece)
        dense_part = jnp.sum(jnp.where(part_hot, (part * part)[:, None], 0.0), 0)
        return jnp.concatenate(
            [
                dense_part,
                expert_hot * jnp.sum(in_vals * in_vals),
                expert_hot * jnp.sum(out_vals * out_vals),
            ]
        )

    sums = sum_all(
        jnp.concatenate(
            [
                local.reshape(1),
                jnp.sum(block_sums(dense_grad, d_in, d_out)).reshape(1),
                block_sums(dense_weight, expert_in, expert_out),
            ]
        )
    )
    loss, grad_total, weight_total = (sums[0] / total, sums[1], sums[2:])
    grad_norm = jnp.sqrt(grad_total)
    clip = CLIP_NORM / jnp.maximum(grad_norm, CLIP_NORM)

    def moments(weight, first, second, gradient):
        gradient = gradient * clip
        first_new = DECAY_ONE * first + (1.0 - DECAY_ONE) * gradient
        second_new = DECAY_TWO * second + (1.0 - DECAY_TWO) * gradient * gradient
        return (
            first_new,
            second_new,
            first_new / (jnp.sqrt(second_new) + EPS_ADAM) + WEIGHT_DECAY * weight,
        )

    dense_m, dense_v, dense_step = moments(dense_weight, dense_first, dense_second, dense_grad)
    in_m, in_v, in_step = moments(expert_in, in_first, in_second, d_in)
    out_m, out_v, out_step = moments(expert_out, out_first, out_second, d_out)
    update_total = sum_all(block_sums(dense_step, in_step, out_step))
    weight_norm = jnp.sqrt(weight_total)
    update_norm = jnp.sqrt(update_total)
    ratio = weight_norm / (update_norm + EPS_NORM)
    whole_hot = segment_onehot(ep_place * shard, shard, experts)
    dense_ratio = jnp.sum(jnp.where(whole_hot, ratio[None, :14], 0.0), 1)
    in_ratio = lax.dynamic_index_in_dim(ratio, 14 + own_expert, 0, keepdims=False)
    out_ratio = lax.dynamic_index_in_dim(ratio, 14 + experts + own_expert, 0, keepdims=False)

    def finish(weight, average, step, rate):
        new = weight - RATE * rate * step
        return (new, AVERAGE * average + (1.0 - AVERAGE) * new, new.astype(LOWTYPE))

    dense_new, dense_avg, dense_low = finish(dense_weight, dense_average, dense_step, dense_ratio)
    in_new, in_avg, in_low = finish(expert_in, in_average, in_step, in_ratio)
    out_new, out_avg, out_low = finish(expert_out, out_average, out_step, out_ratio)
    block_norms = jnp.stack([weight_norm, update_norm], 1)
    return (
        loss.reshape(1),
        grad_norm.reshape(1),
        block_norms,
        dense_new,
        dense_m,
        dense_v,
        dense_avg,
        dense_low,
        in_new,
        in_m,
        in_v,
        in_avg,
        in_low,
        out_new,
        out_m,
        out_v,
        out_avg,
        out_low,
    )


def solution(mesh):
    in_specs = (
        P(("ep", "dp"), None),
        P(("ep", "dp"), None),
        P(("ep", "dp"), None),
        P(("ep", "dp")),
        P(("ep", "dp")),
        P(("ep", "dp"), None),
        P("ep"),
        P("ep"),
        P("ep"),
        P("ep"),
        P("ep", None, "dp"),
        P("ep", None, "dp"),
        P("ep", None, "dp"),
        P("ep", None, "dp"),
        P("ep", "dp", None),
        P("ep", "dp", None),
        P("ep", "dp", None),
        P("ep", "dp", None),
    )
    out_specs = (
        P(),
        P(),
        P(),
        P("ep"),
        P("ep"),
        P("ep"),
        P("ep"),
        P("ep"),
        P("ep", None, "dp"),
        P("ep", None, "dp"),
        P("ep", None, "dp"),
        P("ep", None, "dp"),
        P("ep", None, "dp"),
        P("ep", "dp", None),
        P("ep", "dp", None),
        P("ep", "dp", None),
        P("ep", "dp", None),
        P("ep", "dp", None),
    )
    return jax.shard_map(
        per_device, mesh=mesh, in_specs=in_specs, out_specs=out_specs, check_vma=False
    )
```

```python
import functools
import math

import jax
import jax.numpy as jnp
from jax import lax
from jax.experimental import pallas as pl
from jax.experimental.pallas import tpu as pltpu
from jax.sharding import PartitionSpec as P

D = 384
HEADS = 6
HD = 64
FF = 1536
TOP = 4
C = 40
PIX = 768
TASKS = 4


EPS_NORM = 1e-05
CLIP_NORM = 0.002
RATE = 0.3
DECAY_ONE = 0.5
DECAY_TWO = 0.5
WEIGHT_DECAY = 0.01
EPS_ADAM = 1e-09
AVERAGE = 0.9
SCALE = 0.125
LOWTYPE = jnp.bfloat16
FULLTYPE = jnp.float32


def plain(left, right):
    return jnp.dot(left, right, preferred_element_type=FULLTYPE)


def left_t(left, right):
    return lax.dot_general(left, right, (((0,), (0,)), ((), ())), preferred_element_type=FULLTYPE)


def right_t(left, right):
    return lax.dot_general(left, right, (((1,), (1,)), ((), ())), preferred_element_type=FULLTYPE)


def segment_sizes(experts):
    return (
        [PIX * D]
        + [3 * D * D] * 3
        + [D * D] * 3
        + [D * FF] * 2
        + [FF * D] * 2
        + [TASKS * D * experts, D * C, 14 * D]
    )


def owner_blocks(edges, shard, owners):
    firsts = [sum(edge <= shard * i for edge in edges) for i in range(owners)]
    lasts = [sum(edge < shard * (i + 1) for edge in edges) for i in range(owners)]
    span = max(b - a + 1 for a, b in zip(firsts, lasts))
    return (span, jnp.array(firsts, jnp.int32))


def segment_edges(experts):
    edges, edge = [], 0
    for size in segment_sizes(experts)[:-1]:
        edge += size
        edges.append(edge)
    return edges


VMEM_LIMIT = 56 * 2**20
ROWS = 256
NEG = -1e30


def rows_of(index, size=ROWS):
    return pl.ds(pl.multiple_of(index * size, size), size)


def norm_parts(x):
    cent = x - jnp.mean(x, -1, keepdims=True)
    scale = lax.rsqrt(jnp.mean(cent * cent, -1, keepdims=True) + EPS_NORM)
    return (cent * scale, scale)


def norm_low(x, gain, bias):
    return (norm_parts(x)[0] * gain + bias).astype(LOWTYPE)


def norm_pull(x, gain, grad):
    unit, scale = norm_parts(x)
    inner = grad * gain
    d_x = scale * (
        inner
        - jnp.mean(inner, -1, keepdims=True)
        - unit * jnp.mean(inner * unit, -1, keepdims=True)
    )
    return (d_x, jnp.sum(grad * unit, 0, keepdims=True), jnp.sum(grad, 0, keepdims=True))


def gelu_pair(h):
    cdf = 0.5 + 0.5 * lax.erf(h * 0.7071067811865476)
    e = jnp.exp((h * h) * -0.5)
    return (h * cdf, cdf + h * (e * 0.3989422804014327))


def half_masks(scale):
    lane = lax.broadcasted_iota(jnp.int32, (1, 128), 1)
    return [jnp.where((lane < HD) == (h == 0), scale, 0.0).astype(LOWTYPE) for h in (0, 1)]


def attend_rows(qkv_ref, bias_ref, o_ref, lse_ref):
    seq = qkv_ref.shape[0]
    masks = half_masks(SCALE)
    lane = lax.broadcasted_iota(jnp.int32, (ROWS, 128), 1)

    for pair in range(HEADS // 2):
        cols = pl.ds(pair * 128, 128)

        def body(i, carry, pair=pair, cols=cols):
            rows = rows_of(i)
            query = qkv_ref[rows, cols]
            keys = qkv_ref[:, pl.ds(D + pair * 128, 128)]
            values = qkv_ref[:, pl.ds(2 * D + pair * 128, 128)]
            outs = []
            for h in (0, 1):
                s = right_t(query * masks[h], keys) + bias_ref[...]
                top = jnp.max(s, -1, keepdims=True)
                e = jnp.exp(s - top)
                total = jnp.sum(e, -1, keepdims=True)
                probs = (e * (1.0 / total)).astype(LOWTYPE)
                outs.append(plain(probs, values))
                lse = jnp.broadcast_to(top + jnp.log(total), (ROWS, 128)).T
                lse_ref[pl.ds(2 * pair + h, 1), rows] = lse[0:1, :]
            o_ref[rows, cols] = jnp.where(lane < HD, outs[0], outs[1]).astype(LOWTYPE)
            return carry

        lax.fori_loop(0, seq // ROWS, body, 0)


def forward_kernel(has_patch, has_ff, *refs):
    refs = list(refs)
    x_in = refs.pop(0)
    if has_patch:
        w_patch = refs.pop(0)
    w_qkv, w_attn, norms, bias = refs[:4]
    refs = refs[4:]
    if has_ff:
        w_up, w_down = refs[:2]
        refs = refs[2:]
    if has_patch:
        x_ref = refs.pop(0)
    else:
        x_ref = x_in
    mid_ref, c_ref, qkv_ref, o_ref, lse_ref = refs[:5]
    refs = refs[5:]
    if has_ff:
        next_ref, act_ref, slope_ref = refs
    seq = x_ref.shape[0]

    def project(i, carry):
        rows = rows_of(i)
        if has_patch:
            x_ref[rows, :] = plain(x_in[rows, :], w_patch[...])
        a16 = norm_low(x_ref[rows, :], norms[0:1, :], norms[1:2, :])
        qkv_ref[rows, :] = plain(a16, w_qkv[...]).astype(LOWTYPE)
        return carry

    lax.fori_loop(0, seq // ROWS, project, 0)
    lse_ref[...] = jnp.zeros_like(lse_ref)
    attend_rows(qkv_ref, bias, o_ref, lse_ref)

    def finish(i, carry):
        rows = rows_of(i)
        mid = x_ref[rows, :] + plain(o_ref[rows, :], w_attn[...])
        mid_ref[rows, :] = mid
        c16 = norm_low(mid, norms[2:3, :], norms[3:4, :])
        c_ref[rows, :] = c16
        if has_ff:
            act, slope = gelu_pair(plain(c16, w_up[...]))
            act16 = act.astype(LOWTYPE)
            act_ref[rows, :] = act16
            slope_ref[rows, :] = slope
            next_ref[rows, :] = mid + plain(act16, w_down[...])
        return carry

    lax.fori_loop(0, seq // ROWS, finish, 0)


def in_vmem(count):
    return [pl.BlockSpec(memory_space=pltpu.VMEM)] * count


def local_call(kernel, outs, args, flops, scratch=()):
    moved = sum(math.prod(a.shape) * a.dtype.itemsize for a in (*args, *outs))
    return pl.pallas_call(
        kernel,
        out_shape=outs,
        in_specs=in_vmem(len(args)),
        out_specs=in_vmem(len(outs)),
        scratch_shapes=scratch,
        compiler_params=pltpu.CompilerParams(vmem_limit_bytes=VMEM_LIMIT),
        cost_estimate=pl.CostEstimate(flops=flops, bytes_accessed=moved, transcendentals=0),
    )(*args)


def shaped(shape, dtype):
    return jax.ShapeDtypeStruct(shape, dtype)


def layer_forward(x, w_patch, w_qkv, w_attn, norms, bias, w_up, w_down):
    seq = x.shape[0]
    has_patch, has_ff = (w_patch is not None, w_up is not None)
    args = [x] + [w_patch] * has_patch + [w_qkv, w_attn, norms, bias] + [w_up, w_down] * has_ff
    outs = [shaped((seq, D), FULLTYPE)] * has_patch
    outs += [
        shaped((seq, D), FULLTYPE),
        shaped((seq, D), LOWTYPE),
        shaped((seq, 3 * D), LOWTYPE),
        shaped((seq, D), LOWTYPE),
        shaped((8, seq), FULLTYPE),
    ]
    if has_ff:
        outs += [
            shaped((seq, D), FULLTYPE),
            shaped((seq, FF), LOWTYPE),
            shaped((seq, FF), FULLTYPE),
        ]
    flops = 2 * seq * D * (4 * D + 4 * seq + 2 * FF * has_ff)
    return local_call(functools.partial(forward_kernel, has_patch, has_ff), outs, args, flops)


def attend_pull(qkv_ref, do_ref, lse_ref, valid_ref, dqkv_ref, dk_ref, dv_ref):
    seq = qkv_ref.shape[0]
    scaled, ones = (half_masks(SCALE), half_masks(1.0))
    lane = lax.broadcasted_iota(jnp.int32, (ROWS, 128), 1)

    for pair in range(HEADS // 2):
        cols = pl.ds(pair * 128, 128)
        dk_ref[...] = jnp.zeros_like(dk_ref)
        dv_ref[...] = jnp.zeros_like(dv_ref)

        def body(i, carry, pair=pair, cols=cols):
            rows = rows_of(i)
            query = qkv_ref[rows, cols]
            keys = qkv_ref[:, pl.ds(D + pair * 128, 128)]
            values = qkv_ref[:, pl.ds(2 * D + pair * 128, 128)]
            d_out = do_ref[rows, cols]
            d_query = []
            for h in (0, 1):
                own_q = query * scaled[h]
                own_d = d_out * ones[h]
                s = right_t(keys, own_q) + valid_ref[...]
                probs = jnp.exp(s - lse_ref[pl.ds(2 * pair + h, 1), rows])
                dv_ref[...] += plain(probs.astype(LOWTYPE), own_d)
                d_probs = right_t(values, own_d)
                delta = jnp.sum(probs * d_probs, 0, keepdims=True)
                d_s = (probs * (d_probs - delta)).astype(LOWTYPE)
                dk_ref[...] += plain(d_s, own_q)
                d_query.append(left_t(d_s, keys))
            picked = jnp.where(lane < HD, d_query[0], d_query[1]) * SCALE
            dqkv_ref[rows, cols] = picked.astype(LOWTYPE)
            return carry

        lax.fori_loop(0, seq // ROWS, body, 0)
        dqkv_ref[:, pl.ds(D + pair * 128, 128)] = dk_ref[...].astype(LOWTYPE)
        dqkv_ref[:, pl.ds(2 * D + pair * 128, 128)] = dv_ref[...].astype(LOWTYPE)


def weight_pull(left_ref, right_ref, out_ref, tile=128):
    def body(j, carry):
        cols = rows_of(j, tile)
        out_ref[cols, :] = left_t(left_ref[:, cols], right_ref[...])
        return carry

    lax.fori_loop(0, left_ref.shape[1] // tile, body, 0)


def backward_kernel(has_patch, has_ff, *refs):
    refs = list(refs)
    grad, x_ref, mid_ref, qkv, o_ref, lse, w_qkv, w_attn, norms, valid = refs[:10]
    refs = refs[10:]
    if has_ff:
        c_ref, act, slope, w_up, w_down = refs[:5]
        refs = refs[5:]
    else:
        d_c_ref = refs.pop(0)
    if has_patch:
        patches = refs.pop(0)
    d_qkvw, d_attn, d_norms = refs[:3]
    refs = refs[3:]
    if has_ff:
        d_up, d_down = refs[:2]
        refs = refs[2:]
    if has_patch:
        d_patch = refs.pop(0)
    else:
        dx_ref = refs.pop(0)
    gmid, low, do_ref, dqkv, dk, dv = refs[:6]
    refs = refs[6:]
    if has_ff:
        dh_ref = refs.pop(0)
    seq = grad.shape[0]
    blocks_count = seq // ROWS
    d_norms[...] = jnp.zeros_like(d_norms)

    def feed(i, carry):
        rows = rows_of(i)
        g = grad[rows, :]
        if has_ff:
            g16 = g.astype(LOWTYPE)
            low[rows, :] = g16
            dh16 = (right_t(g16, w_down[...]) * slope[rows, :]).astype(LOWTYPE)
            dh_ref[rows, :] = dh16
            d_c = right_t(dh16, w_up[...])
        else:
            d_c = d_c_ref[rows, :]
        d_x, d_gain, d_bias = norm_pull(mid_ref[rows, :], norms[2:3, :], d_c)
        gmid[rows, :] = g + d_x
        d_norms[2:3, :] += d_gain
        d_norms[3:4, :] += d_bias
        return carry

    lax.fori_loop(0, blocks_count, feed, 0)
    if has_ff:
        weight_pull(act, low, d_down)
        weight_pull(c_ref, dh_ref, d_up)

    def out_pull(i, carry):
        rows = rows_of(i)
        g16 = gmid[rows, :].astype(LOWTYPE)
        low[rows, :] = g16
        do_ref[rows, :] = right_t(g16, w_attn[...]).astype(LOWTYPE)
        return carry

    lax.fori_loop(0, blocks_count, out_pull, 0)
    weight_pull(o_ref, low, d_attn)
    attend_pull(qkv, do_ref, lse, valid, dqkv, dk, dv)

    def in_pull(i, carry):
        rows = rows_of(i)
        d_a = right_t(dqkv[rows, :], w_qkv[...])
        x = x_ref[rows, :]
        d_x, d_gain, d_bias = norm_pull(x, norms[0:1, :], d_a)
        total = gmid[rows, :] + d_x
        if has_patch:
            gmid[rows, :] = total
        else:
            dx_ref[rows, :] = total
        low[rows, :] = norm_low(x, norms[0:1, :], norms[1:2, :])
        d_norms[0:1, :] += d_gain
        d_norms[1:2, :] += d_bias
        return carry

    lax.fori_loop(0, blocks_count, in_pull, 0)
    weight_pull(low, dqkv, d_qkvw)
    if has_patch:

        def lower(i, carry):
            rows = rows_of(i)
            low[rows, :] = gmid[rows, :].astype(LOWTYPE)
            return carry

        lax.fori_loop(0, blocks_count, lower, 0)
        weight_pull(patches, low, d_patch)


def layer_backward(grad, x, kept, w_qkv, w_attn, norms, valid, ff, d_c, patches):
    seq = grad.shape[0]
    mid, c16, qkv16, o16, lse = kept[:5]
    has_ff, has_patch = (ff is not None, patches is not None)
    args = [grad, x, mid, qkv16, o16, lse, w_qkv, w_attn, norms, valid]
    args += [c16, *kept[5:], *ff] if has_ff else [d_c]
    args += [patches] * has_patch
    outs = [
        shaped((D, 3 * D), FULLTYPE),
        shaped((D, D), FULLTYPE),
        shaped((8, D), FULLTYPE),
    ]
    if has_ff:
        outs += [shaped((D, FF), FULLTYPE), shaped((FF, D), FULLTYPE)]
    outs += [shaped((PIX, D), FULLTYPE) if has_patch else shaped((seq, D), FULLTYPE)]
    scratch = [
        pltpu.VMEM((seq, D), FULLTYPE),
        pltpu.VMEM((seq, D), LOWTYPE),
        pltpu.VMEM((seq, D), LOWTYPE),
        pltpu.VMEM((seq, 3 * D), LOWTYPE),
        pltpu.VMEM((seq, 128), FULLTYPE),
        pltpu.VMEM((seq, 128), FULLTYPE),
    ] + [pltpu.VMEM((seq, FF), LOWTYPE)] * has_ff
    flops = 2 * seq * D * (8 * D + 10 * seq + 4 * FF * has_ff + PIX * has_patch)
    return local_call(
        functools.partial(backward_kernel, has_patch, has_ff), outs, args, flops, scratch
    )


def head_kernel(x_ref, norms, w_head, counts, count, total, loss, d_head, d_norms, grad, f_ref, dl_ref):
    seq = x_ref.shape[0]
    d_norms[...] = jnp.zeros_like(d_norms)
    loss[...] = jnp.zeros_like(loss)
    real = lax.broadcasted_iota(jnp.int32, (1, 128), 1) < C

    def body(i, carry):
        rows = rows_of(i)
        x = x_ref[rows, :]
        f16 = norm_low(x, norms[0:1, :], norms[1:2, :])
        f_ref[rows, :] = f16
        logits = plain(f16, w_head[...])
        shown = jnp.where(real, logits, NEG)
        top = jnp.max(shown, -1, keepdims=True)
        e = jnp.exp(shown - top)
        under = jnp.sum(e, -1, keepdims=True)
        weight = count[rows, :]
        classes = counts[rows, :]
        part = weight * (top + jnp.log(under)) - jnp.sum(classes * logits, -1, keepdims=True)
        loss[...] += jnp.broadcast_to(jnp.sum(part, 0, keepdims=True), loss.shape)
        d_logits = ((weight * (e * (1.0 / under)) - classes) / total[...]).astype(LOWTYPE)
        dl_ref[rows, :] = d_logits
        d_x, d_gain, d_bias = norm_pull(x, norms[0:1, :], right_t(d_logits, w_head[...]))
        grad[rows, :] = d_x
        d_norms[0:1, :] += d_gain
        d_norms[1:2, :] += d_bias
        return carry

    lax.fori_loop(0, seq // ROWS, body, 0)
    weight_pull(f_ref, dl_ref, d_head)


def head_call(x, norms, w_head, counts, count, total):
    seq = x.shape[0]
    outs = [
        shaped((1, 128), FULLTYPE),
        shaped((D, 128), FULLTYPE),
        shaped((8, D), FULLTYPE),
        shaped((seq, D), FULLTYPE),
    ]
    args = [
        x,
        norms,
        jnp.pad(w_head, ((0, 0), (0, 128 - C))),
        jnp.pad(counts, ((0, 0), (0, 128 - C))),
        count.reshape(seq, 1),
        total.reshape(1, 1),
    ]
    scratch = [pltpu.VMEM((seq, D), LOWTYPE), pltpu.VMEM((seq, 128), LOWTYPE)]
    return local_call(head_kernel, outs, args, 6 * seq * D * 128, scratch)


SLOTS = 128


def by_load(load, capacity, work):
    for count in range(SLOTS, capacity + 1, SLOTS):
        inside = load > count - SLOTS if count > SLOTS else load >= 0
        if count < capacity:
            inside = inside & (load <= count)
        pl.when(inside)(functools.partial(work, count))


def slot_select(place, count):
    row = lax.broadcasted_iota(jnp.int32, (count, place.shape[1]), 0).astype(FULLTYPE)
    return jnp.where(place == row, 1.0, 0.0).astype(LOWTYPE)


def column_of(table, expert):
    lane = lax.broadcasted_iota(jnp.int32, table.shape, 1)
    return jnp.sum(jnp.where(lane == expert, table, 0.0), -1, keepdims=True)


def patch_select(spread, count):
    lane = lax.broadcasted_iota(jnp.int32, (1, 128), 1).astype(FULLTYPE)
    return jnp.concatenate(
        [
            jnp.where(spread == lane + first, 1.0, 0.0).astype(LOWTYPE)
            for first in range(0, count, 128)
        ],
        1,
    )


def moe_up_kernel(
    loads, c_ref, router, table, place, w_in,
    gates_ref, spread_place, spread_gate, rows_ref, act_ref, slope_ref,
):
    expert = pl.program_id(0)
    seq, capacity, parts = (c_ref.shape[0], rows_ref.shape[0], w_in.shape[1])
    width = w_in.shape[3]

    @pl.when(expert == 0)
    def _():
        def start(i, carry):
            rows = rows_of(i)
            z = plain(c_ref[rows, :], router[...])
            named = table[rows, :] >= 0
            shown = jnp.where(named, z, NEG)
            e = jnp.where(named, jnp.exp(shown - jnp.max(shown, -1, keepdims=True)), 0.0)
            gates_ref[rows, :] = e / jnp.sum(e, -1, keepdims=True)
            return carry

        lax.fori_loop(0, seq // ROWS, start, 0)

    def fan(i, carry):
        rows = rows_of(i)
        for source, out in ((table, spread_place), (gates_ref, spread_gate)):
            out[0, rows, :] = jnp.broadcast_to(column_of(source[rows, :], expert), (ROWS, 128))
        return carry

    lax.fori_loop(0, seq // ROWS, fan, 0)

    def work(count):
        at = pl.ds(0, count)
        rows = plain(slot_select(place[0], count), c_ref[...]).astype(LOWTYPE)
        rows_ref[at, :] = rows
        for part in range(parts):
            step = width // 3 if width % 384 == 0 else width
            for first in range(0, width, step):
                act, slope = gelu_pair(plain(rows, w_in[0, part, :, pl.ds(first, step)]))
                units = pl.ds(part * width + first, step)
                slope_ref[at, units] = slope
                act_ref[at, units] = act.astype(LOWTYPE)
        if count < capacity:
            rows_ref[pl.ds(count, capacity - count), :] = jnp.zeros((capacity - count, D), LOWTYPE)

    by_load(loads[expert], capacity, work)


def moe_down_kernel(loads, mid_ref, spread_place, spread_gate, act_ref, w_out, next_ref, y_ref):
    expert = pl.program_id(0)
    seq, capacity = (mid_ref.shape[0], act_ref.shape[0])

    @pl.when(expert == 0)
    def _():
        next_ref[...] = mid_ref[...]

    def work(count):
        at = pl.ds(0, count)
        y_ref[at, :] = plain(act_ref[at, :], w_out[0]).astype(LOWTYPE)
        if count < capacity:
            y_ref[pl.ds(count, capacity - count), :] = jnp.zeros((capacity - count, D), LOWTYPE)

        def add(i, carry):
            rows = rows_of(i)
            taken = plain(patch_select(spread_place[0, rows, :], count), y_ref[at, :])
            for first in range(0, D, 128):
                lanes = pl.ds(first, 128)
                next_ref[rows, lanes] += spread_gate[0, rows, :] * taken[:, first : first + 128]
            return carry

        lax.fori_loop(0, seq // ROWS, add, 0)

    by_load(loads[expert], capacity, work)


def moe_gate_kernel(
    loads, grad_ref, c_ref, router, gates, place, spread_place, spread_gate, y_ref,
    d_router, d_c, dy_ref, low_ref, dz_ref, d_gates,
):
    expert = pl.program_id(0)
    seq, capacity = (grad_ref.shape[0], y_ref.shape[0])
    lane = lax.broadcasted_iota(jnp.int32, (ROWS, d_gates.shape[1]), 1)

    @pl.when(expert == 0)
    def _():
        d_gates[...] = jnp.zeros_like(d_gates)

    def work(count):
        at = pl.ds(0, count)

        def one(i, carry):
            rows = rows_of(i)
            grad = grad_ref[rows, :]
            gate = spread_gate[0, rows, :]
            taken = plain(patch_select(spread_place[0, rows, :], count), y_ref[at, :])
            d_gate = jnp.sum(grad * taken, -1, keepdims=True)
            d_gates[rows, :] += jnp.where(lane == expert, d_gate, 0.0)
            for first in range(0, D, 128):
                lanes = pl.ds(first, 128)
                low_ref[rows, lanes] = (gate * grad[:, first : first + 128]).astype(LOWTYPE)
            return carry

        lax.fori_loop(0, seq // ROWS, one, 0)
        dy_ref[at, :] = plain(slot_select(place[0], count), low_ref[...]).astype(LOWTYPE)
        if count < capacity:
            dy_ref[pl.ds(count, capacity - count), :] = jnp.zeros((capacity - count, D), LOWTYPE)

    by_load(loads[expert], capacity, work)

    @pl.when(expert == pl.num_programs(0) - 1)
    def _():
        def last(i, carry):
            rows = rows_of(i)
            gate = gates[rows, :]
            d_gate = d_gates[rows, :]
            d_z = gate * (d_gate - jnp.sum(gate * d_gate, -1, keepdims=True))
            dz_ref[rows, :] = d_z.astype(LOWTYPE)
            d_c[rows, :] = right_t(dz_ref[rows, :], router[...])
            return carry

        lax.fori_loop(0, seq // ROWS, last, 0)
        d_router[...] = left_t(c_ref[...], dz_ref[...])


def moe_backward_kernel(loads, start_ref, spread_place, w_in, w_out, dy_ref, slope_ref, d_c, back_ref):
    expert = pl.program_id(0)
    seq, capacity, parts = (d_c.shape[0], dy_ref.shape[0], w_in.shape[1])
    width = w_in.shape[3]

    @pl.when(expert == 0)
    def _():
        d_c[...] = start_ref[...]

    def work(count):
        at = pl.ds(0, count)
        d_y = dy_ref[at, :]
        back = jnp.zeros((count, D), FULLTYPE)
        for part in range(parts):
            units = pl.ds(part * width, width)
            d_act = right_t(d_y, w_out[0, units, :])
            d_h = (d_act * slope_ref[at, units]).astype(LOWTYPE)
            back += right_t(d_h, w_in[0, part])
        back_ref[at, :] = back.astype(LOWTYPE)

        def add(i, carry):
            rows = rows_of(i)
            d_c[rows, :] += plain(patch_select(spread_place[0, rows, :], count), back_ref[at, :])
            return carry

        lax.fori_loop(0, seq // ROWS, add, 0)

    by_load(loads[expert], capacity, work)


def moe_weight_kernel(count, *refs):
    rows_refs, dy_refs = (refs[:count], refs[count : 2 * count])
    w_in, w_out, d_in, d_out = refs[2 * count :]

    @pl.when(pl.program_id(0) == 0)
    def _():
        d_in[...] = jnp.zeros_like(d_in)
        d_out[...] = jnp.zeros_like(d_out)

    width = w_in.shape[1]
    step = 384 if width % 384 == 0 else width
    for rows_ref, dy_ref in zip(rows_refs, dy_refs):
        rows, d_y = (rows_ref[...], dy_ref[...])
        for first in range(0, width, step):
            units = pl.ds(first, step)
            act, slope = gelu_pair(plain(rows, w_in[:, units]))
            d_h = (right_t(d_y, w_out[units, :]) * slope).astype(LOWTYPE)
            d_out[units, :] += left_t(act.astype(LOWTYPE), d_y)
            d_in[:, units] += left_t(rows, d_h)


def whole(shape):
    return pl.BlockSpec(shape, lambda e: (0,) * len(shape))


def gridded(kernel, steps, in_specs, outs, out_specs, args, flops, scratch=()):
    moved = sum(math.prod(a.shape) * a.dtype.itemsize for a in (*args, *outs))
    return pl.pallas_call(
        kernel,
        grid=(steps,),
        out_shape=outs,
        in_specs=in_specs,
        out_specs=out_specs,
        scratch_shapes=scratch,
        compiler_params=pltpu.CompilerParams(vmem_limit_bytes=VMEM_LIMIT),
        cost_estimate=pl.CostEstimate(flops=flops, bytes_accessed=moved, transcendentals=0),
    )(*args)


SCALARS = pl.BlockSpec(memory_space=pltpu.SMEM)


def in_spec(w_in):
    return pl.BlockSpec((1,) + w_in.shape[1:], lambda e: (e, 0, 0, 0))


def out_spec(w_out):
    return pl.BlockSpec((1,) + w_out.shape[1:], lambda e: (e, 0, 0))


def spread_spec(seq):
    return pl.BlockSpec((1, seq, 128), lambda e: (e, 0, 0))


def moe_up(loads, c16, router, table, place, w_in, capacity):
    seq, experts = table.shape
    hidden = w_in.shape[1] * w_in.shape[3]
    per = lambda width: pl.BlockSpec((capacity, width), lambda e: (e, 0))
    return gridded(
        moe_up_kernel,
        experts,
        [SCALARS, whole((seq, D)), whole((D, experts)), whole((seq, experts))]
        + [pl.BlockSpec((1, 1, seq), lambda e: (e, 0, 0)), in_spec(w_in)],
        [
            shaped((seq, experts), FULLTYPE),
            shaped((experts, seq, 128), FULLTYPE),
            shaped((experts, seq, 128), FULLTYPE),
            shaped((experts * capacity, D), LOWTYPE),
            shaped((experts * capacity, hidden), LOWTYPE),
            shaped((experts * capacity, hidden), FULLTYPE),
        ],
        [whole((seq, experts)), spread_spec(seq), spread_spec(seq), per(D), per(hidden), per(hidden)],
        [loads, c16, router, table, place, w_in],
        2 * experts * capacity * D * (hidden + seq),
    )


def moe_down(loads, mid, spread_place, spread_gate, act, w_out):
    seq, experts = (mid.shape[0], w_out.shape[0])
    capacity, hidden = (act.shape[0] // experts, act.shape[1])
    per = lambda width: pl.BlockSpec((capacity, width), lambda e: (e, 0))
    return gridded(
        moe_down_kernel,
        experts,
        [SCALARS, whole((seq, D)), spread_spec(seq), spread_spec(seq), per(hidden), out_spec(w_out)],
        [shaped((seq, D), FULLTYPE), shaped((experts * capacity, D), LOWTYPE)],
        [whole((seq, D)), per(D)],
        [loads, mid, spread_place, spread_gate, act, w_out],
        2 * experts * capacity * D * (hidden + seq),
    )


def moe_gate_backward(loads, grad, c16, router, gates, place, spread_place, spread_gate, y16):
    seq, experts = gates.shape
    capacity = y16.shape[0] // experts
    per = pl.BlockSpec((capacity, D), lambda e: (e, 0))
    return gridded(
        moe_gate_kernel,
        experts,
        [SCALARS, whole((seq, D)), whole((seq, D)), whole((D, experts)), whole((seq, experts))]
        + [pl.BlockSpec((1, 1, seq), lambda e: (e, 0, 0)), spread_spec(seq), spread_spec(seq), per],
        [
            shaped((D, experts), FULLTYPE),
            shaped((seq, D), FULLTYPE),
            shaped((experts * capacity, D), LOWTYPE),
        ],
        [whole((D, experts)), whole((seq, D)), per],
        [loads, grad, c16, router, gates, place, spread_place, spread_gate, y16],
        4 * experts * capacity * D * seq,
        [
            pltpu.VMEM((seq, D), LOWTYPE),
            pltpu.VMEM((seq, experts), LOWTYPE),
            pltpu.VMEM((seq, experts), FULLTYPE),
        ],
    )


def moe_backward(loads, start, spread_place, w_in, w_out, dy16, slope):
    seq, experts = (start.shape[0], w_out.shape[0])
    capacity, hidden = (dy16.shape[0] // experts, w_out.shape[1])
    per = lambda width: pl.BlockSpec((capacity, width), lambda e: (e, 0))
    return gridded(
        moe_backward_kernel,
        experts,
        [SCALARS, whole((seq, D)), spread_spec(seq), in_spec(w_in), out_spec(w_out)]
        + [per(D), per(hidden)],
        [shaped((seq, D), FULLTYPE)],
        [whole((seq, D))],
        [loads, start, spread_place, w_in, w_out, dy16, slope],
        2 * experts * capacity * D * (2 * hidden + seq),
        [pltpu.VMEM((capacity, D), LOWTYPE)],
    )[0]


def moe_weight_backward(rows, dy, w_in, w_out):
    count, width = (rows[0].shape[0], w_in.shape[1])
    step = 512
    per = pl.BlockSpec((step, D), lambda i: (i, 0))
    return gridded(
        functools.partial(moe_weight_kernel, len(rows)),
        count // step,
        [per] * (2 * len(rows)) + [whole((D, width)), whole((width, D))],
        [shaped((D, width), FULLTYPE), shaped((width, D), FULLTYPE)],
        [whole((D, width)), whole((width, D))],
        [*rows, *dy, w_in, w_out],
        10 * count * len(rows) * D * width,
    )


def flat_plan(experts):
    shapes = [(PIX, D)] + [(D, 3 * D)] * 3 + [(D, D)] * 3 + [(D, FF)] * 2 + [(FF, D)] * 2
    plan, start = [], 0
    for height, width in shapes:
        plan.append((start, height, width // 128))
        start += height * width // 128
    return (plan, start)


def owner_rows(shard, parts):
    return -(-((shard + 127 + 127) // 128) // (16 * parts)) * 16 * parts


def chunk_of(rows, most=128):
    return max(c for c in range(16, most + 1, 16) if rows % c == 0)


def unpack_kernel(plan, shard, parts_ref, *refs):
    outs, rest, flat = (refs[: len(plan)], refs[len(plan)], refs[len(plan) + 1])
    owners, rows = parts_ref.shape[:2]
    chunk = chunk_of(rows)
    for owner in range(owners):
        first = shard * owner // 128
        if owner:
            last = flat[pl.ds(first, 1), :]

        def copy(i, carry, owner=owner, first=first):
            flat[pl.ds(first + i * chunk, chunk), :] = parts_ref[
                owner, pl.ds(pl.multiple_of(i * chunk, chunk), chunk), :
            ].astype(FULLTYPE)
            return carry

        lax.fori_loop(0, rows // chunk, copy, 0)
        if owner and shard * owner % 128:
            flat[pl.ds(first, 1), :] += last
    for (start, height, across), out in zip(plan, outs):

        def place(i, carry, start=start, across=across, out=out):
            for c in range(across):
                taken = flat[pl.ds(start + i * 128 * across + c, 128, stride=across), :]
                out[rows_of(i, 128), pl.ds(c * 128, 128)] = taken.astype(LOWTYPE)
            return carry

        lax.fori_loop(0, height // 128, place, 0)
    start = plan[-1][0] + plan[-1][1] * plan[-1][2]
    rest[...] = flat[pl.ds(start, rest.shape[0]), :]


def unpack_weights(parts, shard, experts):
    plan, start = flat_plan(experts)
    owners, rows = parts.shape[:2]
    rest = shard * owners // 128 - start
    outs = [shaped((height, across * 128), LOWTYPE) for _, height, across in plan]
    outs.append(shaped((rest, 128), FULLTYPE))
    flat = pltpu.VMEM((-(-(shard * (owners - 1) // 128 + rows) // 8) * 8, 128), FULLTYPE)
    return local_call(
        functools.partial(unpack_kernel, plan, shard), outs, [parts], 0, [flat]
    )


def pack_kernel(plan, shard, select, place_ref, *refs):
    count = len(plan)
    mats, rest, norms = (refs[:count], refs[count], refs[count + 1 : count + 5])
    outs, flat = (refs[count + 5 : -1], refs[-1])
    for (start, height, across), mat in zip(plan, mats):

        def place(i, carry, start=start, across=across, mat=mat):
            for c in range(across):
                flat[pl.ds(start + i * 128 * across + c, 128, stride=across), :] = mat[
                    rows_of(i, 128), pl.ds(c * 128, 128)
                ]
            return carry

        lax.fori_loop(0, height // 128, place, 0)
    start = plan[-1][0] + plan[-1][1] * plan[-1][2]
    flat[pl.ds(start, rest.shape[0]), :] = rest[...]
    start += rest.shape[0]
    for kind in (0, 1):
        for layer, norm in enumerate(norms):
            for k in range(2 if layer < 3 else 1):
                for c in range(D // 128):
                    row = start + ((7 * kind + 2 * layer + k) * D) // 128 + c
                    flat[row : row + 1, :] = norm[2 * k + kind : 2 * k + kind + 1, c * 128 : c * 128 + 128]
    for out, which in zip(outs, select):
        groups, owners, rows = out.shape[:3]
        chunk = chunk_of(rows)
        for group in range(groups):
            for owner in range(owners):
                member = which(place_ref[0], group)
                first = shard * owner // 128 + member * rows

                def copy(i, carry, out=out, group=group, owner=owner, first=first):
                    out[group, owner, pl.ds(pl.multiple_of(i * chunk, chunk), chunk), :] = flat[
                        pl.ds(first + i * chunk, chunk), :
                    ].astype(out.dtype)
                    return carry

                lax.fori_loop(0, rows // chunk, copy, 0)


def pack_gradients(mats, rest, norms, shard, owners, groups, place, experts):
    plan, _ = flat_plan(experts)
    rows = owner_rows(shard, groups)
    part = rows // groups
    if groups == 2:
        outs = [shaped((1, owners, part, 128), t) for t in (FULLTYPE, EXCHANGE)]
        select = [lambda here, g: here, lambda here, g: 1 - here]
    else:
        outs = [shaped((groups, owners, part, 128), FULLTYPE)]
        select = [lambda here, g: g]
    flat = pltpu.VMEM((-(-(shard * (owners - 1) // 128 + rows) // 8) * 8, 128), FULLTYPE)
    args = [place.reshape(1), *mats, rest, *norms]
    moved = sum(math.prod(a.shape) * a.dtype.itemsize for a in (*args, *outs))
    return pl.pallas_call(
        functools.partial(pack_kernel, plan, shard, select),
        out_shape=outs,
        in_specs=[SCALARS] + in_vmem(len(args) - 1),
        out_specs=in_vmem(len(outs)),
        scratch_shapes=[flat],
        compiler_params=pltpu.CompilerParams(vmem_limit_bytes=PACK_LIMIT),
        cost_estimate=pl.CostEstimate(flops=0, bytes_accessed=moved, transcendentals=0),
    )(*args)


EXCHANGE = jnp.bfloat16
PACK_LIMIT = 60 * 2**20


def swap_dp(value):
    return lax.ppermute(value, "dp", [(0, 1), (1, 0)])


def join_dp(value, place):
    groups = lax.axis_size("dp")
    if groups != 2:
        return lax.all_gather(value, "dp")
    other = swap_dp(value)
    first = place == 0
    return jnp.stack([jnp.where(first, value, other), jnp.where(first, other, value)])


def sum_scatter_dp(parts, place):
    groups = lax.axis_size("dp")
    if groups != 2:
        return lax.psum_scatter(parts, "dp", scatter_dimension=0, tiled=True)[0]
    first = place == 0
    mine = jnp.where(first, parts[0], parts[1])
    return mine + swap_dp(jnp.where(first, parts[1], parts[0]))


def sum_all(value):
    for axis in ("dp", "ep"):
        count = lax.axis_size(axis)
        step = 1
        while step < count:
            value = value + lax.ppermute(value, axis, [(i, i ^ step) for i in range(count)])
            step *= 2
    return value


def to_experts(buffer):
    return lax.all_to_all(buffer, "ep", split_axis=0, concat_axis=0, tiled=True)


def per_device(
    patches,
    labels,
    pixel_mask,
    patch_valid,
    tasks,
    routes,
    dense_weight,
    dense_first,
    dense_second,
    dense_average,
    expert_in,
    in_first,
    in_second,
    in_average,
    expert_out,
    out_first,
    out_second,
    out_average,
):
    ep_count = lax.axis_size("ep")
    experts = min(16, ep_count)
    copies = ep_count // experts
    groups = lax.axis_size("dp")
    ep_place = lax.axis_index("ep")
    dp_place = lax.axis_index("dp")
    own_expert = ep_place // copies
    seq = patches.shape[0]
    capacity = 3 * seq * TOP // (2 * experts)
    shard = dense_weight.shape[0]
    piece = shard // groups
    edges = segment_edges(experts)
    block_count = len(edges) + 1 + 2 * experts
    span, firsts = owner_blocks(edges, shard, ep_count)
    first_block = firsts[ep_place]
    starts = [
        jnp.take(jnp.array([0] + edges + [shard * ep_count] * span, jnp.int32), first_block + k)
        - ep_place * shard
        for k in range(span + 1)
    ]

    def placed(value, at, count):
        return jnp.where(jnp.arange(count) == at, value, 0.0)

    def block_sums(dense_vals, in_vals, out_vals):
        part = lax.dynamic_slice_in_dim(dense_vals, dp_place * piece, piece)
        square = part * part
        index = dp_place * piece + jnp.arange(piece, dtype=jnp.int32)
        listed = placed(jnp.sum(in_vals * in_vals), len(edges) + 1 + own_expert, block_count)
        listed += placed(
            jnp.sum(out_vals * out_vals), len(edges) + 1 + experts + own_expert, block_count
        )
        for k in range(span):
            inside = (index >= starts[k]) & (index < starts[k + 1])
            listed += placed(jnp.sum(jnp.where(inside, square, 0.0)), first_block + k, block_count)
        return listed

    rows = owner_rows(shard, groups)
    offset = lax.rem(ep_place * (shard % 128), 128)
    spread = lax.dynamic_update_slice(
        jnp.zeros((rows * 128,), LOWTYPE), dense_weight.astype(LOWTYPE), (offset,)
    )
    own_part = lax.dynamic_index_in_dim(
        spread.reshape(groups, rows // groups, 128), dp_place, 0, keepdims=False
    )
    parts = lax.all_gather(own_part, ("ep", "dp")).reshape(ep_count, rows, 128)
    low_in, low_out = (expert_in[0].astype(LOWTYPE), expert_out[0].astype(LOWTYPE))
    all_in = lax.all_gather(low_in, ("ep", "dp"))
    all_out = lax.all_gather(low_out, ("ep", "dp"))
    width = low_in.shape[1]
    w_in = all_in.reshape(experts, copies * groups, D, width)
    if width % 128:
        w_in = jnp.swapaxes(w_in, 1, 2).reshape(experts, 1, D, copies * groups * width)
    w_out = all_out.reshape(experts, copies * groups * width, D)

    named = jnp.sum(
        (routes[:, :, None] == jnp.arange(experts, dtype=jnp.int32)[None, None, :]).astype(FULLTYPE),
        1,
    )
    earlier = jnp.arange(seq)[:, None] > jnp.arange(seq)[None, :]
    table = jnp.where(named > 0, plain(earlier.astype(LOWTYPE), named.astype(LOWTYPE)), -1.0)
    place = table.T.reshape(experts, 1, seq)
    loads = jnp.sum(named, 0).astype(jnp.int32)
    bias = jnp.where(patch_valid > 0, 0.0, NEG).astype(FULLTYPE)
    across, down = (bias.reshape(1, seq), bias.reshape(seq, 1))
    weight_pix = (pixel_mask * patch_valid[:, None]).astype(FULLTYPE)
    count_tok = jnp.sum(weight_pix, 1)
    class_hot = labels[:, :, None] == jnp.arange(C, dtype=jnp.int32)[None, None, :]
    counts = jnp.sum(jnp.where(class_hot, weight_pix[:, :, None], 0.0), 1)
    total = sum_all(jnp.sum(count_tok).reshape(1))[0]

    together = lax.optimization_barrier
    weight_sums = block_sums(dense_weight, expert_in, expert_out)
    parts, counts, count_tok, total, table, place, loads, across, down, weight_sums = together(
        (parts, counts, count_tok, total, table, place, loads, across, down, weight_sums)
    )
    *mats, rest = unpack_weights(parts, shard, experts)
    w_patch, w_qkv, w_attn = (mats[0], mats[1:4], mats[4:7])
    w_up, w_down = (mats[7:9], mats[9:11])
    router_rows, head_rows = (TASKS * D * experts // 128, D * C // 128)
    w_router = rest[:router_rows].reshape(TASKS, D, experts).astype(LOWTYPE)
    w_head = rest[router_rows : router_rows + head_rows].reshape(D, C).astype(LOWTYPE)
    norms = rest[router_rows + head_rows :].reshape(2, 7, D)
    task = tasks[0]
    router = lax.dynamic_index_in_dim(w_router, task, 0, keepdims=False)

    def dispatch(send, block):
        third = capacity // 3
        taken = send.reshape(experts, capacity, D)[:, block * third : (block + 1) * third]
        return to_experts(jnp.repeat(taken, copies, axis=0)).reshape(-1, D)

    together = lax.optimization_barrier

    def norm_rows(layer):
        rows = [norms[0, 2 * layer], norms[1, 2 * layer]]
        if layer < 3:
            rows += [norms[0, 2 * layer + 1], norms[1, 2 * layer + 1]]
        return jnp.pad(jnp.stack(rows), ((0, 8 - len(rows)), (0, 0)))

    x0, *kept0, x1, act0, slope0 = layer_forward(
        patches, w_patch, w_qkv[0], w_attn[0], norm_rows(0), across, w_up[0], w_down[0]
    )
    mid1, c16, *kept1 = layer_forward(
        x1, None, w_qkv[1], w_attn[1], norm_rows(1), across, None, None
    )
    gates, spread_place, spread_gate, sent, act1, slope1 = moe_up(
        loads, c16, router, table, place, w_in, capacity
    )
    x2, y16 = moe_down(loads, mid1, spread_place, spread_gate, act1, w_out)
    x2, sent = together((x2, sent))
    rows_a = dispatch(sent, 0)
    *kept2, x3, act2, slope2 = layer_forward(
        x2, None, w_qkv[2], w_attn[2], norm_rows(2), across, w_up[1], w_down[1]
    )
    x3, sent, rows_a = together((x3, sent, rows_a))
    rows_b = dispatch(sent, 1)
    loss_lanes, d_head, d_normf, grad = head_call(
        x3, norm_rows(3), w_head, counts, count_tok, total
    )
    local = loss_lanes[0, 0]
    grad, local = together((grad, local))
    d_qkv2, d_attn2, d_norm2, d_up1, d_down1, grad = layer_backward(
        grad, x2, (*kept2, act2, slope2), w_qkv[2], w_attn[2], norm_rows(2), down,
        (w_up[1], w_down[1]), None, None,
    )
    grad, sent, rows_b = together((grad, sent, rows_b))
    rows_c = dispatch(sent, 2)
    d_own_router, d_c, dy16 = moe_gate_backward(
        loads, grad, c16, router, gates, place, spread_place, spread_gate, y16
    )
    d_c, dy16, rows_c = together((d_c, dy16, rows_c))
    dy_a = dispatch(dy16, 0)
    d_c = moe_backward(loads, d_c, spread_place, w_in, w_out, dy16, slope1)
    d_c, dy16, dy_a = together((d_c, dy16, dy_a))
    dy_b = dispatch(dy16, 1)
    task_hot = (jnp.arange(TASKS, dtype=jnp.int32) == task)[:, None, None]
    d_router = jnp.where(task_hot, d_own_router[None], 0.0)
    d_qkv1, d_attn1, d_norm1, grad = layer_backward(
        grad, x1, (mid1, c16, *kept1), w_qkv[1], w_attn[1], norm_rows(1), down, None, d_c, None
    )
    grad, dy16, dy_b = together((grad, dy16, dy_b))
    dy_c = dispatch(dy16, 2)
    d_qkv0, d_attn0, d_norm0, d_up0, d_down0, d_patch = layer_backward(
        grad, x0, (*kept0, act0, slope0), w_qkv[0], w_attn[0], norm_rows(0), down,
        (w_up[0], w_down[0]), None, patches,
    )
    d_patch, dy_c = together((d_patch, dy_c))
    expert_rows, expert_dy = ([rows_a, rows_b, rows_c], [dy_a, dy_b, dy_c])
    d_rest = jnp.concatenate(
        [
            d_router.reshape(router_rows, 128),
            d_head[:, :C].reshape(head_rows, 128),
        ]
    )
    packed = pack_gradients(
        [d_patch, d_qkv0, d_qkv1, d_qkv2, d_attn0, d_attn1, d_attn2, d_up0, d_up1, d_down0, d_down1],
        d_rest, [d_norm0, d_norm1, d_norm2, d_normf], shard, ep_count, groups, dp_place, experts,
    )
    if groups == 2:
        summed = packed[0][0] + swap_dp(packed[1][0]).astype(FULLTYPE)
    else:
        summed = lax.psum_scatter(packed[0], "dp", scatter_dimension=0, tiled=True)[0]
    arrived = to_experts(summed.astype(LOWTYPE))

    own_in = lax.dynamic_index_in_dim(
        all_in.reshape(ep_count, groups, D, width), ep_place, 0, keepdims=False
    )
    own_out = lax.dynamic_index_in_dim(
        all_out.reshape(ep_count, groups, width, D), ep_place, 0, keepdims=False
    )
    if groups == 2:

        def weight_grads(member):
            return moe_weight_backward(
                expert_rows,
                expert_dy,
                lax.dynamic_index_in_dim(own_in, member, 0, keepdims=False),
                lax.dynamic_index_in_dim(own_out, member, 0, keepdims=False),
            )

        theirs = weight_grads(1 - dp_place)
        away = [swap_dp(t.astype(jnp.bfloat16)) for t in theirs]
        mine = weight_grads(dp_place)
        mine, away, arrived = together((mine, away, arrived))
        d_in, d_out = [(m + t.astype(FULLTYPE))[None] for m, t in zip(mine, away)]
    else:
        d_in, d_out = moe_weight_backward(
            expert_rows,
            expert_dy,
            jnp.swapaxes(own_in, 0, 1).reshape(D, groups * width),
            own_out.reshape(groups * width, D),
        )
        d_in, d_out = (
            lax.psum_scatter(
                value[None].astype(jnp.bfloat16), "dp", scatter_dimension=axis, tiled=True
            ).astype(FULLTYPE)
            for value, axis in ((d_in, 2), (d_out, 1))
        )
    own_sum = jnp.sum(arrived.astype(FULLTYPE), 0)
    dense_grad = lax.dynamic_slice_in_dim(
        join_dp(own_sum, dp_place).reshape(-1), offset, shard
    )
    sums = sum_all(
        placed(local, 0, 2 + block_count)
        + placed(jnp.sum(block_sums(dense_grad, d_in, d_out)), 1, 2 + block_count)
        + jnp.pad(weight_sums, (2, 0))
    )
    loss, grad_total, weight_total = (sums[0] / total, sums[1], sums[2:])
    grad_norm = jnp.sqrt(grad_total)
    clip = CLIP_NORM / jnp.maximum(grad_norm, CLIP_NORM)

    def moments(weight, first, second, gradient):
        gradient = gradient * clip
        first_new = DECAY_ONE * first + (1.0 - DECAY_ONE) * gradient
        second_new = DECAY_TWO * second + (1.0 - DECAY_TWO) * gradient * gradient
        return (
            first_new,
            second_new,
            first_new / (jnp.sqrt(second_new) + EPS_ADAM) + WEIGHT_DECAY * weight,
        )

    dense_m, dense_v, dense_step = moments(dense_weight, dense_first, dense_second, dense_grad)
    in_m, in_v, in_step = moments(expert_in, in_first, in_second, d_in)
    out_m, out_v, out_step = moments(expert_out, out_first, out_second, d_out)
    update_total = sum_all(block_sums(dense_step, in_step, out_step))
    weight_norm = jnp.sqrt(weight_total)
    update_norm = jnp.sqrt(update_total)
    ratio = weight_norm / (update_norm + EPS_NORM)
    whole_index = jnp.arange(shard, dtype=jnp.int32)
    dense_ratio = jnp.broadcast_to(jnp.take(ratio, first_block), (shard,))
    for k in range(1, span):
        dense_ratio = jnp.where(whole_index >= starts[k], jnp.take(ratio, jnp.minimum(first_block + k, block_count - 1)), dense_ratio)
    in_ratio = lax.dynamic_index_in_dim(ratio, 14 + own_expert, 0, keepdims=False)
    out_ratio = lax.dynamic_index_in_dim(ratio, 14 + experts + own_expert, 0, keepdims=False)

    def finish(weight, average, step, rate):
        new = weight - RATE * rate * step
        return (new, AVERAGE * average + (1.0 - AVERAGE) * new, new.astype(LOWTYPE))

    dense_new, dense_avg, dense_low = finish(dense_weight, dense_average, dense_step, dense_ratio)
    in_new, in_avg, in_low = finish(expert_in, in_average, in_step, in_ratio)
    out_new, out_avg, out_low = finish(expert_out, out_average, out_step, out_ratio)
    block_norms = jnp.stack([weight_norm, update_norm], 1)
    return (
        loss.reshape(1),
        grad_norm.reshape(1),
        block_norms,
        dense_new,
        dense_m,
        dense_v,
        dense_avg,
        dense_low,
        in_new,
        in_m,
        in_v,
        in_avg,
        in_low,
        out_new,
        out_m,
        out_v,
        out_avg,
        out_low,
    )


def solution(mesh):
    in_specs = (
        P(("ep", "dp"), None),
        P(("ep", "dp"), None),
        P(("ep", "dp"), None),
        P(("ep", "dp")),
        P(("ep", "dp")),
        P(("ep", "dp"), None),
        P("ep"),
        P("ep"),
        P("ep"),
        P("ep"),
        P("ep", None, "dp"),
        P("ep", None, "dp"),
        P("ep", None, "dp"),
        P("ep", None, "dp"),
        P("ep", "dp", None),
        P("ep", "dp", None),
        P("ep", "dp", None),
        P("ep", "dp", None),
    )
    out_specs = (
        P(),
        P(),
        P(),
        P("ep"),
        P("ep"),
        P("ep"),
        P("ep"),
        P("ep"),
        P("ep", None, "dp"),
        P("ep", None, "dp"),
        P("ep", None, "dp"),
        P("ep", None, "dp"),
        P("ep", None, "dp"),
        P("ep", "dp", None),
        P("ep", "dp", None),
        P("ep", "dp", None),
        P("ep", "dp", None),
        P("ep", "dp", None),
    )
    return jax.shard_map(
        per_device, mesh=mesh, in_specs=in_specs, out_specs=out_specs, check_vma=False
    )
```

```python
import functools
import math

import jax
import jax.numpy as jnp
from jax import lax
from jax.experimental import pallas as pl
from jax.experimental.pallas import tpu as pltpu
from jax.sharding import PartitionSpec as P

D = 384
HEADS = 6
HD = 64
FF = 1536
TOP = 4
C = 40
PIX = 768
TASKS = 4


EPS_NORM = 1e-05
CLIP_NORM = 0.002
RATE = 0.3
DECAY_ONE = 0.5
DECAY_TWO = 0.5
WEIGHT_DECAY = 0.01
EPS_ADAM = 1e-09
AVERAGE = 0.9
SCALE = 0.125
LOWTYPE = jnp.bfloat16
FULLTYPE = jnp.float32


def plain(left, right):
    return jnp.dot(left, right, preferred_element_type=FULLTYPE)


def left_t(left, right):
    return lax.dot_general(left, right, (((0,), (0,)), ((), ())), preferred_element_type=FULLTYPE)


def right_t(left, right):
    return lax.dot_general(left, right, (((1,), (1,)), ((), ())), preferred_element_type=FULLTYPE)


def segment_sizes(experts):
    return (
        [PIX * D]
        + [3 * D * D] * 3
        + [D * D] * 3
        + [D * FF] * 2
        + [FF * D] * 2
        + [TASKS * D * experts, D * C, 14 * D]
    )


def owner_blocks(edges, shard, owners):
    firsts = [sum(edge <= shard * i for edge in edges) for i in range(owners)]
    lasts = [sum(edge < shard * (i + 1) for edge in edges) for i in range(owners)]
    span = max(b - a + 1 for a, b in zip(firsts, lasts))
    return (span, jnp.array(firsts, jnp.int32))


def segment_edges(experts):
    edges, edge = [], 0
    for size in segment_sizes(experts)[:-1]:
        edge += size
        edges.append(edge)
    return edges


VMEM_LIMIT = 56 * 2**20
ROWS = 256
TILE = 32
KEYS = 64
QUERIES = 512
NEG = -1e30


def rows_of(index, size=ROWS):
    return pl.ds(pl.multiple_of(index * size, size), size)


def norm_parts(x):
    cent = x - jnp.mean(x, -1, keepdims=True)
    scale = lax.rsqrt(jnp.mean(cent * cent, -1, keepdims=True) + EPS_NORM)
    return (cent * scale, scale)


def norm_low(x, gain, bias):
    return (norm_parts(x)[0] * gain + bias).astype(LOWTYPE)


def norm_pull(x, gain, grad):
    unit, scale = norm_parts(x)
    inner = grad * gain
    d_x = scale * (
        inner
        - jnp.mean(inner, -1, keepdims=True)
        - unit * jnp.mean(inner * unit, -1, keepdims=True)
    )
    return (d_x, jnp.sum(grad * unit, 0, keepdims=True), jnp.sum(grad, 0, keepdims=True))


def gelu_pair(h):
    cdf = 0.5 + 0.5 * lax.erf(h * 0.7071067811865476)
    e = jnp.exp((h * h) * -0.5)
    return (h * cdf, cdf + h * (e * 0.3989422804014327))


def half_masks(scale):
    lane = lax.broadcasted_iota(jnp.int32, (1, 128), 1)
    return [jnp.where((lane < HD) == (h == 0), scale, 0.0).astype(LOWTYPE) for h in (0, 1)]


def beside_head(head, own, extras):
    lane = lax.broadcasted_iota(jnp.int32, own.shape, 1)
    value = own.astype(FULLTYPE) * half_masks(1.0)[head].astype(FULLTYPE)
    for k, extra in enumerate(extras):
        value = jnp.where(lane == HD * (1 - head) + k, extra, value)
    return value.astype(LOWTYPE)


def three_parts(column):
    high = column.astype(LOWTYPE).astype(FULLTYPE)
    middle = (column - high).astype(LOWTYPE).astype(FULLTYPE)
    return [high, middle, column - high - middle]


def attend_rows(qkv_ref, bias_ref, o_ref, aug_ref, keys_ref, s_ref, p_ref):
    seq = qkv_ref.shape[0]
    masks = half_masks(SCALE)
    lane = lax.broadcasted_iota(jnp.int32, (ROWS, 128), 1)

    for pair in range(HEADS // 2):
        cols = pl.ds(pair * 128, 128)

        def prepare(i, carry, pair=pair):
            rows = rows_of(i)
            keys = qkv_ref[rows, pl.ds(D + pair * 128, 128)]
            for h in (0, 1):
                keys_ref[h, rows, :] = beside_head(h, keys, [bias_ref[rows, :]])
            return carry

        lax.fori_loop(0, seq // ROWS, prepare, 0)

        def body(i, carry, pair=pair, cols=cols):
            rows = rows_of(i)
            query = qkv_ref[rows, cols]
            values = qkv_ref[:, pl.ds(2 * D + pair * 128, 128)]
            outs = []
            for h in (0, 1):
                s_ref[h] = right_t(beside_head(h, query * masks[h], [1.0]), keys_ref[h])
            for h in (0, 1):
                for first in range(0, ROWS, TILE):
                    s = s_ref[h, first : first + TILE, :]
                    top = jnp.max(s, -1, keepdims=True)
                    e = jnp.exp(s - top)
                    total = jnp.sum(e, -1, keepdims=True)
                    p_ref[h, first : first + TILE, :] = (e * (1.0 / total)).astype(LOWTYPE)
                    at = pl.ds(pl.multiple_of(i * ROWS + first, TILE), TILE)
                    aug_ref[at, pl.ds((2 * pair + h) * 128, 128)] = beside_head(
                        h,
                        query[first : first + TILE] * masks[h],
                        [1.0] + three_parts(-(top + jnp.log(total))),
                    )
            for h in (0, 1):
                outs.append(plain(p_ref[h], values))
            o_ref[rows, cols] = jnp.where(lane < HD, outs[0], outs[1]).astype(LOWTYPE)
            return carry

        lax.fori_loop(0, seq // ROWS, body, 0)


def forward_kernel(has_patch, has_ff, *refs):
    refs = list(refs)
    x_in = refs.pop(0)
    if has_patch:
        w_patch = refs.pop(0)
    w_qkv, w_attn, norms, bias = refs[:4]
    refs = refs[4:]
    if has_ff:
        w_up, w_down = refs[:2]
        refs = refs[2:]
    if has_patch:
        x_ref = refs.pop(0)
    else:
        x_ref = x_in
    mid_ref, c_ref, qkv_ref, o_ref, aug_ref = refs[:5]
    refs = refs[5:]
    if has_ff:
        next_ref, act_ref, slope_ref = refs[:3]
    keys_ref, s_ref, p_ref = refs[-3:]
    seq = x_ref.shape[0]

    def project(i, carry):
        rows = rows_of(i)
        if has_patch:
            x_ref[rows, :] = plain(x_in[rows, :], w_patch[...])
        a16 = norm_low(x_ref[rows, :], norms[0:1, :], norms[1:2, :])
        qkv_ref[rows, :] = plain(a16, w_qkv[...]).astype(LOWTYPE)
        return carry

    lax.fori_loop(0, seq // ROWS, project, 0)
    attend_rows(qkv_ref, bias, o_ref, aug_ref, keys_ref, s_ref, p_ref)

    def finish(i, carry):
        rows = rows_of(i)
        mid = x_ref[rows, :] + plain(o_ref[rows, :], w_attn[...])
        mid_ref[rows, :] = mid
        c16 = norm_low(mid, norms[2:3, :], norms[3:4, :])
        c_ref[rows, :] = c16
        if has_ff:
            act, slope = gelu_pair(plain(c16, w_up[...]))
            act16 = act.astype(LOWTYPE)
            act_ref[rows, :] = act16
            slope_ref[rows, :] = slope
            next_ref[rows, :] = mid + plain(act16, w_down[...])
        return carry

    lax.fori_loop(0, seq // ROWS, finish, 0)


def in_vmem(count):
    return [pl.BlockSpec(memory_space=pltpu.VMEM)] * count


def local_call(kernel, outs, args, flops, scratch=()):
    moved = sum(math.prod(a.shape) * a.dtype.itemsize for a in (*args, *outs))
    return pl.pallas_call(
        kernel,
        out_shape=outs,
        in_specs=in_vmem(len(args)),
        out_specs=in_vmem(len(outs)),
        scratch_shapes=scratch,
        compiler_params=pltpu.CompilerParams(vmem_limit_bytes=VMEM_LIMIT),
        cost_estimate=pl.CostEstimate(flops=flops, bytes_accessed=moved, transcendentals=0),
    )(*args)


def shaped(shape, dtype):
    return jax.ShapeDtypeStruct(shape, dtype)


def layer_forward(x, w_patch, w_qkv, w_attn, norms, bias, w_up, w_down):
    seq = x.shape[0]
    has_patch, has_ff = (w_patch is not None, w_up is not None)
    args = [x] + [w_patch] * has_patch + [w_qkv, w_attn, norms, bias] + [w_up, w_down] * has_ff
    outs = [shaped((seq, D), FULLTYPE)] * has_patch
    outs += [
        shaped((seq, D), FULLTYPE),
        shaped((seq, D), LOWTYPE),
        shaped((seq, 3 * D), LOWTYPE),
        shaped((seq, D), LOWTYPE),
        shaped((seq, 128 * HEADS), LOWTYPE),
    ]
    if has_ff:
        outs += [
            shaped((seq, D), FULLTYPE),
            shaped((seq, FF), LOWTYPE),
            shaped((seq, FF), FULLTYPE),
        ]
    flops = 2 * seq * D * (4 * D + 4 * seq + 2 * FF * has_ff)
    kernel = functools.partial(forward_kernel, has_patch, has_ff)
    scratch = [
        pltpu.VMEM((2, seq, 128), LOWTYPE),
        pltpu.VMEM((2, ROWS, seq), FULLTYPE),
        pltpu.VMEM((2, ROWS, seq), LOWTYPE),
    ]
    return local_call(kernel, outs, args, flops, scratch)


def attend_pull(qkv_ref, o_ref, do_ref, aug_ref, valid_ref, dqkv_ref, dk_ref, dv_ref, sides):
    seq = qkv_ref.shape[0]
    keys_ref, values_ref, across_ref, s_ref, dp_ref, p_ref, ds_ref = sides
    ones = half_masks(1.0)

    for pair in range(HEADS // 2):
        cols = pl.ds(pair * 128, 128)
        dk_ref[...] = jnp.zeros_like(dk_ref)
        dv_ref[...] = jnp.zeros_like(dv_ref)

        def prepare(i, carry, pair=pair):
            rows = rows_of(i)
            keys = qkv_ref[rows, pl.ds(D + pair * 128, 128)]
            values = qkv_ref[rows, pl.ds(2 * D + pair * 128, 128)]
            across_ref[:, rows] = keys.astype(FULLTYPE).T.astype(LOWTYPE)
            for h in (0, 1):
                keys_ref[h, rows, :] = beside_head(h, keys, [valid_ref[rows, :], 1.0, 1.0, 1.0])
                values_ref[h, rows, :] = beside_head(h, values, [1.0, 1.0, 1.0])
            return carry

        lax.fori_loop(0, seq // ROWS, prepare, 0)

        def body(i, carry, pair=pair, cols=cols):
            rows = rows_of(i, QUERIES)
            d_out = do_ref[rows, cols]
            both = d_out.astype(FULLTYPE) * o_ref[rows, cols].astype(FULLTYPE)
            d_query = []
            for h in (0, 1):
                own_q = aug_ref[rows, pl.ds((2 * pair + h) * 128, 128)]
                s_ref[h] = right_t(keys_ref[h], own_q)
                delta = jnp.sum(both * ones[h].astype(FULLTYPE), -1, keepdims=True)
                own_d = beside_head(h, d_out, three_parts(-delta))
                dp_ref[h] = right_t(values_ref[h], own_d)
            for h in (0, 1):
                for first in range(0, seq, KEYS):
                    at, side = (pl.ds(first, KEYS), pl.ds(h * QUERIES, QUERIES))
                    probs = jnp.exp(s_ref[h, at, :])
                    p_ref[at, side] = probs.astype(LOWTYPE)
                    ds_ref[at, side] = (probs * dp_ref[h, at, :]).astype(LOWTYPE)
            own = [
                aug_ref[rows, pl.ds((2 * pair + h) * 128, 128)] * ones[h] for h in (0, 1)
            ]
            dv_ref[...] += plain(p_ref[...], jnp.concatenate([d_out * ones[h] for h in (0, 1)]))
            dk_ref[...] += plain(ds_ref[...], jnp.concatenate(own))
            for h in (0, 1):
                d_query.append(
                    plain(across_ref[pl.ds(h * HD, HD), :], ds_ref[:, pl.ds(h * QUERIES, QUERIES)])
                )
            turned = jnp.concatenate(d_query).T * SCALE
            dqkv_ref[rows, cols] = turned.astype(LOWTYPE)
            return carry

        lax.fori_loop(0, seq // QUERIES, body, 0)
        dqkv_ref[:, pl.ds(D + pair * 128, 128)] = dk_ref[...].astype(LOWTYPE)
        dqkv_ref[:, pl.ds(2 * D + pair * 128, 128)] = dv_ref[...].astype(LOWTYPE)


def weight_pull(left_ref, right_ref, out_ref, tile=128):
    def body(j, carry):
        cols = rows_of(j, tile)
        out_ref[cols, :] = left_t(left_ref[:, cols], right_ref[...])
        return carry

    lax.fori_loop(0, left_ref.shape[1] // tile, body, 0)


def backward_kernel(has_patch, has_ff, *refs):
    refs = list(refs)
    grad, x_ref, mid_ref, qkv, o_ref, aug, w_qkv, w_attn, norms, valid = refs[:10]
    refs = refs[10:]
    if has_ff:
        c_ref, act, slope, w_up, w_down = refs[:5]
        refs = refs[5:]
    else:
        d_c_ref = refs.pop(0)
    if has_patch:
        patches = refs.pop(0)
    d_qkvw, d_attn, d_norms = refs[:3]
    refs = refs[3:]
    if has_ff:
        d_up, d_down = refs[:2]
        refs = refs[2:]
    if has_patch:
        d_patch = refs.pop(0)
    else:
        dx_ref = refs.pop(0)
    gmid, low, do_ref, dqkv, dk, dv = refs[:6]
    sides, refs = (refs[6:13], refs[13:])
    if has_ff:
        dh_ref = refs.pop(0)
    seq = grad.shape[0]
    blocks_count = seq // ROWS
    d_norms[...] = jnp.zeros_like(d_norms)

    def feed(i, carry):
        rows = rows_of(i)
        g = grad[rows, :]
        if has_ff:
            g16 = g.astype(LOWTYPE)
            low[rows, :] = g16
            dh16 = (right_t(g16, w_down[...]) * slope[rows, :]).astype(LOWTYPE)
            dh_ref[rows, :] = dh16
            d_c = right_t(dh16, w_up[...])
        else:
            d_c = d_c_ref[rows, :]
        d_x, d_gain, d_bias = norm_pull(mid_ref[rows, :], norms[2:3, :], d_c)
        gmid[rows, :] = g + d_x
        d_norms[2:3, :] += d_gain
        d_norms[3:4, :] += d_bias
        return carry

    lax.fori_loop(0, blocks_count, feed, 0)
    if has_ff:
        weight_pull(act, low, d_down)
        weight_pull(c_ref, dh_ref, d_up)

    def out_pull(i, carry):
        rows = rows_of(i)
        g16 = gmid[rows, :].astype(LOWTYPE)
        low[rows, :] = g16
        do_ref[rows, :] = right_t(g16, w_attn[...]).astype(LOWTYPE)
        return carry

    lax.fori_loop(0, blocks_count, out_pull, 0)
    weight_pull(o_ref, low, d_attn)
    attend_pull(qkv, o_ref, do_ref, aug, valid, dqkv, dk, dv, sides)

    def in_pull(i, carry):
        rows = rows_of(i)
        d_a = right_t(dqkv[rows, :], w_qkv[...])
        x = x_ref[rows, :]
        d_x, d_gain, d_bias = norm_pull(x, norms[0:1, :], d_a)
        total = gmid[rows, :] + d_x
        if has_patch:
            gmid[rows, :] = total
        else:
            dx_ref[rows, :] = total
        low[rows, :] = norm_low(x, norms[0:1, :], norms[1:2, :])
        d_norms[0:1, :] += d_gain
        d_norms[1:2, :] += d_bias
        return carry

    lax.fori_loop(0, blocks_count, in_pull, 0)
    weight_pull(low, dqkv, d_qkvw)
    if has_patch:

        def lower(i, carry):
            rows = rows_of(i)
            low[rows, :] = gmid[rows, :].astype(LOWTYPE)
            return carry

        lax.fori_loop(0, blocks_count, lower, 0)
        weight_pull(patches, low, d_patch)


def layer_backward(grad, x, kept, w_qkv, w_attn, norms, valid, ff, d_c, patches):
    seq = grad.shape[0]
    mid, c16, qkv16, o16, aug = kept[:5]
    has_ff, has_patch = (ff is not None, patches is not None)
    args = [grad, x, mid, qkv16, o16, aug, w_qkv, w_attn, norms, valid]
    args += [c16, *kept[5:], *ff] if has_ff else [d_c]
    args += [patches] * has_patch
    outs = [
        shaped((D, 3 * D), FULLTYPE),
        shaped((D, D), FULLTYPE),
        shaped((8, D), FULLTYPE),
    ]
    if has_ff:
        outs += [shaped((D, FF), FULLTYPE), shaped((FF, D), FULLTYPE)]
    outs += [shaped((PIX, D), FULLTYPE) if has_patch else shaped((seq, D), FULLTYPE)]
    scratch = [
        pltpu.VMEM((seq, D), FULLTYPE),
        pltpu.VMEM((seq, D), LOWTYPE),
        pltpu.VMEM((seq, D), LOWTYPE),
        pltpu.VMEM((seq, 3 * D), LOWTYPE),
        pltpu.VMEM((seq, 128), FULLTYPE),
        pltpu.VMEM((seq, 128), FULLTYPE),
        pltpu.VMEM((2, seq, 128), LOWTYPE),
        pltpu.VMEM((2, seq, 128), LOWTYPE),
        pltpu.VMEM((128, seq), LOWTYPE),
        pltpu.VMEM((2, seq, QUERIES), FULLTYPE),
        pltpu.VMEM((2, seq, QUERIES), FULLTYPE),
        pltpu.VMEM((seq, 2 * QUERIES), LOWTYPE),
        pltpu.VMEM((seq, 2 * QUERIES), LOWTYPE),
    ] + [pltpu.VMEM((seq, FF), LOWTYPE)] * has_ff
    flops = 2 * seq * D * (8 * D + 10 * seq + 4 * FF * has_ff + PIX * has_patch)
    return local_call(
        functools.partial(backward_kernel, has_patch, has_ff), outs, args, flops, scratch
    )


def head_kernel(x_ref, norms, w_head, counts, count, total, loss, d_head, d_norms, grad, f_ref, dl_ref):
    seq = x_ref.shape[0]
    d_norms[...] = jnp.zeros_like(d_norms)
    loss[...] = jnp.zeros_like(loss)
    real = lax.broadcasted_iota(jnp.int32, (1, 128), 1) < C

    def body(i, carry):
        rows = rows_of(i)
        x = x_ref[rows, :]
        f16 = norm_low(x, norms[0:1, :], norms[1:2, :])
        f_ref[rows, :] = f16
        logits = plain(f16, w_head[...])
        shown = jnp.where(real, logits, NEG)
        top = jnp.max(shown, -1, keepdims=True)
        e = jnp.exp(shown - top)
        under = jnp.sum(e, -1, keepdims=True)
        weight = count[rows, :]
        classes = counts[rows, :]
        part = weight * (top + jnp.log(under)) - jnp.sum(classes * logits, -1, keepdims=True)
        loss[...] += jnp.broadcast_to(jnp.sum(part, 0, keepdims=True), loss.shape)
        d_logits = ((weight * (e * (1.0 / under)) - classes) / total[...]).astype(LOWTYPE)
        dl_ref[rows, :] = d_logits
        d_x, d_gain, d_bias = norm_pull(x, norms[0:1, :], right_t(d_logits, w_head[...]))
        grad[rows, :] = d_x
        d_norms[0:1, :] += d_gain
        d_norms[1:2, :] += d_bias
        return carry

    lax.fori_loop(0, seq // ROWS, body, 0)
    weight_pull(f_ref, dl_ref, d_head)


def head_call(x, norms, w_head, counts, count, total):
    seq = x.shape[0]
    outs = [
        shaped((1, 128), FULLTYPE),
        shaped((D, 128), FULLTYPE),
        shaped((8, D), FULLTYPE),
        shaped((seq, D), FULLTYPE),
    ]
    args = [
        x,
        norms,
        jnp.pad(w_head, ((0, 0), (0, 128 - C))),
        jnp.pad(counts, ((0, 0), (0, 128 - C))),
        count.reshape(seq, 1),
        total.reshape(1, 1),
    ]
    scratch = [pltpu.VMEM((seq, D), LOWTYPE), pltpu.VMEM((seq, 128), LOWTYPE)]
    return local_call(head_kernel, outs, args, 6 * seq * D * 128, scratch)


SLOTS = 128


def by_load(load, capacity, work):
    for count in range(SLOTS, capacity + 1, SLOTS):
        inside = load > count - SLOTS if count > SLOTS else load >= 0
        if count < capacity:
            inside = inside & (load <= count)
        pl.when(inside)(functools.partial(work, count))


def slot_select(place, count):
    row = lax.broadcasted_iota(jnp.int32, (count, place.shape[1]), 0).astype(FULLTYPE)
    return jnp.where(place == row, 1.0, 0.0).astype(LOWTYPE)


def put_blocks(refs, rows):
    for block, ref in enumerate(refs):
        if block * SLOTS < rows.shape[0]:
            ref[0] = rows[block * SLOTS : (block + 1) * SLOTS]
        else:
            ref[0] = jnp.zeros(ref.shape[1:], ref.dtype)


def column_of(table, expert):
    lane = lax.broadcasted_iota(jnp.int32, table.shape, 1)
    return jnp.sum(jnp.where(lane == expert, table, 0.0), -1, keepdims=True)


def patch_select(spread, count):
    lane = lax.broadcasted_iota(jnp.int32, (1, 128), 1).astype(FULLTYPE)
    return jnp.concatenate(
        [
            jnp.where(spread == lane + first, 1.0, 0.0).astype(LOWTYPE)
            for first in range(0, count, 128)
        ],
        1,
    )


def moe_up_kernel(
    loads, c_ref, router, table, place, w_in,
    gates_ref, spread_place, spread_gate, act_ref, slope_ref, *rows_refs,
):
    expert = pl.program_id(0)
    seq, capacity, parts = (c_ref.shape[0], act_ref.shape[0], w_in.shape[1])
    width = w_in.shape[3]

    @pl.when(expert == 0)
    def _():
        def start(i, carry):
            rows = rows_of(i)
            z = plain(c_ref[rows, :], router[...])
            named = table[rows, :] >= 0
            shown = jnp.where(named, z, NEG)
            e = jnp.where(named, jnp.exp(shown - jnp.max(shown, -1, keepdims=True)), 0.0)
            gates_ref[rows, :] = e / jnp.sum(e, -1, keepdims=True)
            return carry

        lax.fori_loop(0, seq // ROWS, start, 0)

    def fan(i, carry):
        rows = rows_of(i)
        for source, out in ((table, spread_place), (gates_ref, spread_gate)):
            out[0, rows, :] = jnp.broadcast_to(column_of(source[rows, :], expert), (ROWS, 128))
        return carry

    lax.fori_loop(0, seq // ROWS, fan, 0)

    def work(count):
        at = pl.ds(0, count)
        rows = plain(slot_select(place[0], count), c_ref[...]).astype(LOWTYPE)
        put_blocks(rows_refs, rows)
        for part in range(parts):
            step = width // 3 if width % 384 == 0 else width
            for first in range(0, width, step):
                act, slope = gelu_pair(plain(rows, w_in[0, part, :, pl.ds(first, step)]))
                units = pl.ds(part * width + first, step)
                slope_ref[at, units] = slope
                act_ref[at, units] = act.astype(LOWTYPE)

    by_load(loads[expert], capacity, work)


def moe_down_kernel(loads, mid_ref, spread_place, spread_gate, act_ref, w_out, next_ref, y_ref):
    expert = pl.program_id(0)
    seq, capacity = (mid_ref.shape[0], act_ref.shape[0])

    @pl.when(expert == 0)
    def _():
        next_ref[...] = mid_ref[...]

    def work(count):
        at = pl.ds(0, count)
        y_ref[at, :] = plain(act_ref[at, :], w_out[0]).astype(LOWTYPE)
        if count < capacity:
            y_ref[pl.ds(count, capacity - count), :] = jnp.zeros((capacity - count, D), LOWTYPE)

        def add(i, carry):
            rows = rows_of(i)
            taken = plain(patch_select(spread_place[0, rows, :], count), y_ref[at, :])
            for first in range(0, D, 128):
                lanes = pl.ds(first, 128)
                next_ref[rows, lanes] += spread_gate[0, rows, :] * taken[:, first : first + 128]
            return carry

        lax.fori_loop(0, seq // ROWS, add, 0)

    by_load(loads[expert], capacity, work)


def moe_gate_kernel(
    loads, grad_ref, c_ref, router, gates, place, spread_place, spread_gate, y_ref,
    d_router, d_c, *refs,
):
    dy_refs, (low_ref, dz_ref, d_gates) = (refs[:-3], refs[-3:])
    expert = pl.program_id(0)
    seq, capacity = (grad_ref.shape[0], y_ref.shape[0])
    lane = lax.broadcasted_iota(jnp.int32, (ROWS, d_gates.shape[1]), 1)

    @pl.when(expert == 0)
    def _():
        d_gates[...] = jnp.zeros_like(d_gates)

    def work(count):
        at = pl.ds(0, count)

        def one(i, carry):
            rows = rows_of(i)
            grad = grad_ref[rows, :]
            gate = spread_gate[0, rows, :]
            taken = plain(patch_select(spread_place[0, rows, :], count), y_ref[at, :])
            d_gate = jnp.sum(grad * taken, -1, keepdims=True)
            d_gates[rows, :] += jnp.where(lane == expert, d_gate, 0.0)
            for first in range(0, D, 128):
                lanes = pl.ds(first, 128)
                low_ref[rows, lanes] = (gate * grad[:, first : first + 128]).astype(LOWTYPE)
            return carry

        lax.fori_loop(0, seq // ROWS, one, 0)
        put_blocks(dy_refs, plain(slot_select(place[0], count), low_ref[...]).astype(LOWTYPE))

    by_load(loads[expert], capacity, work)

    @pl.when(expert == pl.num_programs(0) - 1)
    def _():
        def last(i, carry):
            rows = rows_of(i)
            gate = gates[rows, :]
            d_gate = d_gates[rows, :]
            d_z = gate * (d_gate - jnp.sum(gate * d_gate, -1, keepdims=True))
            dz_ref[rows, :] = d_z.astype(LOWTYPE)
            d_c[rows, :] = right_t(dz_ref[rows, :], router[...])
            return carry

        lax.fori_loop(0, seq // ROWS, last, 0)
        d_router[...] = left_t(c_ref[...], dz_ref[...])


def moe_backward_kernel(loads, start_ref, spread_place, w_in, w_out, slope_ref, *refs):
    dy_refs, (d_c, back_ref) = (refs[:-2], refs[-2:])
    expert = pl.program_id(0)
    seq, capacity, parts = (d_c.shape[0], slope_ref.shape[0], w_in.shape[1])
    width = w_in.shape[3]

    @pl.when(expert == 0)
    def _():
        d_c[...] = start_ref[...]

    def work(count):
        at = pl.ds(0, count)
        d_y = jnp.concatenate([ref[0] for ref in dy_refs[: count // SLOTS]])
        back = jnp.zeros((count, D), FULLTYPE)
        for part in range(parts):
            units = pl.ds(part * width, width)
            d_act = right_t(d_y, w_out[0, units, :])
            d_h = (d_act * slope_ref[at, units]).astype(LOWTYPE)
            back += right_t(d_h, w_in[0, part])
        back_ref[at, :] = back.astype(LOWTYPE)

        def add(i, carry):
            rows = rows_of(i)
            d_c[rows, :] += plain(patch_select(spread_place[0, rows, :], count), back_ref[at, :])
            return carry

        lax.fori_loop(0, seq // ROWS, add, 0)

    by_load(loads[expert], capacity, work)


def moe_weight_kernel(count, *refs):
    rows_refs, dy_refs = (refs[:count], refs[count : 2 * count])
    w_in, w_out, d_in, d_out = refs[2 * count :]

    @pl.when(pl.program_id(0) == 0)
    def _():
        d_in[...] = jnp.zeros_like(d_in)
        d_out[...] = jnp.zeros_like(d_out)

    width = w_in.shape[1]
    step = 384 if width % 384 == 0 else width
    for rows_ref, dy_ref in zip(rows_refs, dy_refs):
        rows, d_y = (rows_ref[...], dy_ref[...])
        for first in range(0, width, step):
            units = pl.ds(first, step)
            act, slope = gelu_pair(plain(rows, w_in[:, units]))
            d_h = (right_t(d_y, w_out[units, :]) * slope).astype(LOWTYPE)
            d_out[units, :] += left_t(act.astype(LOWTYPE), d_y)
            d_in[:, units] += left_t(rows, d_h)


def whole(shape):
    return pl.BlockSpec(shape, lambda e: (0,) * len(shape))


def gridded(kernel, steps, in_specs, outs, out_specs, args, flops, scratch=()):
    moved = sum(math.prod(a.shape) * a.dtype.itemsize for a in (*args, *outs))
    return pl.pallas_call(
        kernel,
        grid=(steps,),
        out_shape=outs,
        in_specs=in_specs,
        out_specs=out_specs,
        scratch_shapes=scratch,
        compiler_params=pltpu.CompilerParams(vmem_limit_bytes=VMEM_LIMIT),
        cost_estimate=pl.CostEstimate(flops=flops, bytes_accessed=moved, transcendentals=0),
    )(*args)


SCALARS = pl.BlockSpec(memory_space=pltpu.SMEM)


def in_spec(w_in):
    return pl.BlockSpec((1,) + w_in.shape[1:], lambda e: (e, 0, 0, 0))


def out_spec(w_out):
    return pl.BlockSpec((1,) + w_out.shape[1:], lambda e: (e, 0, 0))


def spread_spec(seq):
    return pl.BlockSpec((1, seq, 128), lambda e: (e, 0, 0))


def block_shapes(experts, capacity):
    return [shaped((experts, SLOTS, D), LOWTYPE)] * (capacity // SLOTS)


def block_specs(capacity):
    return [pl.BlockSpec((1, SLOTS, D), lambda e: (e, 0, 0))] * (capacity // SLOTS)


def moe_up(loads, c16, router, table, place, w_in, capacity):
    seq, experts = table.shape
    hidden = w_in.shape[1] * w_in.shape[3]
    per = lambda width: pl.BlockSpec((capacity, width), lambda e: (e, 0))
    return gridded(
        moe_up_kernel,
        experts,
        [SCALARS, whole((seq, D)), whole((D, experts)), whole((seq, experts))]
        + [pl.BlockSpec((1, 1, seq), lambda e: (e, 0, 0)), in_spec(w_in)],
        [
            shaped((seq, experts), FULLTYPE),
            shaped((experts, seq, 128), FULLTYPE),
            shaped((experts, seq, 128), FULLTYPE),
            shaped((experts * capacity, hidden), LOWTYPE),
            shaped((experts * capacity, hidden), FULLTYPE),
        ]
        + block_shapes(experts, capacity),
        [whole((seq, experts)), spread_spec(seq), spread_spec(seq), per(hidden), per(hidden)]
        + block_specs(capacity),
        [loads, c16, router, table, place, w_in],
        2 * experts * capacity * D * (hidden + seq),
    )


def moe_down(loads, mid, spread_place, spread_gate, act, w_out):
    seq, experts = (mid.shape[0], w_out.shape[0])
    capacity, hidden = (act.shape[0] // experts, act.shape[1])
    per = lambda width: pl.BlockSpec((capacity, width), lambda e: (e, 0))
    return gridded(
        moe_down_kernel,
        experts,
        [SCALARS, whole((seq, D)), spread_spec(seq), spread_spec(seq), per(hidden), out_spec(w_out)],
        [shaped((seq, D), FULLTYPE), shaped((experts * capacity, D), LOWTYPE)],
        [whole((seq, D)), per(D)],
        [loads, mid, spread_place, spread_gate, act, w_out],
        2 * experts * capacity * D * (hidden + seq),
    )


def moe_gate_backward(loads, grad, c16, router, gates, place, spread_place, spread_gate, y16):
    seq, experts = gates.shape
    capacity = y16.shape[0] // experts
    per = pl.BlockSpec((capacity, D), lambda e: (e, 0))
    return gridded(
        moe_gate_kernel,
        experts,
        [SCALARS, whole((seq, D)), whole((seq, D)), whole((D, experts)), whole((seq, experts))]
        + [pl.BlockSpec((1, 1, seq), lambda e: (e, 0, 0)), spread_spec(seq), spread_spec(seq), per],
        [
            shaped((D, experts), FULLTYPE),
            shaped((seq, D), FULLTYPE),
        ]
        + block_shapes(experts, capacity),
        [whole((D, experts)), whole((seq, D))] + block_specs(capacity),
        [loads, grad, c16, router, gates, place, spread_place, spread_gate, y16],
        4 * experts * capacity * D * seq,
        [
            pltpu.VMEM((seq, D), LOWTYPE),
            pltpu.VMEM((seq, experts), LOWTYPE),
            pltpu.VMEM((seq, experts), FULLTYPE),
        ],
    )


def moe_backward(loads, start, spread_place, w_in, w_out, dy, slope):
    seq, experts = (start.shape[0], w_out.shape[0])
    capacity, hidden = (slope.shape[0] // experts, w_out.shape[1])
    per = lambda width: pl.BlockSpec((capacity, width), lambda e: (e, 0))
    return gridded(
        moe_backward_kernel,
        experts,
        [SCALARS, whole((seq, D)), spread_spec(seq), in_spec(w_in), out_spec(w_out)]
        + [per(hidden)]
        + block_specs(capacity),
        [shaped((seq, D), FULLTYPE)],
        [whole((seq, D))],
        [loads, start, spread_place, w_in, w_out, slope, *dy],
        2 * experts * capacity * D * (2 * hidden + seq),
        [pltpu.VMEM((capacity, D), LOWTYPE)],
    )[0]


def moe_weight_backward(rows, dy, w_in, w_out):
    count, width = (rows[0].shape[0], w_in.shape[1])
    step = 512
    per = pl.BlockSpec((step, D), lambda i: (i, 0))
    return gridded(
        functools.partial(moe_weight_kernel, len(rows)),
        count // step,
        [per] * (2 * len(rows)) + [whole((D, width)), whole((width, D))],
        [shaped((D, width), FULLTYPE), shaped((width, D), FULLTYPE)],
        [whole((D, width)), whole((width, D))],
        [*rows, *dy, w_in, w_out],
        10 * count * len(rows) * D * width,
    )


def flat_plan(experts):
    shapes = [(PIX, D)] + [(D, 3 * D)] * 3 + [(D, D)] * 3 + [(D, FF)] * 2 + [(FF, D)] * 2
    plan, start = [], 0
    for height, width in shapes:
        plan.append((start, height, width // 128))
        start += height * width // 128
    return (plan, start)


def owner_rows(shard, parts):
    return -(-((shard + 127 + 127) // 128) // (16 * parts)) * 16 * parts


def chunk_of(rows, most=128):
    return max(c for c in range(16, most + 1, 16) if rows % c == 0)


def unpack_kernel(plan, shard, owners, orders, place_ref, *refs):
    chains = len(orders)
    own, other = (refs[:chains], refs[chains : 2 * chains])
    refs = refs[2 * chains :]
    outs, rest, flat = (refs[: len(plan)], refs[len(plan)], refs[len(plan) + 1])
    sizes = [ref.shape[0] // owners for ref in own]
    mine, core = (place_ref[0], place_ref[1])

    def collect(owner, carry):
        first = shard * owner // 128
        last = flat[pl.ds(jnp.maximum(first, 0), 1), :]
        shared = jnp.where(lax.rem(shard * owner, 128) == 0, 0.0, 1.0)
        for half in (0, 1):
            for chain, order in enumerate(orders):
                away = jnp.bitwise_xor(mine, owner)
                slot = sum(
                    jnp.bitwise_and(away // bit, 1) * 2**k for k, bit in enumerate(order)
                )
                size, before = (sizes[chain], half * sum(sizes) + sum(sizes[:chain]))
                source = pl.ds(pl.multiple_of(slot * size, 16), size)
                target = pl.ds(first + before, size)
                for ref, wanted in ((own[chain], core == half), (other[chain], core != half)):

                    @pl.when(wanted)
                    def _(ref=ref, source=source, target=target):
                        flat[target, :] = ref[source, :].astype(FULLTYPE)

        flat[pl.ds(first, 1), :] += last * shared
        return carry

    flat[0:8, :] = jnp.zeros((8, 128), FULLTYPE)
    lax.fori_loop(0, owners, collect, 0)
    spread_flat(plan, flat, outs, rest)


def unpack_parts_kernel(plan, shard, parts_ref, *refs):
    outs, rest, flat = (refs[: len(plan)], refs[len(plan)], refs[len(plan) + 1])
    owners, rows = parts_ref.shape[:2]
    chunk = chunk_of(rows)
    for owner in range(owners):
        first = shard * owner // 128
        if owner:
            last = flat[pl.ds(first, 1), :]

        def copy(i, carry, owner=owner, first=first):
            flat[pl.ds(first + i * chunk, chunk), :] = parts_ref[
                owner, pl.ds(pl.multiple_of(i * chunk, chunk), chunk), :
            ].astype(FULLTYPE)
            return carry

        lax.fori_loop(0, rows // chunk, copy, 0)
        if owner and shard * owner % 128:
            flat[pl.ds(first, 1), :] += last
    spread_flat(plan, flat, outs, rest)


def spread_flat(plan, flat, outs, rest):
    for (start, height, across), out in zip(plan, outs):

        def place(i, carry, start=start, across=across, out=out):
            for c in range(across):
                taken = flat[pl.ds(start + i * 128 * across + c, 128, stride=across), :]
                out[rows_of(i, 128), pl.ds(c * 128, 128)] = taken.astype(LOWTYPE)
            return carry

        lax.fori_loop(0, height // 128, place, 0)
    start = plan[-1][0] + plan[-1][1] * plan[-1][2]
    rest[...] = flat[pl.ds(start, rest.shape[0]), :]


ORDERS = ((1, 2, 4, 8), (2, 4, 8, 1), (4, 8, 1, 2))


def chain_sizes(rows):
    units = rows // 16
    first = max(1, units * 2 // 9)
    second = (units - first) // 2
    return [16 * first, 16 * second, 16 * (units - first - second)]


def gather_weights(part, shard, ep_place, dp_place, experts, beside):
    plan, start = flat_plan(experts)
    owners, groups = (lax.axis_size("ep"), lax.axis_size("dp"))
    rows = owner_rows(shard, groups)
    outs = [shaped((height, across * 128), LOWTYPE) for _, height, across in plan]
    outs.append(shaped((shard * owners // 128 - start, 128), FULLTYPE))
    flat = pltpu.VMEM((-(-(shard * (owners - 1) // 128 + rows) // 8) * 8, 128), FULLTYPE)
    if (owners, groups) != (16, 2) or part.shape[0] < 48:
        parts = lax.all_gather(part, ("ep", "dp")).reshape(owners, rows, 128)
        kernel, args = (functools.partial(unpack_parts_kernel, plan, shard), [parts])
        return (local_call(kernel, outs, args, 0, [flat]), beside[0](*beside[1]))
    sizes = chain_sizes(part.shape[0])
    chains = [part[sum(sizes[:c]) : sum(sizes[: c + 1])] for c in range(len(ORDERS))]
    work, inputs = beside
    for step in range(len(ORDERS[0])):
        got = [
            lax.ppermute(v, "ep", [(i, i ^ order[step]) for i in range(owners)])
            for v, order in zip(chains, ORDERS)
        ]
        if step == len(ORDERS[0]) - 2:
            got, inputs = lax.optimization_barrier((got, inputs))
        elif step == len(ORDERS[0]) - 1:
            got, results = lax.optimization_barrier((got, work(*inputs)))
        else:
            got = lax.optimization_barrier(got)
        chains = [jnp.concatenate([v, g]) for v, g in zip(chains, got)]
    args = [jnp.stack([ep_place, dp_place]).astype(jnp.int32), *chains, *map(swap_dp, chains)]
    moved = sum(math.prod(a.shape) * a.dtype.itemsize for a in (*args, *outs))
    mats = pl.pallas_call(
        functools.partial(unpack_kernel, plan, shard, owners, ORDERS),
        out_shape=outs,
        in_specs=[SCALARS] + in_vmem(len(args) - 1),
        out_specs=in_vmem(len(outs)),
        scratch_shapes=[flat],
        compiler_params=pltpu.CompilerParams(vmem_limit_bytes=VMEM_LIMIT),
        cost_estimate=pl.CostEstimate(flops=0, bytes_accessed=moved, transcendentals=0),
    )(*args)
    return (mats, results)


def pack_kernel(plan, shard, select, place_ref, *refs):
    count = len(plan)
    mats, rest, norms = (refs[:count], refs[count], refs[count + 1 : count + 5])
    outs, flat = (refs[count + 5 : -1], refs[-1])
    for (start, height, across), mat in zip(plan, mats):

        def place(i, carry, start=start, across=across, mat=mat):
            for c in range(across):
                flat[pl.ds(start + i * 128 * across + c, 128, stride=across), :] = mat[
                    rows_of(i, 128), pl.ds(c * 128, 128)
                ]
            return carry

        lax.fori_loop(0, height // 128, place, 0)
    start = plan[-1][0] + plan[-1][1] * plan[-1][2]
    flat[pl.ds(start, rest.shape[0]), :] = rest[...]
    start += rest.shape[0]
    for kind in (0, 1):
        for layer, norm in enumerate(norms):
            for k in range(2 if layer < 3 else 1):
                for c in range(D // 128):
                    row = start + ((7 * kind + 2 * layer + k) * D) // 128 + c
                    flat[row : row + 1, :] = norm[2 * k + kind : 2 * k + kind + 1, c * 128 : c * 128 + 128]
    for out, which in zip(outs, select):
        groups, owners, rows = out.shape[:3]
        chunk = chunk_of(rows)
        for group in range(groups):
            for owner in range(owners):
                member = which(place_ref[0], group)
                first = shard * owner // 128 + member * rows

                def copy(i, carry, out=out, group=group, owner=owner, first=first):
                    out[group, owner, pl.ds(pl.multiple_of(i * chunk, chunk), chunk), :] = flat[
                        pl.ds(first + i * chunk, chunk), :
                    ].astype(out.dtype)
                    return carry

                lax.fori_loop(0, rows // chunk, copy, 0)


def pack_gradients(mats, rest, norms, shard, owners, groups, place, experts):
    plan, _ = flat_plan(experts)
    rows = owner_rows(shard, groups)
    part = rows // groups
    if groups == 2:
        outs = [shaped((1, owners, part, 128), t) for t in (FULLTYPE, EXCHANGE)]
        select = [lambda here, g: here, lambda here, g: 1 - here]
    else:
        outs = [shaped((groups, owners, part, 128), FULLTYPE)]
        select = [lambda here, g: g]
    flat = pltpu.VMEM((-(-(shard * (owners - 1) // 128 + rows) // 8) * 8, 128), FULLTYPE)
    args = [place.reshape(1), *mats, rest, *norms]
    moved = sum(math.prod(a.shape) * a.dtype.itemsize for a in (*args, *outs))
    return pl.pallas_call(
        functools.partial(pack_kernel, plan, shard, select),
        out_shape=outs,
        in_specs=[SCALARS] + in_vmem(len(args) - 1),
        out_specs=in_vmem(len(outs)),
        scratch_shapes=[flat],
        compiler_params=pltpu.CompilerParams(vmem_limit_bytes=PACK_LIMIT),
        cost_estimate=pl.CostEstimate(flops=0, bytes_accessed=moved, transcendentals=0),
    )(*args)


EXCHANGE = jnp.bfloat16
PACK_LIMIT = 60 * 2**20


def swap_dp(value):
    return lax.ppermute(value, "dp", [(0, 1), (1, 0)])


def join_dp(value, place):
    groups = lax.axis_size("dp")
    if groups != 2:
        return lax.all_gather(value, "dp")
    other = swap_dp(value)
    first = place == 0
    return jnp.stack([jnp.where(first, value, other), jnp.where(first, other, value)])


def sum_scatter_dp(parts, place):
    groups = lax.axis_size("dp")
    if groups != 2:
        return lax.psum_scatter(parts, "dp", scatter_dimension=0, tiled=True)[0]
    first = place == 0
    mine = jnp.where(first, parts[0], parts[1])
    return mine + swap_dp(jnp.where(first, parts[1], parts[0]))


def sum_all(value):
    for axis in ("dp", "ep"):
        count = lax.axis_size(axis)
        step = 1
        while step < count:
            value = value + lax.ppermute(value, axis, [(i, i ^ step) for i in range(count)])
            step *= 2
    return value


def to_experts(buffer):
    return lax.all_to_all(buffer, "ep", split_axis=0, concat_axis=0, tiled=True)


def per_device(
    patches,
    labels,
    pixel_mask,
    patch_valid,
    tasks,
    routes,
    dense_weight,
    dense_first,
    dense_second,
    dense_average,
    expert_in,
    in_first,
    in_second,
    in_average,
    expert_out,
    out_first,
    out_second,
    out_average,
):
    ep_count = lax.axis_size("ep")
    experts = min(16, ep_count)
    copies = ep_count // experts
    groups = lax.axis_size("dp")
    ep_place = lax.axis_index("ep")
    dp_place = lax.axis_index("dp")
    own_expert = ep_place // copies
    seq = patches.shape[0]
    capacity = 3 * seq * TOP // (2 * experts)
    shard = dense_weight.shape[0]
    piece = shard // groups
    edges = segment_edges(experts)
    block_count = len(edges) + 1 + 2 * experts
    span, firsts = owner_blocks(edges, shard, ep_count)
    first_block = firsts[ep_place]
    starts = [
        jnp.take(jnp.array([0] + edges + [shard * ep_count] * span, jnp.int32), first_block + k)
        - ep_place * shard
        for k in range(span + 1)
    ]

    def placed(value, at, count):
        return jnp.where(jnp.arange(count) == at, value, 0.0)

    def block_sums(dense_vals, in_vals, out_vals):
        part = lax.dynamic_slice_in_dim(dense_vals, dp_place * piece, piece)
        square = part * part
        index = dp_place * piece + jnp.arange(piece, dtype=jnp.int32)
        listed = placed(jnp.sum(in_vals * in_vals), len(edges) + 1 + own_expert, block_count)
        listed += placed(
            jnp.sum(out_vals * out_vals), len(edges) + 1 + experts + own_expert, block_count
        )
        for k in range(span):
            inside = (index >= starts[k]) & (index < starts[k + 1])
            listed += placed(jnp.sum(jnp.where(inside, square, 0.0)), first_block + k, block_count)
        return listed

    rows = owner_rows(shard, groups)
    offset = lax.rem(ep_place * (shard % 128), 128)
    spread = lax.dynamic_update_slice(
        jnp.zeros((rows * 128,), LOWTYPE), dense_weight.astype(LOWTYPE), (offset,)
    )
    own_part = lax.dynamic_index_in_dim(
        spread.reshape(groups, rows // groups, 128), dp_place, 0, keepdims=False
    )
    low_in, low_out = (expert_in[0].astype(LOWTYPE), expert_out[0].astype(LOWTYPE))
    all_in = lax.all_gather(low_in, ("ep", "dp"))
    all_out = lax.all_gather(low_out, ("ep", "dp"))
    width = low_in.shape[1]
    w_out = all_out.reshape(experts, copies * groups * width, D)

    together = lax.optimization_barrier

    def prepare(labels, pixel_mask, patch_valid, routes, weights):
        named = jnp.sum(
            (routes[:, :, None] == jnp.arange(experts, dtype=jnp.int32)[None, None, :]).astype(FULLTYPE),
            1,
        )
        earlier = jnp.arange(seq)[:, None] > jnp.arange(seq)[None, :]
        table = jnp.where(named > 0, plain(earlier.astype(LOWTYPE), named.astype(LOWTYPE)), -1.0)
        weight_pix = (pixel_mask * patch_valid[:, None]).astype(FULLTYPE)
        class_hot = labels[:, :, None] == jnp.arange(C, dtype=jnp.int32)[None, None, :]
        return (
            table,
            table.T.reshape(experts, 1, seq),
            jnp.sum(named, 0).astype(jnp.int32),
            jnp.where(patch_valid > 0, 0.0, NEG).astype(FULLTYPE).reshape(seq, 1),
            jnp.sum(weight_pix, 1),
            jnp.sum(jnp.where(class_hot, weight_pix[:, :, None], 0.0), 1),
            block_sums(*weights),
        )

    (*mats, rest), prepared = gather_weights(
        own_part,
        shard,
        ep_place,
        dp_place,
        experts,
        (
            prepare,
            (labels, pixel_mask, patch_valid, routes, (dense_weight, expert_in, expert_out)),
        ),
    )
    table, place, loads, down, count_tok, counts, weight_sums = prepared
    steps = [(axis, 2**k) for axis in ("dp", "ep") for k in range(lax.axis_size(axis).bit_length() - 1)]
    fourth = -(-len(steps) // 4)

    def add_steps(value, turn):
        for axis, step in steps[turn * fourth : (turn + 1) * fourth]:
            count = lax.axis_size(axis)
            value = value + lax.ppermute(value, axis, [(i, i ^ step) for i in range(count)])
        return value

    total = add_steps(jnp.sum(count_tok).reshape(1), 0)
    w_patch, w_qkv, w_attn = (mats[0], mats[1:4], mats[4:7])
    w_up, w_down = (mats[7:9], mats[9:11])
    router_rows, head_rows = (TASKS * D * experts // 128, D * C // 128)
    w_router = rest[:router_rows].reshape(TASKS, D, experts).astype(LOWTYPE)
    w_head = rest[router_rows : router_rows + head_rows].reshape(D, C).astype(LOWTYPE)
    norms = rest[router_rows + head_rows :].reshape(2, 7, D)
    task = tasks[0]
    router = lax.dynamic_index_in_dim(w_router, task, 0, keepdims=False)

    def dispatch(send):
        return to_experts(jnp.repeat(send, copies, axis=0)).reshape(-1, D)

    together = lax.optimization_barrier

    def norm_rows(layer):
        rows = [norms[0, 2 * layer], norms[1, 2 * layer]]
        if layer < 3:
            rows += [norms[0, 2 * layer + 1], norms[1, 2 * layer + 1]]
        return jnp.pad(jnp.stack(rows), ((0, 8 - len(rows)), (0, 0)))

    x0, *kept0, x1, act0, slope0 = layer_forward(
        patches, w_patch, w_qkv[0], w_attn[0], norm_rows(0), down, w_up[0], w_down[0]
    )
    x1, all_in, total = together((x1, all_in, total))
    total = add_steps(total, 1)
    mid1, c16, *kept1 = layer_forward(
        x1, None, w_qkv[1], w_attn[1], norm_rows(1), down, None, None
    )
    c16, total = together((c16, total))
    total = add_steps(total, 2)
    w_in = all_in.reshape(experts, copies * groups, D, width)
    if width % 128:
        w_in = jnp.swapaxes(w_in, 1, 2).reshape(experts, 1, D, copies * groups * width)
    gates, spread_place, spread_gate, act1, slope1, *sent = moe_up(
        loads, c16, router, table, place, w_in, capacity
    )
    x2, y16 = moe_down(loads, mid1, spread_place, spread_gate, act1, w_out)
    x2, sent, total = together((x2, sent, total))
    total = add_steps(total, 3)
    rows_a = dispatch(sent[0])
    *kept2, x3, act2, slope2 = layer_forward(
        x2, None, w_qkv[2], w_attn[2], norm_rows(2), down, w_up[1], w_down[1]
    )
    x3, sent, rows_a = together((x3, sent, rows_a))
    rows_b = dispatch(sent[1])
    loss_lanes, d_head, d_normf, grad = head_call(
        x3, norm_rows(3), w_head, counts, count_tok, total
    )
    local = loss_lanes[0, 0]
    grad, local = together((grad, local))
    d_qkv2, d_attn2, d_norm2, d_up1, d_down1, grad = layer_backward(
        grad, x2, (*kept2, act2, slope2), w_qkv[2], w_attn[2], norm_rows(2), down,
        (w_up[1], w_down[1]), None, None,
    )
    grad, sent, rows_b = together((grad, sent, rows_b))
    rows_c = dispatch(sent[2])
    d_own_router, d_c, *dy16 = moe_gate_backward(
        loads, grad, c16, router, gates, place, spread_place, spread_gate, y16
    )
    d_c, dy16, rows_c = together((d_c, dy16, rows_c))
    dy_a = dispatch(dy16[0])
    d_c = moe_backward(loads, d_c, spread_place, w_in, w_out, dy16, slope1)
    d_c, dy16, dy_a = together((d_c, dy16, dy_a))
    dy_b = dispatch(dy16[1])
    task_hot = (jnp.arange(TASKS, dtype=jnp.int32) == task)[:, None, None]
    d_router = jnp.where(task_hot, d_own_router[None], 0.0)
    d_qkv1, d_attn1, d_norm1, grad = layer_backward(
        grad, x1, (mid1, c16, *kept1), w_qkv[1], w_attn[1], norm_rows(1), down, None, d_c, None
    )
    grad, dy16, dy_b = together((grad, dy16, dy_b))
    dy_c = dispatch(dy16[2])
    d_qkv0, d_attn0, d_norm0, d_up0, d_down0, d_patch = layer_backward(
        grad, x0, (*kept0, act0, slope0), w_qkv[0], w_attn[0], norm_rows(0), down,
        (w_up[0], w_down[0]), None, patches,
    )
    d_patch, dy_c = together((d_patch, dy_c))
    expert_rows, expert_dy = ([rows_a, rows_b, rows_c], [dy_a, dy_b, dy_c])
    d_rest = jnp.concatenate(
        [
            d_router.reshape(router_rows, 128),
            d_head[:, :C].reshape(head_rows, 128),
        ]
    )
    packed = pack_gradients(
        [d_patch, d_qkv0, d_qkv1, d_qkv2, d_attn0, d_attn1, d_attn2, d_up0, d_up1, d_down0, d_down1],
        d_rest, [d_norm0, d_norm1, d_norm2, d_normf], shard, ep_count, groups, dp_place, experts,
    )
    if groups == 2:
        summed = packed[0][0] + swap_dp(packed[1][0]).astype(FULLTYPE)
    else:
        summed = lax.psum_scatter(packed[0], "dp", scatter_dimension=0, tiled=True)[0]
    arrived = to_experts(summed.astype(LOWTYPE))

    own_in = lax.dynamic_index_in_dim(
        all_in.reshape(ep_count, groups, D, width), ep_place, 0, keepdims=False
    )
    own_out = lax.dynamic_index_in_dim(
        all_out.reshape(ep_count, groups, width, D), ep_place, 0, keepdims=False
    )
    if groups == 2:

        def weight_grads(member):
            return moe_weight_backward(
                expert_rows,
                expert_dy,
                lax.dynamic_index_in_dim(own_in, member, 0, keepdims=False),
                lax.dynamic_index_in_dim(own_out, member, 0, keepdims=False),
            )

        theirs = weight_grads(1 - dp_place)
        away = [swap_dp(t.astype(jnp.bfloat16)) for t in theirs]
        mine = weight_grads(dp_place)
        mine, away, arrived = together((mine, away, arrived))
        d_in, d_out = [(m + t.astype(FULLTYPE))[None] for m, t in zip(mine, away)]
    else:
        d_in, d_out = moe_weight_backward(
            expert_rows,
            expert_dy,
            jnp.swapaxes(own_in, 0, 1).reshape(D, groups * width),
            own_out.reshape(groups * width, D),
        )
        d_in, d_out = (
            lax.psum_scatter(
                value[None].astype(jnp.bfloat16), "dp", scatter_dimension=axis, tiled=True
            ).astype(FULLTYPE)
            for value, axis in ((d_in, 2), (d_out, 1))
        )
    own_sum = jnp.sum(arrived.astype(FULLTYPE), 0)
    dense_grad = lax.dynamic_slice_in_dim(
        join_dp(own_sum, dp_place).reshape(-1), offset, shard
    )
    sums = sum_all(
        placed(local, 0, 2 + block_count)
        + placed(jnp.sum(block_sums(dense_grad, d_in, d_out)), 1, 2 + block_count)
        + jnp.pad(weight_sums, (2, 0))
    )
    loss, grad_total, weight_total = (sums[0] / total, sums[1], sums[2:])
    grad_norm = jnp.sqrt(grad_total)
    clip = CLIP_NORM / jnp.maximum(grad_norm, CLIP_NORM)

    def moments(weight, first, second, gradient):
        gradient = gradient * clip
        first_new = DECAY_ONE * first + (1.0 - DECAY_ONE) * gradient
        second_new = DECAY_TWO * second + (1.0 - DECAY_TWO) * gradient * gradient
        return (
            first_new,
            second_new,
            first_new / (jnp.sqrt(second_new) + EPS_ADAM) + WEIGHT_DECAY * weight,
        )

    dense_m, dense_v, dense_step = moments(dense_weight, dense_first, dense_second, dense_grad)
    in_m, in_v, in_step = moments(expert_in, in_first, in_second, d_in)
    out_m, out_v, out_step = moments(expert_out, out_first, out_second, d_out)
    update_total = sum_all(block_sums(dense_step, in_step, out_step))
    weight_norm = jnp.sqrt(weight_total)
    update_norm = jnp.sqrt(update_total)
    ratio = weight_norm / (update_norm + EPS_NORM)
    whole_index = jnp.arange(shard, dtype=jnp.int32)
    dense_ratio = jnp.broadcast_to(jnp.take(ratio, first_block), (shard,))
    for k in range(1, span):
        dense_ratio = jnp.where(whole_index >= starts[k], jnp.take(ratio, jnp.minimum(first_block + k, block_count - 1)), dense_ratio)
    in_ratio = lax.dynamic_index_in_dim(ratio, 14 + own_expert, 0, keepdims=False)
    out_ratio = lax.dynamic_index_in_dim(ratio, 14 + experts + own_expert, 0, keepdims=False)

    def finish(weight, average, step, rate):
        new = weight - RATE * rate * step
        return (new, AVERAGE * average + (1.0 - AVERAGE) * new, new.astype(LOWTYPE))

    dense_new, dense_avg, dense_low = finish(dense_weight, dense_average, dense_step, dense_ratio)
    in_new, in_avg, in_low = finish(expert_in, in_average, in_step, in_ratio)
    out_new, out_avg, out_low = finish(expert_out, out_average, out_step, out_ratio)
    block_norms = jnp.stack([weight_norm, update_norm], 1)
    return (
        loss.reshape(1),
        grad_norm.reshape(1),
        block_norms,
        dense_new,
        dense_m,
        dense_v,
        dense_avg,
        dense_low,
        in_new,
        in_m,
        in_v,
        in_avg,
        in_low,
        out_new,
        out_m,
        out_v,
        out_avg,
        out_low,
    )


def solution(mesh):
    in_specs = (
        P(("ep", "dp"), None),
        P(("ep", "dp"), None),
        P(("ep", "dp"), None),
        P(("ep", "dp")),
        P(("ep", "dp")),
        P(("ep", "dp"), None),
        P("ep"),
        P("ep"),
        P("ep"),
        P("ep"),
        P("ep", None, "dp"),
        P("ep", None, "dp"),
        P("ep", None, "dp"),
        P("ep", None, "dp"),
        P("ep", "dp", None),
        P("ep", "dp", None),
        P("ep", "dp", None),
        P("ep", "dp", None),
    )
    out_specs = (
        P(),
        P(),
        P(),
        P("ep"),
        P("ep"),
        P("ep"),
        P("ep"),
        P("ep"),
        P("ep", None, "dp"),
        P("ep", None, "dp"),
        P("ep", None, "dp"),
        P("ep", None, "dp"),
        P("ep", None, "dp"),
        P("ep", "dp", None),
        P("ep", "dp", None),
        P("ep", "dp", None),
        P("ep", "dp", None),
        P("ep", "dp", None),
    )
    return jax.shard_map(
        per_device, mesh=mesh, in_specs=in_specs, out_specs=out_specs, check_vma=False
    )
```

```python
import functools
import math

import jax
import jax.numpy as jnp
from jax import lax
from jax.experimental import pallas as pl
from jax.experimental.pallas import tpu as pltpu
from jax.sharding import PartitionSpec as P

D = 384
HEADS = 6
HD = 64
FF = 1536
TOP = 4
C = 40
PIX = 768
TASKS = 4


EPS_NORM = 1e-05
CLIP_NORM = 0.002
RATE = 0.3
DECAY_ONE = 0.5
DECAY_TWO = 0.5
WEIGHT_DECAY = 0.01
EPS_ADAM = 1e-09
AVERAGE = 0.9
SCALE = 0.125
LOWTYPE = jnp.bfloat16
FULLTYPE = jnp.float32


def plain(left, right):
    return jnp.dot(left, right, preferred_element_type=FULLTYPE)


def left_t(left, right):
    return lax.dot_general(left, right, (((0,), (0,)), ((), ())), preferred_element_type=FULLTYPE)


def right_t(left, right):
    return lax.dot_general(left, right, (((1,), (1,)), ((), ())), preferred_element_type=FULLTYPE)


def segment_sizes(experts):
    return (
        [PIX * D]
        + [3 * D * D] * 3
        + [D * D] * 3
        + [D * FF] * 2
        + [FF * D] * 2
        + [TASKS * D * experts, D * C, 14 * D]
    )


def owner_blocks(edges, shard, owners):
    firsts = [sum(edge <= shard * i for edge in edges) for i in range(owners)]
    lasts = [sum(edge < shard * (i + 1) for edge in edges) for i in range(owners)]
    span = max(b - a + 1 for a, b in zip(firsts, lasts))
    return (span, jnp.array(firsts, jnp.int32))


def segment_edges(experts):
    edges, edge = [], 0
    for size in segment_sizes(experts)[:-1]:
        edge += size
        edges.append(edge)
    return edges


VMEM_LIMIT = 56 * 2**20
ROWS = 512
TILE = 32
KEYS = 64
QUERIES = 512
NEG = -1e30


def rows_of(index, size=ROWS):
    return pl.ds(pl.multiple_of(index * size, size), size)


def norm_parts(x):
    cent = x - jnp.mean(x, -1, keepdims=True)
    scale = lax.rsqrt(jnp.mean(cent * cent, -1, keepdims=True) + EPS_NORM)
    return (cent * scale, scale)


def norm_low(x, gain, bias):
    return (norm_parts(x)[0] * gain + bias).astype(LOWTYPE)


def norm_pull(x, gain, grad):
    unit, scale = norm_parts(x)
    inner = grad * gain
    d_x = scale * (
        inner
        - jnp.mean(inner, -1, keepdims=True)
        - unit * jnp.mean(inner * unit, -1, keepdims=True)
    )
    return (d_x, jnp.sum(grad * unit, 0, keepdims=True), jnp.sum(grad, 0, keepdims=True))


def gelu_pair(h):
    cdf = 0.5 + 0.5 * lax.erf(h * 0.7071067811865476)
    e = jnp.exp((h * h) * -0.5)
    return (h * cdf, cdf + h * (e * 0.3989422804014327))


def half_masks(scale):
    lane = lax.broadcasted_iota(jnp.int32, (1, 128), 1)
    return [jnp.where((lane < HD) == (h == 0), scale, 0.0).astype(LOWTYPE) for h in (0, 1)]


def beside_head(head, own, extras):
    lane = lax.broadcasted_iota(jnp.int32, own.shape, 1)
    value = own.astype(FULLTYPE) * half_masks(1.0)[head].astype(FULLTYPE)
    for k, extra in enumerate(extras):
        value = jnp.where(lane == HD * (1 - head) + k, extra, value)
    return value.astype(LOWTYPE)


def three_parts(column):
    high = column.astype(LOWTYPE).astype(FULLTYPE)
    middle = (column - high).astype(LOWTYPE).astype(FULLTYPE)
    return [high, middle, column - high - middle]


def attend_rows(qkv_ref, bias_ref, o_ref, aug_ref, keys_ref, s_ref, p_ref):
    seq = qkv_ref.shape[0]
    masks = half_masks(SCALE)
    lane = lax.broadcasted_iota(jnp.int32, (ROWS, 128), 1)

    for pair in range(HEADS // 2):
        cols = pl.ds(pair * 128, 128)

        def prepare(i, carry, pair=pair):
            rows = rows_of(i)
            keys = qkv_ref[rows, pl.ds(D + pair * 128, 128)]
            for h in (0, 1):
                keys_ref[h, rows, :] = beside_head(h, keys, [bias_ref[rows, :]])
            return carry

        lax.fori_loop(0, seq // ROWS, prepare, 0)

        def body(i, carry, pair=pair, cols=cols):
            rows = rows_of(i)
            query = qkv_ref[rows, cols]
            values = qkv_ref[:, pl.ds(2 * D + pair * 128, 128)]
            outs = []
            for h in (0, 1):
                s_ref[h] = right_t(beside_head(h, query * masks[h], [1.0]), keys_ref[h])
            for h in (0, 1):
                for first in range(0, ROWS, TILE):
                    s = s_ref[h, first : first + TILE, :]
                    top = jnp.max(s, -1, keepdims=True)
                    e = jnp.exp(s - top)
                    total = jnp.sum(e, -1, keepdims=True)
                    p_ref[h, first : first + TILE, :] = (e * (1.0 / total)).astype(LOWTYPE)
                    at = pl.ds(pl.multiple_of(i * ROWS + first, TILE), TILE)
                    aug_ref[at, pl.ds((2 * pair + h) * 128, 128)] = beside_head(
                        h,
                        query[first : first + TILE] * masks[h],
                        [1.0] + three_parts(-(top + jnp.log(total))),
                    )
            for h in (0, 1):
                outs.append(plain(p_ref[h], values))
            o_ref[rows, cols] = jnp.where(lane < HD, outs[0], outs[1]).astype(LOWTYPE)
            return carry

        lax.fori_loop(0, seq // ROWS, body, 0)


def forward_kernel(has_patch, has_ff, *refs):
    refs = list(refs)
    x_in = refs.pop(0)
    if has_patch:
        w_patch = refs.pop(0)
    w_qkv, w_attn, norms, bias = refs[:4]
    refs = refs[4:]
    if has_ff:
        w_up, w_down = refs[:2]
        refs = refs[2:]
    if has_patch:
        x_ref = refs.pop(0)
    else:
        x_ref = x_in
    mid_ref, c_ref, qkv_ref, o_ref, aug_ref = refs[:5]
    refs = refs[5:]
    if has_ff:
        next_ref, act_ref, slope_ref = refs[:3]
    keys_ref, s_ref, p_ref = refs[-3:]
    seq = x_ref.shape[0]

    def project(i, carry):
        rows = rows_of(i)
        if has_patch:
            x_ref[rows, :] = plain(x_in[rows, :], w_patch[...])
        a16 = norm_low(x_ref[rows, :], norms[0:1, :], norms[1:2, :])
        qkv_ref[rows, :] = plain(a16, w_qkv[...]).astype(LOWTYPE)
        return carry

    lax.fori_loop(0, seq // ROWS, project, 0)
    attend_rows(qkv_ref, bias, o_ref, aug_ref, keys_ref, s_ref, p_ref)

    def finish(i, carry):
        rows = rows_of(i)
        mid = x_ref[rows, :] + plain(o_ref[rows, :], w_attn[...])
        mid_ref[rows, :] = mid
        c16 = norm_low(mid, norms[2:3, :], norms[3:4, :])
        c_ref[rows, :] = c16
        if has_ff:
            act, slope = gelu_pair(plain(c16, w_up[...]))
            act16 = act.astype(LOWTYPE)
            act_ref[rows, :] = act16
            slope_ref[rows, :] = slope
            next_ref[rows, :] = mid + plain(act16, w_down[...])
        return carry

    lax.fori_loop(0, seq // ROWS, finish, 0)


def in_vmem(count):
    return [pl.BlockSpec(memory_space=pltpu.VMEM)] * count


def local_call(kernel, outs, args, flops, scratch=()):
    moved = sum(math.prod(a.shape) * a.dtype.itemsize for a in (*args, *outs))
    return pl.pallas_call(
        kernel,
        out_shape=outs,
        in_specs=in_vmem(len(args)),
        out_specs=in_vmem(len(outs)),
        scratch_shapes=scratch,
        compiler_params=pltpu.CompilerParams(vmem_limit_bytes=VMEM_LIMIT),
        cost_estimate=pl.CostEstimate(flops=flops, bytes_accessed=moved, transcendentals=0),
    )(*args)


def shaped(shape, dtype):
    return jax.ShapeDtypeStruct(shape, dtype)


def layer_forward(x, w_patch, w_qkv, w_attn, norms, bias, w_up, w_down):
    seq = x.shape[0]
    has_patch, has_ff = (w_patch is not None, w_up is not None)
    args = [x] + [w_patch] * has_patch + [w_qkv, w_attn, norms, bias] + [w_up, w_down] * has_ff
    outs = [shaped((seq, D), FULLTYPE)] * has_patch
    outs += [
        shaped((seq, D), FULLTYPE),
        shaped((seq, D), LOWTYPE),
        shaped((seq, 3 * D), LOWTYPE),
        shaped((seq, D), LOWTYPE),
        shaped((seq, 128 * HEADS), LOWTYPE),
    ]
    if has_ff:
        outs += [
            shaped((seq, D), FULLTYPE),
            shaped((seq, FF), LOWTYPE),
            shaped((seq, FF), FULLTYPE),
        ]
    flops = 2 * seq * D * (4 * D + 4 * seq + 2 * FF * has_ff)
    kernel = functools.partial(forward_kernel, has_patch, has_ff)
    scratch = [
        pltpu.VMEM((2, seq, 128), LOWTYPE),
        pltpu.VMEM((2, ROWS, seq), FULLTYPE),
        pltpu.VMEM((2, ROWS, seq), LOWTYPE),
    ]
    return local_call(kernel, outs, args, flops, scratch)


def attend_pull(qkv_ref, o_ref, do_ref, aug_ref, valid_ref, dqkv_ref, dk_ref, dv_ref, sides):
    seq = qkv_ref.shape[0]
    keys_ref, values_ref, across_ref, s_ref, dp_ref, p_ref, ds_ref = sides
    ones = half_masks(1.0)

    for pair in range(HEADS // 2):
        cols = pl.ds(pair * 128, 128)
        dk_ref[...] = jnp.zeros_like(dk_ref)
        dv_ref[...] = jnp.zeros_like(dv_ref)

        def prepare(i, carry, pair=pair):
            rows = rows_of(i)
            keys = qkv_ref[rows, pl.ds(D + pair * 128, 128)]
            values = qkv_ref[rows, pl.ds(2 * D + pair * 128, 128)]
            across_ref[:, rows] = keys.astype(FULLTYPE).T.astype(LOWTYPE)
            for h in (0, 1):
                keys_ref[h, rows, :] = beside_head(h, keys, [valid_ref[rows, :], 1.0, 1.0, 1.0])
                values_ref[h, rows, :] = beside_head(h, values, [1.0, 1.0, 1.0])
            return carry

        lax.fori_loop(0, seq // ROWS, prepare, 0)

        def body(i, carry, pair=pair, cols=cols):
            rows = rows_of(i, QUERIES)
            d_out = do_ref[rows, cols]
            both = d_out.astype(FULLTYPE) * o_ref[rows, cols].astype(FULLTYPE)
            d_query = []
            for h in (0, 1):
                own_q = aug_ref[rows, pl.ds((2 * pair + h) * 128, 128)]
                s_ref[h] = right_t(keys_ref[h], own_q)
                delta = jnp.sum(both * ones[h].astype(FULLTYPE), -1, keepdims=True)
                own_d = beside_head(h, d_out, three_parts(-delta))
                dp_ref[h] = right_t(values_ref[h], own_d)
            for h in (0, 1):
                for first in range(0, seq, KEYS):
                    at, side = (pl.ds(first, KEYS), pl.ds(h * QUERIES, QUERIES))
                    probs = jnp.exp(s_ref[h, at, :])
                    p_ref[at, side] = probs.astype(LOWTYPE)
                    ds_ref[at, side] = (probs * dp_ref[h, at, :]).astype(LOWTYPE)
            own = [
                aug_ref[rows, pl.ds((2 * pair + h) * 128, 128)] * ones[h] for h in (0, 1)
            ]
            dv_ref[...] += plain(p_ref[...], jnp.concatenate([d_out * ones[h] for h in (0, 1)]))
            dk_ref[...] += plain(ds_ref[...], jnp.concatenate(own))
            for h in (0, 1):
                d_query.append(
                    plain(across_ref[pl.ds(h * HD, HD), :], ds_ref[:, pl.ds(h * QUERIES, QUERIES)])
                )
            turned = jnp.concatenate(d_query).T * SCALE
            dqkv_ref[rows, cols] = turned.astype(LOWTYPE)
            return carry

        lax.fori_loop(0, seq // QUERIES, body, 0)
        dqkv_ref[:, pl.ds(D + pair * 128, 128)] = dk_ref[...].astype(LOWTYPE)
        dqkv_ref[:, pl.ds(2 * D + pair * 128, 128)] = dv_ref[...].astype(LOWTYPE)


def weight_pull(left_ref, right_ref, out_ref, tile=384):
    def body(j, carry):
        cols = rows_of(j, tile)
        out_ref[cols, :] = left_t(left_ref[:, cols], right_ref[...])
        return carry

    lax.fori_loop(0, left_ref.shape[1] // tile, body, 0)


def backward_kernel(has_patch, has_ff, *refs):
    refs = list(refs)
    grad, x_ref, mid_ref, qkv, o_ref, aug, w_qkv, w_attn, norms, valid = refs[:10]
    refs = refs[10:]
    if has_ff:
        c_ref, act, slope, w_up, w_down = refs[:5]
        refs = refs[5:]
    else:
        d_c_ref = refs.pop(0)
    if has_patch:
        patches = refs.pop(0)
    d_qkvw, d_attn, d_norms = refs[:3]
    refs = refs[3:]
    if has_ff:
        d_up, d_down = refs[:2]
        refs = refs[2:]
    if has_patch:
        d_patch = refs.pop(0)
    else:
        dx_ref = refs.pop(0)
    gmid, low, do_ref, dqkv, dk, dv = refs[:6]
    sides, refs = (refs[6:13], refs[13:])
    if has_ff:
        dh_ref = refs.pop(0)
    seq = grad.shape[0]
    blocks_count = seq // ROWS
    d_norms[...] = jnp.zeros_like(d_norms)

    def feed(i, carry):
        rows = rows_of(i)
        g = grad[rows, :]
        if has_ff:
            g16 = g.astype(LOWTYPE)
            low[rows, :] = g16
            dh16 = (right_t(g16, w_down[...]) * slope[rows, :]).astype(LOWTYPE)
            dh_ref[rows, :] = dh16
            d_c = right_t(dh16, w_up[...])
        else:
            d_c = d_c_ref[rows, :]
        d_x, d_gain, d_bias = norm_pull(mid_ref[rows, :], norms[2:3, :], d_c)
        gmid[rows, :] = g + d_x
        d_norms[2:3, :] += d_gain
        d_norms[3:4, :] += d_bias
        return carry

    lax.fori_loop(0, blocks_count, feed, 0)
    if has_ff:
        weight_pull(act, low, d_down)
        weight_pull(c_ref, dh_ref, d_up)

    def out_pull(i, carry):
        rows = rows_of(i)
        g16 = gmid[rows, :].astype(LOWTYPE)
        low[rows, :] = g16
        do_ref[rows, :] = right_t(g16, w_attn[...]).astype(LOWTYPE)
        return carry

    lax.fori_loop(0, blocks_count, out_pull, 0)
    weight_pull(o_ref, low, d_attn)
    attend_pull(qkv, o_ref, do_ref, aug, valid, dqkv, dk, dv, sides)

    def in_pull(i, carry):
        rows = rows_of(i)
        d_a = right_t(dqkv[rows, :], w_qkv[...])
        x = x_ref[rows, :]
        d_x, d_gain, d_bias = norm_pull(x, norms[0:1, :], d_a)
        total = gmid[rows, :] + d_x
        if has_patch:
            gmid[rows, :] = total
        else:
            dx_ref[rows, :] = total
        low[rows, :] = norm_low(x, norms[0:1, :], norms[1:2, :])
        d_norms[0:1, :] += d_gain
        d_norms[1:2, :] += d_bias
        return carry

    lax.fori_loop(0, blocks_count, in_pull, 0)
    weight_pull(low, dqkv, d_qkvw)
    if has_patch:

        def lower(i, carry):
            rows = rows_of(i)
            low[rows, :] = gmid[rows, :].astype(LOWTYPE)
            return carry

        lax.fori_loop(0, blocks_count, lower, 0)
        weight_pull(patches, low, d_patch)


def layer_backward(grad, x, kept, w_qkv, w_attn, norms, valid, ff, d_c, patches):
    seq = grad.shape[0]
    mid, c16, qkv16, o16, aug = kept[:5]
    has_ff, has_patch = (ff is not None, patches is not None)
    args = [grad, x, mid, qkv16, o16, aug, w_qkv, w_attn, norms, valid]
    args += [c16, *kept[5:], *ff] if has_ff else [d_c]
    args += [patches] * has_patch
    outs = [
        shaped((D, 3 * D), FULLTYPE),
        shaped((D, D), FULLTYPE),
        shaped((8, D), FULLTYPE),
    ]
    if has_ff:
        outs += [shaped((D, FF), FULLTYPE), shaped((FF, D), FULLTYPE)]
    outs += [shaped((PIX, D), FULLTYPE) if has_patch else shaped((seq, D), FULLTYPE)]
    scratch = [
        pltpu.VMEM((seq, D), FULLTYPE),
        pltpu.VMEM((seq, D), LOWTYPE),
        pltpu.VMEM((seq, D), LOWTYPE),
        pltpu.VMEM((seq, 3 * D), LOWTYPE),
        pltpu.VMEM((seq, 128), FULLTYPE),
        pltpu.VMEM((seq, 128), FULLTYPE),
        pltpu.VMEM((2, seq, 128), LOWTYPE),
        pltpu.VMEM((2, seq, 128), LOWTYPE),
        pltpu.VMEM((128, seq), LOWTYPE),
        pltpu.VMEM((2, seq, QUERIES), FULLTYPE),
        pltpu.VMEM((2, seq, QUERIES), FULLTYPE),
        pltpu.VMEM((seq, 2 * QUERIES), LOWTYPE),
        pltpu.VMEM((seq, 2 * QUERIES), LOWTYPE),
    ] + [pltpu.VMEM((seq, FF), LOWTYPE)] * has_ff
    flops = 2 * seq * D * (8 * D + 10 * seq + 4 * FF * has_ff + PIX * has_patch)
    return local_call(
        functools.partial(backward_kernel, has_patch, has_ff), outs, args, flops, scratch
    )


def head_kernel(x_ref, norms, w_head, counts, count, total, loss, d_head, d_norms, grad, f_ref, dl_ref):
    seq = x_ref.shape[0]
    d_norms[...] = jnp.zeros_like(d_norms)
    loss[...] = jnp.zeros_like(loss)
    real = lax.broadcasted_iota(jnp.int32, (1, 128), 1) < C

    def body(i, carry):
        rows = rows_of(i)
        x = x_ref[rows, :]
        f16 = norm_low(x, norms[0:1, :], norms[1:2, :])
        f_ref[rows, :] = f16
        logits = plain(f16, w_head[...])
        shown = jnp.where(real, logits, NEG)
        top = jnp.max(shown, -1, keepdims=True)
        e = jnp.exp(shown - top)
        under = jnp.sum(e, -1, keepdims=True)
        weight = count[rows, :]
        classes = counts[rows, :]
        part = weight * (top + jnp.log(under)) - jnp.sum(classes * logits, -1, keepdims=True)
        loss[...] += jnp.broadcast_to(jnp.sum(part, 0, keepdims=True), loss.shape)
        d_logits = ((weight * (e * (1.0 / under)) - classes) / total[...]).astype(LOWTYPE)
        dl_ref[rows, :] = d_logits
        d_x, d_gain, d_bias = norm_pull(x, norms[0:1, :], right_t(d_logits, w_head[...]))
        grad[rows, :] = d_x
        d_norms[0:1, :] += d_gain
        d_norms[1:2, :] += d_bias
        return carry

    lax.fori_loop(0, seq // ROWS, body, 0)
    weight_pull(f_ref, dl_ref, d_head)


def head_call(x, norms, w_head, counts, count, total):
    seq = x.shape[0]
    outs = [
        shaped((1, 128), FULLTYPE),
        shaped((D, 128), FULLTYPE),
        shaped((8, D), FULLTYPE),
        shaped((seq, D), FULLTYPE),
    ]
    args = [
        x,
        norms,
        jnp.pad(w_head, ((0, 0), (0, 128 - C))),
        jnp.pad(counts, ((0, 0), (0, 128 - C))),
        count.reshape(seq, 1),
        total.reshape(1, 1),
    ]
    scratch = [pltpu.VMEM((seq, D), LOWTYPE), pltpu.VMEM((seq, 128), LOWTYPE)]
    return local_call(head_kernel, outs, args, 6 * seq * D * 128, scratch)


SLOTS = 128


def by_load(load, capacity, work):
    for count in range(SLOTS, capacity + 1, SLOTS):
        inside = load > count - SLOTS if count > SLOTS else load >= 0
        if count < capacity:
            inside = inside & (load <= count)
        pl.when(inside)(functools.partial(work, count))


def slot_select(place, count):
    row = lax.broadcasted_iota(jnp.int32, (count, place.shape[1]), 0).astype(FULLTYPE)
    return jnp.where(place == row, 1.0, 0.0).astype(LOWTYPE)


def put_blocks(refs, rows):
    for block, ref in enumerate(refs):
        if block * SLOTS < rows.shape[0]:
            ref[0] = rows[block * SLOTS : (block + 1) * SLOTS]
        else:
            ref[0] = jnp.zeros(ref.shape[1:], ref.dtype)


def column_of(table, expert):
    lane = lax.broadcasted_iota(jnp.int32, table.shape, 1)
    return jnp.sum(jnp.where(lane == expert, table, 0.0), -1, keepdims=True)


def patch_select(spread, count):
    lane = lax.broadcasted_iota(jnp.int32, (1, 128), 1).astype(FULLTYPE)
    return jnp.concatenate(
        [
            jnp.where(spread == lane + first, 1.0, 0.0).astype(LOWTYPE)
            for first in range(0, count, 128)
        ],
        1,
    )


def moe_up_kernel(
    loads, c_ref, router, table, place, w_in,
    gates_ref, spread_place, spread_gate, act_ref, slope_ref, *rows_refs,
):
    expert = pl.program_id(0)
    seq, capacity, parts = (c_ref.shape[0], act_ref.shape[0], w_in.shape[1])
    width = w_in.shape[3]

    @pl.when(expert == 0)
    def _():
        def start(i, carry):
            rows = rows_of(i)
            z = plain(c_ref[rows, :], router[...])
            named = table[rows, :] >= 0
            shown = jnp.where(named, z, NEG)
            e = jnp.where(named, jnp.exp(shown - jnp.max(shown, -1, keepdims=True)), 0.0)
            gates_ref[rows, :] = e / jnp.sum(e, -1, keepdims=True)
            return carry

        lax.fori_loop(0, seq // ROWS, start, 0)

    def fan(i, carry):
        rows = rows_of(i)
        for source, out in ((table, spread_place), (gates_ref, spread_gate)):
            out[0, rows, :] = jnp.broadcast_to(column_of(source[rows, :], expert), (ROWS, 128))
        return carry

    lax.fori_loop(0, seq // ROWS, fan, 0)

    def work(count):
        at = pl.ds(0, count)
        rows = plain(slot_select(place[0], count), c_ref[...]).astype(LOWTYPE)
        put_blocks(rows_refs, rows)
        for part in range(parts):
            step = width // 3 if width % 384 == 0 else width
            for first in range(0, width, step):
                act, slope = gelu_pair(plain(rows, w_in[0, part, :, pl.ds(first, step)]))
                units = pl.ds(part * width + first, step)
                slope_ref[at, units] = slope
                act_ref[at, units] = act.astype(LOWTYPE)

    by_load(loads[expert], capacity, work)


def moe_down_kernel(loads, mid_ref, spread_place, spread_gate, act_ref, w_out, next_ref, taken_ref, y_ref):
    expert = pl.program_id(0)
    seq, capacity = (mid_ref.shape[0], act_ref.shape[0])

    @pl.when(expert == 0)
    def _():
        next_ref[...] = mid_ref[...]

    def work(count):
        at = pl.ds(0, count)
        y_ref[at, :] = plain(act_ref[at, :], w_out[0]).astype(LOWTYPE)

        def add(i, carry):
            rows = rows_of(i)
            taken = plain(patch_select(spread_place[0, rows, :], count), y_ref[at, :])
            taken_ref[0, rows, :] = taken.astype(LOWTYPE)
            for first in range(0, D, 128):
                lanes = pl.ds(first, 128)
                next_ref[rows, lanes] += spread_gate[0, rows, :] * taken[:, first : first + 128]
            return carry

        lax.fori_loop(0, seq // ROWS, add, 0)

    by_load(loads[expert], capacity, work)


def moe_gate_kernel(
    loads, grad_ref, c_ref, router, gates, place, spread_gate, taken_ref,
    d_router, d_c, *refs,
):
    dy_refs, (low_ref, dz_ref, d_gates) = (refs[:-3], refs[-3:])
    expert = pl.program_id(0)
    seq, capacity = (grad_ref.shape[0], SLOTS * len(dy_refs))
    lane = lax.broadcasted_iota(jnp.int32, (ROWS, d_gates.shape[1]), 1)

    @pl.when(expert == 0)
    def _():
        d_gates[...] = jnp.zeros_like(d_gates)

    def work(count):
        def one(i, carry):
            rows = rows_of(i)
            grad = grad_ref[rows, :]
            gate = spread_gate[0, rows, :]
            taken = taken_ref[0, rows, :].astype(FULLTYPE)
            d_gate = jnp.sum(grad * taken, -1, keepdims=True)
            d_gates[rows, :] += jnp.where(lane == expert, d_gate, 0.0)
            for first in range(0, D, 128):
                lanes = pl.ds(first, 128)
                low_ref[rows, lanes] = (gate * grad[:, first : first + 128]).astype(LOWTYPE)
            return carry

        lax.fori_loop(0, seq // ROWS, one, 0)
        put_blocks(dy_refs, plain(slot_select(place[0], count), low_ref[...]).astype(LOWTYPE))

    by_load(loads[expert], capacity, work)

    @pl.when(expert == pl.num_programs(0) - 1)
    def _():
        def last(i, carry):
            rows = rows_of(i)
            gate = gates[rows, :]
            d_gate = d_gates[rows, :]
            d_z = gate * (d_gate - jnp.sum(gate * d_gate, -1, keepdims=True))
            dz_ref[rows, :] = d_z.astype(LOWTYPE)
            d_c[rows, :] = right_t(dz_ref[rows, :], router[...])
            return carry

        lax.fori_loop(0, seq // ROWS, last, 0)
        d_router[...] = left_t(c_ref[...], dz_ref[...])


def moe_backward_kernel(loads, start_ref, spread_place, w_in, w_out, slope_ref, *refs):
    dy_refs, (d_c, back_ref) = (refs[:-2], refs[-2:])
    expert = pl.program_id(0)
    seq, capacity, parts = (d_c.shape[0], slope_ref.shape[0], w_in.shape[1])
    width = w_in.shape[3]

    @pl.when(expert == 0)
    def _():
        d_c[...] = start_ref[...]

    def work(count):
        at = pl.ds(0, count)
        d_y = jnp.concatenate([ref[0] for ref in dy_refs[: count // SLOTS]])
        back = jnp.zeros((count, D), FULLTYPE)
        for part in range(parts):
            units = pl.ds(part * width, width)
            d_act = right_t(d_y, w_out[0, units, :])
            d_h = (d_act * slope_ref[at, units]).astype(LOWTYPE)
            back += right_t(d_h, w_in[0, part])
        back_ref[at, :] = back.astype(LOWTYPE)

        def add(i, carry):
            rows = rows_of(i)
            d_c[rows, :] += plain(patch_select(spread_place[0, rows, :], count), back_ref[at, :])
            return carry

        lax.fori_loop(0, seq // ROWS, add, 0)

    by_load(loads[expert], capacity, work)


def moe_weight_kernel(count, *refs):
    rows_refs, dy_refs = (refs[:count], refs[count : 2 * count])
    w_in, w_out, d_in, d_out = refs[2 * count :]

    @pl.when(pl.program_id(0) == 0)
    def _():
        d_in[...] = jnp.zeros_like(d_in)
        d_out[...] = jnp.zeros_like(d_out)

    width = w_in.shape[1]
    step = 384 if width % 384 == 0 else width
    for rows_ref, dy_ref in zip(rows_refs, dy_refs):
        rows, d_y = (rows_ref[...], dy_ref[...])
        for first in range(0, width, step):
            units = pl.ds(first, step)
            act, slope = gelu_pair(plain(rows, w_in[:, units]))
            d_h = (right_t(d_y, w_out[units, :]) * slope).astype(LOWTYPE)
            d_out[units, :] += left_t(act.astype(LOWTYPE), d_y)
            d_in[:, units] += left_t(rows, d_h)


def whole(shape):
    return pl.BlockSpec(shape, lambda e: (0,) * len(shape))


def gridded(kernel, steps, in_specs, outs, out_specs, args, flops, scratch=()):
    moved = sum(math.prod(a.shape) * a.dtype.itemsize for a in (*args, *outs))
    return pl.pallas_call(
        kernel,
        grid=(steps,),
        out_shape=outs,
        in_specs=in_specs,
        out_specs=out_specs,
        scratch_shapes=scratch,
        compiler_params=pltpu.CompilerParams(vmem_limit_bytes=VMEM_LIMIT),
        cost_estimate=pl.CostEstimate(flops=flops, bytes_accessed=moved, transcendentals=0),
    )(*args)


SCALARS = pl.BlockSpec(memory_space=pltpu.SMEM)


def in_spec(w_in):
    return pl.BlockSpec((1,) + w_in.shape[1:], lambda e: (e, 0, 0, 0))


def out_spec(w_out):
    return pl.BlockSpec((1,) + w_out.shape[1:], lambda e: (e, 0, 0))


def spread_spec(seq):
    return pl.BlockSpec((1, seq, 128), lambda e: (e, 0, 0))


def taken_spec(seq):
    return pl.BlockSpec((1, seq, D), lambda e: (e, 0, 0))


def block_shapes(experts, capacity):
    return [shaped((experts, SLOTS, D), LOWTYPE)] * (capacity // SLOTS)


def block_specs(capacity):
    return [pl.BlockSpec((1, SLOTS, D), lambda e: (e, 0, 0))] * (capacity // SLOTS)


def moe_up(loads, c16, router, table, place, w_in, capacity):
    seq, experts = table.shape
    hidden = w_in.shape[1] * w_in.shape[3]
    per = lambda width: pl.BlockSpec((capacity, width), lambda e: (e, 0))
    return gridded(
        moe_up_kernel,
        experts,
        [SCALARS, whole((seq, D)), whole((D, experts)), whole((seq, experts))]
        + [pl.BlockSpec((1, 1, seq), lambda e: (e, 0, 0)), in_spec(w_in)],
        [
            shaped((seq, experts), FULLTYPE),
            shaped((experts, seq, 128), FULLTYPE),
            shaped((experts, seq, 128), FULLTYPE),
            shaped((experts * capacity, hidden), LOWTYPE),
            shaped((experts * capacity, hidden), FULLTYPE),
        ]
        + block_shapes(experts, capacity),
        [whole((seq, experts)), spread_spec(seq), spread_spec(seq), per(hidden), per(hidden)]
        + block_specs(capacity),
        [loads, c16, router, table, place, w_in],
        2 * experts * capacity * D * (hidden + seq),
    )


def moe_down(loads, mid, spread_place, spread_gate, act, w_out):
    seq, experts = (mid.shape[0], w_out.shape[0])
    capacity, hidden = (act.shape[0] // experts, act.shape[1])
    per = lambda width: pl.BlockSpec((capacity, width), lambda e: (e, 0))
    return gridded(
        moe_down_kernel,
        experts,
        [SCALARS, whole((seq, D)), spread_spec(seq), spread_spec(seq), per(hidden), out_spec(w_out)],
        [shaped((seq, D), FULLTYPE), shaped((experts, seq, D), LOWTYPE)],
        [whole((seq, D)), taken_spec(seq)],
        [loads, mid, spread_place, spread_gate, act, w_out],
        2 * experts * capacity * D * (hidden + seq),
        [pltpu.VMEM((capacity, D), LOWTYPE)],
    )


def moe_gate_backward(loads, grad, c16, router, gates, place, spread_gate, taken, capacity):
    seq, experts = gates.shape
    return gridded(
        moe_gate_kernel,
        experts,
        [SCALARS, whole((seq, D)), whole((seq, D)), whole((D, experts)), whole((seq, experts))]
        + [pl.BlockSpec((1, 1, seq), lambda e: (e, 0, 0)), spread_spec(seq), taken_spec(seq)],
        [
            shaped((D, experts), FULLTYPE),
            shaped((seq, D), FULLTYPE),
        ]
        + block_shapes(experts, capacity),
        [whole((D, experts)), whole((seq, D))] + block_specs(capacity),
        [loads, grad, c16, router, gates, place, spread_gate, taken],
        4 * experts * capacity * D * seq,
        [
            pltpu.VMEM((seq, D), LOWTYPE),
            pltpu.VMEM((seq, experts), LOWTYPE),
            pltpu.VMEM((seq, experts), FULLTYPE),
        ],
    )


def moe_backward(loads, start, spread_place, w_in, w_out, dy, slope):
    seq, experts = (start.shape[0], w_out.shape[0])
    capacity, hidden = (slope.shape[0] // experts, w_out.shape[1])
    per = lambda width: pl.BlockSpec((capacity, width), lambda e: (e, 0))
    return gridded(
        moe_backward_kernel,
        experts,
        [SCALARS, whole((seq, D)), spread_spec(seq), in_spec(w_in), out_spec(w_out)]
        + [per(hidden)]
        + block_specs(capacity),
        [shaped((seq, D), FULLTYPE)],
        [whole((seq, D))],
        [loads, start, spread_place, w_in, w_out, slope, *dy],
        2 * experts * capacity * D * (2 * hidden + seq),
        [pltpu.VMEM((capacity, D), LOWTYPE)],
    )[0]


def moe_weight_backward(rows, dy, w_in, w_out):
    count, width = (rows[0].shape[0], w_in.shape[1])
    step = 512
    per = pl.BlockSpec((step, D), lambda i: (i, 0))
    return gridded(
        functools.partial(moe_weight_kernel, len(rows)),
        count // step,
        [per] * (2 * len(rows)) + [whole((D, width)), whole((width, D))],
        [shaped((D, width), FULLTYPE), shaped((width, D), FULLTYPE)],
        [whole((D, width)), whole((width, D))],
        [*rows, *dy, w_in, w_out],
        10 * count * len(rows) * D * width,
    )


def flat_plan(experts):
    shapes = [(PIX, D)] + [(D, 3 * D)] * 3 + [(D, D)] * 3 + [(D, FF)] * 2 + [(FF, D)] * 2
    plan, start = [], 0
    for height, width in shapes:
        plan.append((start, height, width // 128))
        start += height * width // 128
    return (plan, start)


def owner_rows(shard, parts):
    return -(-((shard + 127 + 127) // 128) // (16 * parts)) * 16 * parts


def chunk_of(rows, most=128):
    return max(c for c in range(16, most + 1, 16) if rows % c == 0)


def unpack_kernel(plan, shard, owners, orders, place_ref, *refs):
    chains = len(orders)
    own, other = (refs[:chains], refs[chains : 2 * chains])
    refs = refs[2 * chains :]
    outs, rest, flat = (refs[: len(plan)], refs[len(plan)], refs[len(plan) + 1])
    sizes = [ref.shape[0] // owners for ref in own]
    mine, core = (place_ref[0], place_ref[1])

    def collect(owner, carry):
        first = shard * owner // 128
        last = flat[pl.ds(jnp.maximum(first, 0), 1), :]
        shared = jnp.where(lax.rem(shard * owner, 128) == 0, 0.0, 1.0)
        for half in (0, 1):
            for chain, order in enumerate(orders):
                away = jnp.bitwise_xor(mine, owner)
                slot = sum(
                    jnp.bitwise_and(away // bit, 1) * 2**k for k, bit in enumerate(order)
                )
                size, before = (sizes[chain], half * sum(sizes) + sum(sizes[:chain]))
                source = pl.ds(pl.multiple_of(slot * size, 16), size)
                target = pl.ds(first + before, size)
                for ref, wanted in ((own[chain], core == half), (other[chain], core != half)):

                    @pl.when(wanted)
                    def _(ref=ref, source=source, target=target):
                        flat[target, :] = ref[source, :].astype(FULLTYPE)

        flat[pl.ds(first, 1), :] += last * shared
        return carry

    flat[0:8, :] = jnp.zeros((8, 128), FULLTYPE)
    lax.fori_loop(0, owners, collect, 0)
    spread_flat(plan, flat, outs, rest)


def unpack_parts_kernel(plan, shard, parts_ref, *refs):
    outs, rest, flat = (refs[: len(plan)], refs[len(plan)], refs[len(plan) + 1])
    owners, rows = parts_ref.shape[:2]
    chunk = chunk_of(rows)
    for owner in range(owners):
        first = shard * owner // 128
        if owner:
            last = flat[pl.ds(first, 1), :]

        def copy(i, carry, owner=owner, first=first):
            flat[pl.ds(first + i * chunk, chunk), :] = parts_ref[
                owner, pl.ds(pl.multiple_of(i * chunk, chunk), chunk), :
            ].astype(FULLTYPE)
            return carry

        lax.fori_loop(0, rows // chunk, copy, 0)
        if owner and shard * owner % 128:
            flat[pl.ds(first, 1), :] += last
    spread_flat(plan, flat, outs, rest)


def spread_flat(plan, flat, outs, rest):
    for (start, height, across), out in zip(plan, outs):

        def place(i, carry, start=start, across=across, out=out):
            for c in range(across):
                taken = flat[pl.ds(start + i * 128 * across + c, 128, stride=across), :]
                out[rows_of(i, 128), pl.ds(c * 128, 128)] = taken.astype(LOWTYPE)
            return carry

        lax.fori_loop(0, height // 128, place, 0)
    start = plan[-1][0] + plan[-1][1] * plan[-1][2]
    rest[...] = flat[pl.ds(start, rest.shape[0]), :]


ORDERS = ((4, 8, 1, 2), (4, 8, 2, 1))


def chain_sizes(rows):
    units = rows // 16
    return [16 * (units // 2), 16 * (units - units // 2)]


def gather_weights(part, shard, ep_place, dp_place, experts, beside):
    plan, start = flat_plan(experts)
    owners, groups = (lax.axis_size("ep"), lax.axis_size("dp"))
    rows = owner_rows(shard, groups)
    outs = [shaped((height, across * 128), LOWTYPE) for _, height, across in plan]
    outs.append(shaped((shard * owners // 128 - start, 128), FULLTYPE))
    flat = pltpu.VMEM((-(-(shard * (owners - 1) // 128 + rows) // 8) * 8, 128), FULLTYPE)
    if (owners, groups) != (16, 2) or part.shape[0] < 32:
        parts = lax.all_gather(part, ("ep", "dp")).reshape(owners, rows, 128)
        kernel, args = (functools.partial(unpack_parts_kernel, plan, shard), [parts])
        return (local_call(kernel, outs, args, 0, [flat]), beside[0](*beside[1]))
    sizes = chain_sizes(part.shape[0])
    chains = [part[sum(sizes[:c]) : sum(sizes[: c + 1])] for c in range(len(ORDERS))]
    work, inputs = beside
    for step in range(len(ORDERS[0])):
        got = [
            lax.ppermute(v, "ep", [(i, i ^ order[step]) for i in range(owners)])
            for v, order in zip(chains, ORDERS)
        ]
        if step == len(ORDERS[0]) - 2:
            got, inputs = lax.optimization_barrier((got, inputs))
        elif step == len(ORDERS[0]) - 1:
            got, results = lax.optimization_barrier((got, work(*inputs)))
        else:
            got = lax.optimization_barrier(got)
        chains = [jnp.concatenate([v, g]) for v, g in zip(chains, got)]
    args = [jnp.stack([ep_place, dp_place]).astype(jnp.int32), *chains, *map(swap_dp, chains)]
    moved = sum(math.prod(a.shape) * a.dtype.itemsize for a in (*args, *outs))
    mats = pl.pallas_call(
        functools.partial(unpack_kernel, plan, shard, owners, ORDERS),
        out_shape=outs,
        in_specs=[SCALARS] + in_vmem(len(args) - 1),
        out_specs=in_vmem(len(outs)),
        scratch_shapes=[flat],
        compiler_params=pltpu.CompilerParams(vmem_limit_bytes=VMEM_LIMIT),
        cost_estimate=pl.CostEstimate(flops=0, bytes_accessed=moved, transcendentals=0),
    )(*args)
    return (mats, results)


def pack_kernel(plan, shard, select, place_ref, *refs):
    count = len(plan)
    mats, rest, norms = (refs[:count], refs[count], refs[count + 1 : count + 5])
    outs, flat = (refs[count + 5 : -1], refs[-1])
    for (start, height, across), mat in zip(plan, mats):

        def place(i, carry, start=start, across=across, mat=mat):
            for c in range(across):
                flat[pl.ds(start + i * 128 * across + c, 128, stride=across), :] = mat[
                    rows_of(i, 128), pl.ds(c * 128, 128)
                ]
            return carry

        lax.fori_loop(0, height // 128, place, 0)
    start = plan[-1][0] + plan[-1][1] * plan[-1][2]
    flat[pl.ds(start, rest.shape[0]), :] = rest[...]
    start += rest.shape[0]
    for kind in (0, 1):
        for layer, norm in enumerate(norms):
            for k in range(2 if layer < 3 else 1):
                for c in range(D // 128):
                    row = start + ((7 * kind + 2 * layer + k) * D) // 128 + c
                    flat[row : row + 1, :] = norm[2 * k + kind : 2 * k + kind + 1, c * 128 : c * 128 + 128]
    for out, which in zip(outs, select):
        groups, owners, rows = out.shape[:3]
        chunk = chunk_of(rows)
        for group in range(groups):
            for owner in range(owners):
                member = which(place_ref[0], group)
                first = shard * owner // 128 + member * rows

                def copy(i, carry, out=out, group=group, owner=owner, first=first):
                    out[group, owner, pl.ds(pl.multiple_of(i * chunk, chunk), chunk), :] = flat[
                        pl.ds(first + i * chunk, chunk), :
                    ].astype(out.dtype)
                    return carry

                lax.fori_loop(0, rows // chunk, copy, 0)


def pack_gradients(mats, rest, norms, shard, owners, groups, place, experts):
    plan, _ = flat_plan(experts)
    rows = owner_rows(shard, groups)
    part = rows // groups
    if groups == 2:
        outs = [shaped((1, owners, part, 128), t) for t in (FULLTYPE, EXCHANGE)]
        select = [lambda here, g: here, lambda here, g: 1 - here]
    else:
        outs = [shaped((groups, owners, part, 128), FULLTYPE)]
        select = [lambda here, g: g]
    flat = pltpu.VMEM((-(-(shard * (owners - 1) // 128 + rows) // 8) * 8, 128), FULLTYPE)
    args = [place.reshape(1), *mats, rest, *norms]
    moved = sum(math.prod(a.shape) * a.dtype.itemsize for a in (*args, *outs))
    return pl.pallas_call(
        functools.partial(pack_kernel, plan, shard, select),
        out_shape=outs,
        in_specs=[SCALARS] + in_vmem(len(args) - 1),
        out_specs=in_vmem(len(outs)),
        scratch_shapes=[flat],
        compiler_params=pltpu.CompilerParams(vmem_limit_bytes=PACK_LIMIT),
        cost_estimate=pl.CostEstimate(flops=0, bytes_accessed=moved, transcendentals=0),
    )(*args)


EXCHANGE = jnp.bfloat16
PACK_LIMIT = 60 * 2**20


def swap_dp(value):
    return lax.ppermute(value, "dp", [(0, 1), (1, 0)])


def join_dp(value, place):
    groups = lax.axis_size("dp")
    if groups != 2:
        return lax.all_gather(value, "dp")
    other = swap_dp(value)
    first = place == 0
    return jnp.stack([jnp.where(first, value, other), jnp.where(first, other, value)])


def sum_scatter_dp(parts, place):
    groups = lax.axis_size("dp")
    if groups != 2:
        return lax.psum_scatter(parts, "dp", scatter_dimension=0, tiled=True)[0]
    first = place == 0
    mine = jnp.where(first, parts[0], parts[1])
    return mine + swap_dp(jnp.where(first, parts[1], parts[0]))


def sum_all(value):
    for axis in ("dp", "ep"):
        count = lax.axis_size(axis)
        step = 1
        while step < count:
            value = value + lax.ppermute(value, axis, [(i, i ^ step) for i in range(count)])
            step *= 2
    return value


def to_experts(buffer):
    return lax.all_to_all(buffer, "ep", split_axis=0, concat_axis=0, tiled=True)


def per_device(
    patches,
    labels,
    pixel_mask,
    patch_valid,
    tasks,
    routes,
    dense_weight,
    dense_first,
    dense_second,
    dense_average,
    expert_in,
    in_first,
    in_second,
    in_average,
    expert_out,
    out_first,
    out_second,
    out_average,
):
    ep_count = lax.axis_size("ep")
    experts = min(16, ep_count)
    copies = ep_count // experts
    groups = lax.axis_size("dp")
    ep_place = lax.axis_index("ep")
    dp_place = lax.axis_index("dp")
    own_expert = ep_place // copies
    seq = patches.shape[0]
    capacity = 3 * seq * TOP // (2 * experts)
    shard = dense_weight.shape[0]
    piece = shard // groups
    edges = segment_edges(experts)
    block_count = len(edges) + 1 + 2 * experts
    span, firsts = owner_blocks(edges, shard, ep_count)
    first_block = firsts[ep_place]
    starts = [
        jnp.take(jnp.array([0] + edges + [shard * ep_count] * span, jnp.int32), first_block + k)
        - ep_place * shard
        for k in range(span + 1)
    ]

    def placed(value, at, count):
        return jnp.where(jnp.arange(count) == at, value, 0.0)

    def block_sums(dense_vals, in_vals, out_vals):
        part = lax.dynamic_slice_in_dim(dense_vals, dp_place * piece, piece)
        square = part * part
        index = dp_place * piece + jnp.arange(piece, dtype=jnp.int32)
        listed = placed(jnp.sum(in_vals * in_vals), len(edges) + 1 + own_expert, block_count)
        listed += placed(
            jnp.sum(out_vals * out_vals), len(edges) + 1 + experts + own_expert, block_count
        )
        for k in range(span):
            inside = (index >= starts[k]) & (index < starts[k + 1])
            listed += placed(jnp.sum(jnp.where(inside, square, 0.0)), first_block + k, block_count)
        return listed

    rows = owner_rows(shard, groups)
    offset = lax.rem(ep_place * (shard % 128), 128)
    spread = lax.dynamic_update_slice(
        jnp.zeros((rows * 128,), LOWTYPE), dense_weight.astype(LOWTYPE), (offset,)
    )
    own_part = lax.dynamic_index_in_dim(
        spread.reshape(groups, rows // groups, 128), dp_place, 0, keepdims=False
    )
    low_in, low_out = (expert_in[0].astype(LOWTYPE), expert_out[0].astype(LOWTYPE))
    all_in = lax.all_gather(low_in, ("ep", "dp"))
    all_out = lax.all_gather(low_out, ("ep", "dp"))
    width = low_in.shape[1]
    w_out = all_out.reshape(experts, copies * groups * width, D)

    together = lax.optimization_barrier

    def prepare(labels, pixel_mask, patch_valid, routes, weights):
        named = jnp.sum(
            (routes[:, :, None] == jnp.arange(experts, dtype=jnp.int32)[None, None, :]).astype(FULLTYPE),
            1,
        )
        earlier = jnp.arange(seq)[:, None] > jnp.arange(seq)[None, :]
        table = jnp.where(named > 0, plain(earlier.astype(LOWTYPE), named.astype(LOWTYPE)), -1.0)
        weight_pix = (pixel_mask * patch_valid[:, None]).astype(FULLTYPE)
        class_hot = labels[:, :, None] == jnp.arange(C, dtype=jnp.int32)[None, None, :]
        return (
            table,
            table.T.reshape(experts, 1, seq),
            jnp.sum(named, 0).astype(jnp.int32),
            jnp.where(patch_valid > 0, 0.0, NEG).astype(FULLTYPE).reshape(seq, 1),
            jnp.sum(weight_pix, 1),
            jnp.sum(jnp.where(class_hot, weight_pix[:, :, None], 0.0), 1),
            block_sums(*weights),
        )

    (*mats, rest), prepared = gather_weights(
        own_part,
        shard,
        ep_place,
        dp_place,
        experts,
        (
            prepare,
            (labels, pixel_mask, patch_valid, routes, (dense_weight, expert_in, expert_out)),
        ),
    )
    table, place, loads, down, count_tok, counts, weight_sums = prepared
    first_block, starts, table = together((first_block, starts, table))
    steps = [(axis, 2**k) for axis in ("dp", "ep") for k in range(lax.axis_size(axis).bit_length() - 1)]
    fourth = -(-len(steps) // 4)

    def add_steps(value, turn):
        for axis, step in steps[turn * fourth : (turn + 1) * fourth]:
            count = lax.axis_size(axis)
            value = value + lax.ppermute(value, axis, [(i, i ^ step) for i in range(count)])
        return value

    total = add_steps(jnp.sum(count_tok).reshape(1), 0)
    w_patch, w_qkv, w_attn = (mats[0], mats[1:4], mats[4:7])
    w_up, w_down = (mats[7:9], mats[9:11])
    router_rows, head_rows = (TASKS * D * experts // 128, D * C // 128)
    w_router = rest[:router_rows].reshape(TASKS, D, experts).astype(LOWTYPE)
    w_head = rest[router_rows : router_rows + head_rows].reshape(D, C).astype(LOWTYPE)
    norms = rest[router_rows + head_rows :].reshape(2, 7, D)
    task = tasks[0]
    router = lax.dynamic_index_in_dim(w_router, task, 0, keepdims=False)

    def dispatch(send):
        return to_experts(jnp.repeat(send, copies, axis=0)).reshape(-1, D)

    together = lax.optimization_barrier

    def norm_rows(layer):
        rows = [norms[0, 2 * layer], norms[1, 2 * layer]]
        if layer < 3:
            rows += [norms[0, 2 * layer + 1], norms[1, 2 * layer + 1]]
        return jnp.pad(jnp.stack(rows), ((0, 8 - len(rows)), (0, 0)))

    x0, *kept0, x1, act0, slope0 = layer_forward(
        patches, w_patch, w_qkv[0], w_attn[0], norm_rows(0), down, w_up[0], w_down[0]
    )
    x1, all_in, total = together((x1, all_in, total))
    total = add_steps(total, 1)
    mid1, c16, *kept1 = layer_forward(
        x1, None, w_qkv[1], w_attn[1], norm_rows(1), down, None, None
    )
    c16, total = together((c16, total))
    total = add_steps(total, 2)
    w_in = all_in.reshape(experts, copies * groups, D, width)
    if width % 128:
        w_in = jnp.swapaxes(w_in, 1, 2).reshape(experts, 1, D, copies * groups * width)
    gates, spread_place, spread_gate, act1, slope1, *sent = moe_up(
        loads, c16, router, table, place, w_in, capacity
    )
    x2, taken = moe_down(loads, mid1, spread_place, spread_gate, act1, w_out)
    x2, sent, total = together((x2, sent, total))
    total = add_steps(total, 3)
    rows_a = dispatch(sent[0])
    *kept2, x3, act2, slope2 = layer_forward(
        x2, None, w_qkv[2], w_attn[2], norm_rows(2), down, w_up[1], w_down[1]
    )
    x3, sent, rows_a = together((x3, sent, rows_a))
    rows_b = dispatch(sent[1])
    loss_lanes, d_head, d_normf, grad = head_call(
        x3, norm_rows(3), w_head, counts, count_tok, total
    )
    local = loss_lanes[0, 0]
    grad, local = together((grad, local))
    d_qkv2, d_attn2, d_norm2, d_up1, d_down1, grad = layer_backward(
        grad, x2, (*kept2, act2, slope2), w_qkv[2], w_attn[2], norm_rows(2), down,
        (w_up[1], w_down[1]), None, None,
    )
    grad, sent, rows_b = together((grad, sent, rows_b))
    rows_c = dispatch(sent[2])
    d_own_router, d_c, *dy16 = moe_gate_backward(
        loads, grad, c16, router, gates, place, spread_gate, taken, capacity
    )
    d_c, dy16, rows_c = together((d_c, dy16, rows_c))
    dy_a = dispatch(dy16[0])
    d_c = moe_backward(loads, d_c, spread_place, w_in, w_out, dy16, slope1)
    d_c, dy16, dy_a = together((d_c, dy16, dy_a))
    dy_b = dispatch(dy16[1])
    task_hot = (jnp.arange(TASKS, dtype=jnp.int32) == task)[:, None, None]
    d_router = jnp.where(task_hot, d_own_router[None], 0.0)
    d_qkv1, d_attn1, d_norm1, grad = layer_backward(
        grad, x1, (mid1, c16, *kept1), w_qkv[1], w_attn[1], norm_rows(1), down, None, d_c, None
    )
    grad, dy16, dy_b = together((grad, dy16, dy_b))
    dy_c = dispatch(dy16[2])
    d_qkv0, d_attn0, d_norm0, d_up0, d_down0, d_patch = layer_backward(
        grad, x0, (*kept0, act0, slope0), w_qkv[0], w_attn[0], norm_rows(0), down,
        (w_up[0], w_down[0]), None, patches,
    )
    d_patch, dy_c = together((d_patch, dy_c))
    expert_rows, expert_dy = ([rows_a, rows_b, rows_c], [dy_a, dy_b, dy_c])
    d_rest = jnp.concatenate(
        [
            d_router.reshape(router_rows, 128),
            d_head[:, :C].reshape(head_rows, 128),
        ]
    )
    packed = pack_gradients(
        [d_patch, d_qkv0, d_qkv1, d_qkv2, d_attn0, d_attn1, d_attn2, d_up0, d_up1, d_down0, d_down1],
        d_rest, [d_norm0, d_norm1, d_norm2, d_normf], shard, ep_count, groups, dp_place, experts,
    )
    if groups == 2:
        summed = packed[0][0] + swap_dp(packed[1][0]).astype(FULLTYPE)
    else:
        summed = lax.psum_scatter(packed[0], "dp", scatter_dimension=0, tiled=True)[0]
    arrived = to_experts(summed.astype(LOWTYPE))

    own_in = lax.dynamic_index_in_dim(
        all_in.reshape(ep_count, groups, D, width), ep_place, 0, keepdims=False
    )
    own_out = lax.dynamic_index_in_dim(
        all_out.reshape(ep_count, groups, width, D), ep_place, 0, keepdims=False
    )
    if groups == 2:

        def weight_grads(member):
            return moe_weight_backward(
                expert_rows,
                expert_dy,
                lax.dynamic_index_in_dim(own_in, member, 0, keepdims=False),
                lax.dynamic_index_in_dim(own_out, member, 0, keepdims=False),
            )

        theirs = weight_grads(1 - dp_place)
        away = [swap_dp(t.astype(jnp.bfloat16)) for t in theirs]
        mine = weight_grads(dp_place)
        mine, away, arrived = together((mine, away, arrived))
        d_in, d_out = [(m + t.astype(FULLTYPE))[None] for m, t in zip(mine, away)]
    else:
        d_in, d_out = moe_weight_backward(
            expert_rows,
            expert_dy,
            jnp.swapaxes(own_in, 0, 1).reshape(D, groups * width),
            own_out.reshape(groups * width, D),
        )
        d_in, d_out = (
            lax.psum_scatter(
                value[None].astype(jnp.bfloat16), "dp", scatter_dimension=axis, tiled=True
            ).astype(FULLTYPE)
            for value, axis in ((d_in, 2), (d_out, 1))
        )
    own_sum = jnp.sum(arrived.astype(FULLTYPE), 0)
    dense_grad = lax.dynamic_slice_in_dim(
        join_dp(own_sum, dp_place).reshape(-1), offset, shard
    )
    own_grad = lax.dynamic_slice_in_dim(dense_grad, dp_place * piece, piece)
    sums = sum_all(
        together(placed(local, 0, 2 + block_count)
        + placed(jnp.sum(own_grad * own_grad) + jnp.sum(d_in * d_in) + jnp.sum(d_out * d_out), 1, 2 + block_count)
        + jnp.pad(weight_sums, (2, 0)))
    )
    loss, grad_total, weight_total = (sums[0] / total, sums[1], sums[2:])
    grad_norm = jnp.sqrt(grad_total)
    clip = CLIP_NORM / jnp.maximum(grad_norm, CLIP_NORM)

    def moments(weight, first, second, gradient):
        gradient = gradient * clip
        first_new = DECAY_ONE * first + (1.0 - DECAY_ONE) * gradient
        second_new = DECAY_TWO * second + (1.0 - DECAY_TWO) * gradient * gradient
        return (
            first_new,
            second_new,
            first_new / (jnp.sqrt(second_new) + EPS_ADAM) + WEIGHT_DECAY * weight,
        )

    dense_m, dense_v, dense_step = moments(dense_weight, dense_first, dense_second, dense_grad)
    in_m, in_v, in_step = moments(expert_in, in_first, in_second, d_in)
    out_m, out_v, out_step = moments(expert_out, out_first, out_second, d_out)
    update_total = sum_all(together(block_sums(dense_step, in_step, out_step)))
    weight_norm = jnp.sqrt(weight_total)
    update_norm = jnp.sqrt(update_total)
    ratio = weight_norm / (update_norm + EPS_NORM)
    whole_index = jnp.arange(shard, dtype=jnp.int32)
    dense_ratio = jnp.broadcast_to(jnp.take(ratio, first_block), (shard,))
    for k in range(1, span):
        dense_ratio = jnp.where(whole_index >= starts[k], jnp.take(ratio, jnp.minimum(first_block + k, block_count - 1)), dense_ratio)
    in_ratio = lax.dynamic_index_in_dim(ratio, 14 + own_expert, 0, keepdims=False)
    out_ratio = lax.dynamic_index_in_dim(ratio, 14 + experts + own_expert, 0, keepdims=False)

    def finish(weight, average, step, rate):
        new = weight - RATE * rate * step
        return (new, AVERAGE * average + (1.0 - AVERAGE) * new, new.astype(LOWTYPE))

    dense_new, dense_avg, dense_low = finish(dense_weight, dense_average, dense_step, dense_ratio)
    in_new, in_avg, in_low = finish(expert_in, in_average, in_step, in_ratio)
    out_new, out_avg, out_low = finish(expert_out, out_average, out_step, out_ratio)
    block_norms = jnp.stack([weight_norm, update_norm], 1)
    return (
        loss.reshape(1),
        grad_norm.reshape(1),
        block_norms,
        dense_new,
        dense_m,
        dense_v,
        dense_avg,
        dense_low,
        in_new,
        in_m,
        in_v,
        in_avg,
        in_low,
        out_new,
        out_m,
        out_v,
        out_avg,
        out_low,
    )


def solution(mesh):
    in_specs = (
        P(("ep", "dp"), None),
        P(("ep", "dp"), None),
        P(("ep", "dp"), None),
        P(("ep", "dp")),
        P(("ep", "dp")),
        P(("ep", "dp"), None),
        P("ep"),
        P("ep"),
        P("ep"),
        P("ep"),
        P("ep", None, "dp"),
        P("ep", None, "dp"),
        P("ep", None, "dp"),
        P("ep", None, "dp"),
        P("ep", "dp", None),
        P("ep", "dp", None),
        P("ep", "dp", None),
        P("ep", "dp", None),
    )
    out_specs = (
        P(),
        P(),
        P(),
        P("ep"),
        P("ep"),
        P("ep"),
        P("ep"),
        P("ep"),
        P("ep", None, "dp"),
        P("ep", None, "dp"),
        P("ep", None, "dp"),
        P("ep", None, "dp"),
        P("ep", None, "dp"),
        P("ep", "dp", None),
        P("ep", "dp", None),
        P("ep", "dp", None),
        P("ep", "dp", None),
        P("ep", "dp", None),
    )
    return jax.shard_map(
        per_device, mesh=mesh, in_specs=in_specs, out_specs=out_specs, check_vma=False
    )
```

```python
import functools
import math

import jax
import jax.numpy as jnp
from jax import lax
from jax.experimental import pallas as pl
from jax.experimental.pallas import tpu as pltpu
from jax.sharding import PartitionSpec as P

D = 384
HEADS = 6
HD = 64
FF = 1536
TOP = 4
C = 40
PIX = 768
TASKS = 4


EPS_NORM = 1e-05
CLIP_NORM = 0.002
RATE = 0.3
DECAY_ONE = 0.5
DECAY_TWO = 0.5
WEIGHT_DECAY = 0.01
EPS_ADAM = 1e-09
AVERAGE = 0.9
SCALE = 0.125
LOWTYPE = jnp.bfloat16
FULLTYPE = jnp.float32


def plain(left, right):
    return jnp.dot(left, right, preferred_element_type=FULLTYPE)


def left_t(left, right):
    return lax.dot_general(left, right, (((0,), (0,)), ((), ())), preferred_element_type=FULLTYPE)


def right_t(left, right):
    return lax.dot_general(left, right, (((1,), (1,)), ((), ())), preferred_element_type=FULLTYPE)


def segment_sizes(experts):
    return (
        [PIX * D]
        + [3 * D * D] * 3
        + [D * D] * 3
        + [D * FF] * 2
        + [FF * D] * 2
        + [TASKS * D * experts, D * C, 14 * D]
    )


def owner_blocks(edges, shard, owners):
    firsts = [sum(edge <= shard * i for edge in edges) for i in range(owners)]
    lasts = [sum(edge < shard * (i + 1) for edge in edges) for i in range(owners)]
    span = max(b - a + 1 for a, b in zip(firsts, lasts))
    return (span, jnp.array(firsts, jnp.int32))


def segment_edges(experts):
    edges, edge = [], 0
    for size in segment_sizes(experts)[:-1]:
        edge += size
        edges.append(edge)
    return edges


VMEM_LIMIT = 56 * 2**20
ROWS = 512
TILE = 32
KEYS = 64
QUERIES = 512
NEG = -1e30


def rows_of(index, size=ROWS):
    return pl.ds(pl.multiple_of(index * size, size), size)


def norm_parts(x):
    cent = x - jnp.mean(x, -1, keepdims=True)
    scale = lax.rsqrt(jnp.mean(cent * cent, -1, keepdims=True) + EPS_NORM)
    return (cent * scale, scale)


def norm_low(x, gain, bias):
    return (norm_parts(x)[0] * gain + bias).astype(LOWTYPE)


def norm_pull(x, gain, grad):
    unit, scale = norm_parts(x)
    inner = grad * gain
    d_x = scale * (
        inner
        - jnp.mean(inner, -1, keepdims=True)
        - unit * jnp.mean(inner * unit, -1, keepdims=True)
    )
    return (d_x, jnp.sum(grad * unit, 0, keepdims=True), jnp.sum(grad, 0, keepdims=True))


def gelu_pair(h):
    cdf = 0.5 + 0.5 * lax.erf(h * 0.7071067811865476)
    e = jnp.exp((h * h) * -0.5)
    return (h * cdf, cdf + h * (e * 0.3989422804014327))


def half_masks(scale):
    lane = lax.broadcasted_iota(jnp.int32, (1, 128), 1)
    return [jnp.where((lane < HD) == (h == 0), scale, 0.0).astype(LOWTYPE) for h in (0, 1)]


def beside_head(head, own, extras):
    lane = lax.broadcasted_iota(jnp.int32, own.shape, 1)
    value = own.astype(FULLTYPE) * half_masks(1.0)[head].astype(FULLTYPE)
    for k, extra in enumerate(extras):
        value = jnp.where(lane == HD * (1 - head) + k, extra, value)
    return value.astype(LOWTYPE)


def three_parts(column):
    high = column.astype(LOWTYPE).astype(FULLTYPE)
    middle = (column - high).astype(LOWTYPE).astype(FULLTYPE)
    return [high, middle, column - high - middle]


def attend_rows(qkv_ref, bias_ref, o_ref, aug_ref, keys_ref, s_ref, p_ref):
    seq = qkv_ref.shape[0]
    masks = half_masks(SCALE)
    lane = lax.broadcasted_iota(jnp.int32, (ROWS, 128), 1)

    for pair in range(HEADS // 2):
        cols = pl.ds(pair * 128, 128)

        def prepare(i, carry, pair=pair):
            rows = rows_of(i)
            keys = qkv_ref[rows, pl.ds(D + pair * 128, 128)]
            for h in (0, 1):
                keys_ref[h, rows, :] = beside_head(h, keys, [bias_ref[rows, :]])
            return carry

        lax.fori_loop(0, seq // ROWS, prepare, 0)

        def body(i, carry, pair=pair, cols=cols):
            rows = rows_of(i)
            query = qkv_ref[rows, cols]
            values = qkv_ref[:, pl.ds(2 * D + pair * 128, 128)]
            outs = []
            for h in (0, 1):
                s_ref[h] = right_t(beside_head(h, query * masks[h], [1.0]), keys_ref[h])
            for h in (0, 1):
                for first in range(0, ROWS, TILE):
                    s = s_ref[h, first : first + TILE, :]
                    top = jnp.max(s, -1, keepdims=True)
                    e = jnp.exp(s - top)
                    total = jnp.sum(e, -1, keepdims=True)
                    p_ref[h, first : first + TILE, :] = (e * (1.0 / total)).astype(LOWTYPE)
                    at = pl.ds(pl.multiple_of(i * ROWS + first, TILE), TILE)
                    aug_ref[at, pl.ds((2 * pair + h) * 128, 128)] = beside_head(
                        h,
                        query[first : first + TILE] * masks[h],
                        [1.0] + three_parts(-(top + jnp.log(total))),
                    )
            for h in (0, 1):
                outs.append(plain(p_ref[h], values))
            o_ref[rows, cols] = jnp.where(lane < HD, outs[0], outs[1]).astype(LOWTYPE)
            return carry

        lax.fori_loop(0, seq // ROWS, body, 0)


def forward_kernel(has_patch, has_ff, *refs):
    refs = list(refs)
    x_in = refs.pop(0)
    if has_patch:
        w_patch = refs.pop(0)
    w_qkv, w_attn, norms, bias = refs[:4]
    refs = refs[4:]
    if has_ff:
        w_up, w_down = refs[:2]
        refs = refs[2:]
    if has_patch:
        x_ref = refs.pop(0)
    else:
        x_ref = x_in
    mid_ref, c_ref, qkv_ref, o_ref, aug_ref = refs[:5]
    refs = refs[5:]
    if has_ff:
        next_ref, act_ref, slope_ref = refs[:3]
    keys_ref, s_ref, p_ref = refs[-3:]
    seq = x_ref.shape[0]

    def project(i, carry):
        rows = rows_of(i)
        if has_patch:
            x_ref[rows, :] = plain(x_in[rows, :], w_patch[...])
        a16 = norm_low(x_ref[rows, :], norms[0:1, :], norms[1:2, :])
        qkv_ref[rows, :] = plain(a16, w_qkv[...]).astype(LOWTYPE)
        return carry

    lax.fori_loop(0, seq // ROWS, project, 0)
    attend_rows(qkv_ref, bias, o_ref, aug_ref, keys_ref, s_ref, p_ref)

    def finish(i, carry):
        rows = rows_of(i)
        mid = x_ref[rows, :] + plain(o_ref[rows, :], w_attn[...])
        mid_ref[rows, :] = mid
        c16 = norm_low(mid, norms[2:3, :], norms[3:4, :])
        c_ref[rows, :] = c16
        if has_ff:
            act, slope = gelu_pair(plain(c16, w_up[...]))
            act16 = act.astype(LOWTYPE)
            act_ref[rows, :] = act16
            slope_ref[rows, :] = slope
            next_ref[rows, :] = mid + plain(act16, w_down[...])
        return carry

    lax.fori_loop(0, seq // ROWS, finish, 0)


def in_vmem(count):
    return [pl.BlockSpec(memory_space=pltpu.VMEM)] * count


def local_call(kernel, outs, args, flops, scratch=()):
    moved = sum(math.prod(a.shape) * a.dtype.itemsize for a in (*args, *outs))
    return pl.pallas_call(
        kernel,
        out_shape=outs,
        in_specs=in_vmem(len(args)),
        out_specs=in_vmem(len(outs)),
        scratch_shapes=scratch,
        compiler_params=pltpu.CompilerParams(vmem_limit_bytes=VMEM_LIMIT),
        cost_estimate=pl.CostEstimate(flops=flops, bytes_accessed=moved, transcendentals=0),
    )(*args)


def shaped(shape, dtype):
    return jax.ShapeDtypeStruct(shape, dtype)


def layer_forward(x, w_patch, w_qkv, w_attn, norms, bias, w_up, w_down):
    seq = x.shape[0]
    has_patch, has_ff = (w_patch is not None, w_up is not None)
    args = [x] + [w_patch] * has_patch + [w_qkv, w_attn, norms, bias] + [w_up, w_down] * has_ff
    outs = [shaped((seq, D), FULLTYPE)] * has_patch
    outs += [
        shaped((seq, D), FULLTYPE),
        shaped((seq, D), LOWTYPE),
        shaped((seq, 3 * D), LOWTYPE),
        shaped((seq, D), LOWTYPE),
        shaped((seq, 128 * HEADS), LOWTYPE),
    ]
    if has_ff:
        outs += [
            shaped((seq, D), FULLTYPE),
            shaped((seq, FF), LOWTYPE),
            shaped((seq, FF), FULLTYPE),
        ]
    flops = 2 * seq * D * (4 * D + 4 * seq + 2 * FF * has_ff)
    kernel = functools.partial(forward_kernel, has_patch, has_ff)
    scratch = [
        pltpu.VMEM((2, seq, 128), LOWTYPE),
        pltpu.VMEM((2, ROWS, seq), FULLTYPE),
        pltpu.VMEM((2, ROWS, seq), LOWTYPE),
    ]
    return local_call(kernel, outs, args, flops, scratch)


def attend_pull(qkv_ref, o_ref, do_ref, aug_ref, valid_ref, dqkv_ref, dk_ref, dv_ref, sides):
    seq = qkv_ref.shape[0]
    keys_ref, values_ref, across_ref, s_ref, dp_ref, p_ref, ds_ref = sides
    ones = half_masks(1.0)

    for pair in range(HEADS // 2):
        cols = pl.ds(pair * 128, 128)
        dk_ref[...] = jnp.zeros_like(dk_ref)
        dv_ref[...] = jnp.zeros_like(dv_ref)

        def prepare(i, carry, pair=pair):
            rows = rows_of(i)
            keys = qkv_ref[rows, pl.ds(D + pair * 128, 128)]
            values = qkv_ref[rows, pl.ds(2 * D + pair * 128, 128)]
            across_ref[:, rows] = keys.astype(FULLTYPE).T.astype(LOWTYPE)
            for h in (0, 1):
                keys_ref[h, rows, :] = beside_head(h, keys, [valid_ref[rows, :], 1.0, 1.0, 1.0])
                values_ref[h, rows, :] = beside_head(h, values, [1.0, 1.0, 1.0])
            return carry

        lax.fori_loop(0, seq // ROWS, prepare, 0)

        def body(i, carry, pair=pair, cols=cols):
            rows = rows_of(i, QUERIES)
            d_out = do_ref[rows, cols]
            both = d_out.astype(FULLTYPE) * o_ref[rows, cols].astype(FULLTYPE)
            d_query = []
            for h in (0, 1):
                own_q = aug_ref[rows, pl.ds((2 * pair + h) * 128, 128)]
                s_ref[h] = right_t(keys_ref[h], own_q)
                delta = jnp.sum(both * ones[h].astype(FULLTYPE), -1, keepdims=True)
                own_d = beside_head(h, d_out, three_parts(-delta))
                dp_ref[h] = right_t(values_ref[h], own_d)
            for h in (0, 1):
                for first in range(0, seq, KEYS):
                    at, side = (pl.ds(first, KEYS), pl.ds(h * QUERIES, QUERIES))
                    probs = jnp.exp(s_ref[h, at, :])
                    p_ref[at, side] = probs.astype(LOWTYPE)
                    ds_ref[at, side] = (probs * dp_ref[h, at, :]).astype(LOWTYPE)
            own = [
                aug_ref[rows, pl.ds((2 * pair + h) * 128, 128)] * ones[h] for h in (0, 1)
            ]
            dv_ref[...] += plain(p_ref[...], jnp.concatenate([d_out * ones[h] for h in (0, 1)]))
            dk_ref[...] += plain(ds_ref[...], jnp.concatenate(own))
            for h in (0, 1):
                d_query.append(
                    plain(across_ref[pl.ds(h * HD, HD), :], ds_ref[:, pl.ds(h * QUERIES, QUERIES)])
                )
            turned = jnp.concatenate(d_query).T * SCALE
            dqkv_ref[rows, cols] = turned.astype(LOWTYPE)
            return carry

        lax.fori_loop(0, seq // QUERIES, body, 0)
        dqkv_ref[:, pl.ds(D + pair * 128, 128)] = dk_ref[...].astype(LOWTYPE)
        dqkv_ref[:, pl.ds(2 * D + pair * 128, 128)] = dv_ref[...].astype(LOWTYPE)


def weight_pull(left_ref, right_ref, out_ref, tile=384):
    def body(j, carry):
        cols = rows_of(j, tile)
        out_ref[cols, :] = left_t(left_ref[:, cols], right_ref[...])
        return carry

    lax.fori_loop(0, left_ref.shape[1] // tile, body, 0)


def backward_kernel(has_patch, has_ff, *refs):
    refs = list(refs)
    grad, x_ref, mid_ref, qkv, o_ref, aug, w_qkv, w_attn, norms, valid = refs[:10]
    refs = refs[10:]
    if has_ff:
        c_ref, act, slope, w_up, w_down = refs[:5]
        refs = refs[5:]
    else:
        d_c_ref = refs.pop(0)
    if has_patch:
        patches = refs.pop(0)
    d_qkvw, d_attn, d_norms = refs[:3]
    refs = refs[3:]
    if has_ff:
        d_up, d_down = refs[:2]
        refs = refs[2:]
    if has_patch:
        d_patch = refs.pop(0)
    else:
        dx_ref = refs.pop(0)
    gmid, low, do_ref, dqkv, dk, dv = refs[:6]
    sides, refs = (refs[6:13], refs[13:])
    if has_ff:
        dh_ref = refs.pop(0)
    seq = grad.shape[0]
    blocks_count = seq // ROWS
    d_norms[...] = jnp.zeros_like(d_norms)

    def feed(i, carry):
        rows = rows_of(i)
        g = grad[rows, :]
        if has_ff:
            g16 = g.astype(LOWTYPE)
            low[rows, :] = g16
            dh16 = (right_t(g16, w_down[...]) * slope[rows, :]).astype(LOWTYPE)
            dh_ref[rows, :] = dh16
            d_c = right_t(dh16, w_up[...])
        else:
            d_c = d_c_ref[rows, :]
        d_x, d_gain, d_bias = norm_pull(mid_ref[rows, :], norms[2:3, :], d_c)
        gmid[rows, :] = g + d_x
        d_norms[2:3, :] += d_gain
        d_norms[3:4, :] += d_bias
        return carry

    lax.fori_loop(0, blocks_count, feed, 0)
    if has_ff:
        weight_pull(act, low, d_down)
        weight_pull(c_ref, dh_ref, d_up)

    def out_pull(i, carry):
        rows = rows_of(i)
        g16 = gmid[rows, :].astype(LOWTYPE)
        low[rows, :] = g16
        do_ref[rows, :] = right_t(g16, w_attn[...]).astype(LOWTYPE)
        return carry

    lax.fori_loop(0, blocks_count, out_pull, 0)
    weight_pull(o_ref, low, d_attn)
    attend_pull(qkv, o_ref, do_ref, aug, valid, dqkv, dk, dv, sides)

    def in_pull(i, carry):
        rows = rows_of(i)
        d_a = right_t(dqkv[rows, :], w_qkv[...])
        x = x_ref[rows, :]
        d_x, d_gain, d_bias = norm_pull(x, norms[0:1, :], d_a)
        total = gmid[rows, :] + d_x
        if has_patch:
            gmid[rows, :] = total
        else:
            dx_ref[rows, :] = total
        low[rows, :] = norm_low(x, norms[0:1, :], norms[1:2, :])
        d_norms[0:1, :] += d_gain
        d_norms[1:2, :] += d_bias
        return carry

    lax.fori_loop(0, blocks_count, in_pull, 0)
    weight_pull(low, dqkv, d_qkvw)
    if has_patch:

        def lower(i, carry):
            rows = rows_of(i)
            low[rows, :] = gmid[rows, :].astype(LOWTYPE)
            return carry

        lax.fori_loop(0, blocks_count, lower, 0)
        weight_pull(patches, low, d_patch)


def layer_backward(grad, x, kept, w_qkv, w_attn, norms, valid, ff, d_c, patches):
    seq = grad.shape[0]
    mid, c16, qkv16, o16, aug = kept[:5]
    has_ff, has_patch = (ff is not None, patches is not None)
    args = [grad, x, mid, qkv16, o16, aug, w_qkv, w_attn, norms, valid]
    args += [c16, *kept[5:], *ff] if has_ff else [d_c]
    args += [patches] * has_patch
    outs = [
        shaped((D, 3 * D), FULLTYPE),
        shaped((D, D), FULLTYPE),
        shaped((8, D), FULLTYPE),
    ]
    if has_ff:
        outs += [shaped((D, FF), FULLTYPE), shaped((FF, D), FULLTYPE)]
    outs += [shaped((PIX, D), FULLTYPE) if has_patch else shaped((seq, D), FULLTYPE)]
    scratch = [
        pltpu.VMEM((seq, D), FULLTYPE),
        pltpu.VMEM((seq, D), LOWTYPE),
        pltpu.VMEM((seq, D), LOWTYPE),
        pltpu.VMEM((seq, 3 * D), LOWTYPE),
        pltpu.VMEM((seq, 128), FULLTYPE),
        pltpu.VMEM((seq, 128), FULLTYPE),
        pltpu.VMEM((2, seq, 128), LOWTYPE),
        pltpu.VMEM((2, seq, 128), LOWTYPE),
        pltpu.VMEM((128, seq), LOWTYPE),
        pltpu.VMEM((2, seq, QUERIES), FULLTYPE),
        pltpu.VMEM((2, seq, QUERIES), FULLTYPE),
        pltpu.VMEM((seq, 2 * QUERIES), LOWTYPE),
        pltpu.VMEM((seq, 2 * QUERIES), LOWTYPE),
    ] + [pltpu.VMEM((seq, FF), LOWTYPE)] * has_ff
    flops = 2 * seq * D * (8 * D + 10 * seq + 4 * FF * has_ff + PIX * has_patch)
    return local_call(
        functools.partial(backward_kernel, has_patch, has_ff), outs, args, flops, scratch
    )


def head_kernel(x_ref, norms, w_head, counts, count, total, loss, d_head, d_norms, grad, f_ref, dl_ref):
    seq = x_ref.shape[0]
    d_norms[...] = jnp.zeros_like(d_norms)
    loss[...] = jnp.zeros_like(loss)
    real = lax.broadcasted_iota(jnp.int32, (1, 128), 1) < C

    def body(i, carry):
        rows = rows_of(i)
        x = x_ref[rows, :]
        f16 = norm_low(x, norms[0:1, :], norms[1:2, :])
        f_ref[rows, :] = f16
        logits = plain(f16, w_head[...])
        shown = jnp.where(real, logits, NEG)
        top = jnp.max(shown, -1, keepdims=True)
        e = jnp.exp(shown - top)
        under = jnp.sum(e, -1, keepdims=True)
        weight = count[rows, :]
        classes = counts[rows, :]
        part = weight * (top + jnp.log(under)) - jnp.sum(classes * logits, -1, keepdims=True)
        loss[...] += jnp.broadcast_to(jnp.sum(part, 0, keepdims=True), loss.shape)
        d_logits = ((weight * (e * (1.0 / under)) - classes) / total[...]).astype(LOWTYPE)
        dl_ref[rows, :] = d_logits
        d_x, d_gain, d_bias = norm_pull(x, norms[0:1, :], right_t(d_logits, w_head[...]))
        grad[rows, :] = d_x
        d_norms[0:1, :] += d_gain
        d_norms[1:2, :] += d_bias
        return carry

    lax.fori_loop(0, seq // ROWS, body, 0)
    weight_pull(f_ref, dl_ref, d_head)


def head_call(x, norms, w_head, counts, count, total):
    seq = x.shape[0]
    outs = [
        shaped((1, 128), FULLTYPE),
        shaped((D, 128), FULLTYPE),
        shaped((8, D), FULLTYPE),
        shaped((seq, D), FULLTYPE),
    ]
    args = [
        x,
        norms,
        jnp.pad(w_head, ((0, 0), (0, 128 - C))),
        jnp.pad(counts, ((0, 0), (0, 128 - C))),
        count.reshape(seq, 1),
        total.reshape(1, 1),
    ]
    scratch = [pltpu.VMEM((seq, D), LOWTYPE), pltpu.VMEM((seq, 128), LOWTYPE)]
    return local_call(head_kernel, outs, args, 6 * seq * D * 128, scratch)


SLOTS = 128


def by_load(load, capacity, work):
    for count in range(SLOTS, capacity + 1, SLOTS):
        inside = load > count - SLOTS if count > SLOTS else load >= 0
        if count < capacity:
            inside = inside & (load <= count)
        pl.when(inside)(functools.partial(work, count))


def slot_select(place, count):
    row = lax.broadcasted_iota(jnp.int32, (count, place.shape[1]), 0).astype(FULLTYPE)
    return jnp.where(place == row, 1.0, 0.0).astype(LOWTYPE)


def put_blocks(refs, rows):
    for block, ref in enumerate(refs):
        if block * SLOTS < rows.shape[0]:
            ref[0] = rows[block * SLOTS : (block + 1) * SLOTS]
        else:
            ref[0] = jnp.zeros(ref.shape[1:], ref.dtype)


def column_of(table, expert):
    lane = lax.broadcasted_iota(jnp.int32, table.shape, 1)
    return jnp.sum(jnp.where(lane == expert, table, 0.0), -1, keepdims=True)


def patch_select(spread, count):
    lane = lax.broadcasted_iota(jnp.int32, (1, 128), 1).astype(FULLTYPE)
    return jnp.concatenate(
        [
            jnp.where(spread == lane + first, 1.0, 0.0).astype(LOWTYPE)
            for first in range(0, count, 128)
        ],
        1,
    )


def moe_up_kernel(
    loads, c_ref, router, table, place, w_in,
    gates_ref, spread_place, spread_gate, act_ref, slope_ref, *rows_refs,
):
    expert = pl.program_id(0)
    seq, capacity, parts = (c_ref.shape[0], act_ref.shape[0], w_in.shape[1])
    width = w_in.shape[3]

    @pl.when(expert == 0)
    def _():
        def start(i, carry):
            rows = rows_of(i)
            z = plain(c_ref[rows, :], router[...])
            named = table[rows, :] >= 0
            shown = jnp.where(named, z, NEG)
            e = jnp.where(named, jnp.exp(shown - jnp.max(shown, -1, keepdims=True)), 0.0)
            gates_ref[rows, :] = e / jnp.sum(e, -1, keepdims=True)
            return carry

        lax.fori_loop(0, seq // ROWS, start, 0)

    def fan(i, carry):
        rows = rows_of(i)
        for source, out in ((table, spread_place), (gates_ref, spread_gate)):
            out[0, rows, :] = jnp.broadcast_to(column_of(source[rows, :], expert), (ROWS, 128))
        return carry

    lax.fori_loop(0, seq // ROWS, fan, 0)

    def work(count):
        at = pl.ds(0, count)
        rows = plain(slot_select(place[0], count), c_ref[...]).astype(LOWTYPE)
        put_blocks(rows_refs, rows)
        for part in range(parts):
            step = width // 3 if width % 384 == 0 else width
            for first in range(0, width, step):
                act, slope = gelu_pair(plain(rows, w_in[0, part, :, pl.ds(first, step)]))
                units = pl.ds(part * width + first, step)
                slope_ref[at, units] = slope
                act_ref[at, units] = act.astype(LOWTYPE)

    by_load(loads[expert], capacity, work)


def moe_down_kernel(loads, mid_ref, spread_place, spread_gate, act_ref, w_out, next_ref, taken_ref, y_ref):
    expert = pl.program_id(0)
    seq, capacity = (mid_ref.shape[0], act_ref.shape[0])

    @pl.when(expert == 0)
    def _():
        next_ref[...] = mid_ref[...]

    def work(count):
        at = pl.ds(0, count)
        y_ref[at, :] = plain(act_ref[at, :], w_out[0]).astype(LOWTYPE)

        def add(i, carry):
            rows = rows_of(i)
            taken = plain(patch_select(spread_place[0, rows, :], count), y_ref[at, :])
            taken_ref[0, rows, :] = taken.astype(LOWTYPE)
            for first in range(0, D, 128):
                lanes = pl.ds(first, 128)
                next_ref[rows, lanes] += spread_gate[0, rows, :] * taken[:, first : first + 128]
            return carry

        lax.fori_loop(0, seq // ROWS, add, 0)

    by_load(loads[expert], capacity, work)


def moe_gate_kernel(
    loads, grad_ref, c_ref, router, gates, place, spread_gate, taken_ref,
    d_router, d_c, *refs,
):
    dy_refs, (low_ref, dz_ref, d_gates) = (refs[:-3], refs[-3:])
    expert = pl.program_id(0)
    seq, capacity = (grad_ref.shape[0], SLOTS * len(dy_refs))
    lane = lax.broadcasted_iota(jnp.int32, (ROWS, d_gates.shape[1]), 1)

    @pl.when(expert == 0)
    def _():
        d_gates[...] = jnp.zeros_like(d_gates)

    def work(count):
        def one(i, carry):
            rows = rows_of(i)
            grad = grad_ref[rows, :]
            gate = spread_gate[0, rows, :]
            taken = taken_ref[0, rows, :].astype(FULLTYPE)
            d_gate = jnp.sum(grad * taken, -1, keepdims=True)
            d_gates[rows, :] += jnp.where(lane == expert, d_gate, 0.0)
            for first in range(0, D, 128):
                lanes = pl.ds(first, 128)
                low_ref[rows, lanes] = (gate * grad[:, first : first + 128]).astype(LOWTYPE)
            return carry

        lax.fori_loop(0, seq // ROWS, one, 0)
        put_blocks(dy_refs, plain(slot_select(place[0], count), low_ref[...]).astype(LOWTYPE))

    by_load(loads[expert], capacity, work)

    @pl.when(expert == pl.num_programs(0) - 1)
    def _():
        def last(i, carry):
            rows = rows_of(i)
            gate = gates[rows, :]
            d_gate = d_gates[rows, :]
            d_z = gate * (d_gate - jnp.sum(gate * d_gate, -1, keepdims=True))
            dz_ref[rows, :] = d_z.astype(LOWTYPE)
            d_c[rows, :] = right_t(dz_ref[rows, :], router[...])
            return carry

        lax.fori_loop(0, seq // ROWS, last, 0)
        d_router[...] = left_t(c_ref[...], dz_ref[...])


def moe_backward_kernel(loads, start_ref, spread_place, w_in, w_out, slope_ref, *refs):
    dy_refs, (d_c, back_ref) = (refs[:-2], refs[-2:])
    expert = pl.program_id(0)
    seq, capacity, parts = (d_c.shape[0], slope_ref.shape[0], w_in.shape[1])
    width = w_in.shape[3]

    @pl.when(expert == 0)
    def _():
        d_c[...] = start_ref[...]

    def work(count):
        at = pl.ds(0, count)
        d_y = jnp.concatenate([ref[0] for ref in dy_refs[: count // SLOTS]])
        back = jnp.zeros((count, D), FULLTYPE)
        for part in range(parts):
            units = pl.ds(part * width, width)
            d_act = right_t(d_y, w_out[0, units, :])
            d_h = (d_act * slope_ref[at, units]).astype(LOWTYPE)
            back += right_t(d_h, w_in[0, part])
        back_ref[at, :] = back.astype(LOWTYPE)

        def add(i, carry):
            rows = rows_of(i)
            d_c[rows, :] += plain(patch_select(spread_place[0, rows, :], count), back_ref[at, :])
            return carry

        lax.fori_loop(0, seq // ROWS, add, 0)

    by_load(loads[expert], capacity, work)


def moe_weight_kernel(count, *refs):
    rows_refs, dy_refs = (refs[:count], refs[count : 2 * count])
    w_in, w_out, d_in, d_out = refs[2 * count :]

    @pl.when(pl.program_id(0) == 0)
    def _():
        d_in[...] = jnp.zeros_like(d_in)
        d_out[...] = jnp.zeros_like(d_out)

    width = w_in.shape[1]
    step = 384 if width % 384 == 0 else width
    for rows_ref, dy_ref in zip(rows_refs, dy_refs):
        rows, d_y = (rows_ref[...], dy_ref[...])
        for first in range(0, width, step):
            units = pl.ds(first, step)
            act, slope = gelu_pair(plain(rows, w_in[:, units]))
            d_h = (right_t(d_y, w_out[units, :]) * slope).astype(LOWTYPE)
            d_out[units, :] += left_t(act.astype(LOWTYPE), d_y)
            d_in[:, units] += left_t(rows, d_h)


def whole(shape):
    return pl.BlockSpec(shape, lambda e: (0,) * len(shape))


def gridded(kernel, steps, in_specs, outs, out_specs, args, flops, scratch=()):
    moved = sum(math.prod(a.shape) * a.dtype.itemsize for a in (*args, *outs))
    return pl.pallas_call(
        kernel,
        grid=(steps,),
        out_shape=outs,
        in_specs=in_specs,
        out_specs=out_specs,
        scratch_shapes=scratch,
        compiler_params=pltpu.CompilerParams(vmem_limit_bytes=VMEM_LIMIT),
        cost_estimate=pl.CostEstimate(flops=flops, bytes_accessed=moved, transcendentals=0),
    )(*args)


SCALARS = pl.BlockSpec(memory_space=pltpu.SMEM)


def in_spec(w_in):
    return pl.BlockSpec((1,) + w_in.shape[1:], lambda e: (e, 0, 0, 0))


def out_spec(w_out):
    return pl.BlockSpec((1,) + w_out.shape[1:], lambda e: (e, 0, 0))


def spread_spec(seq):
    return pl.BlockSpec((1, seq, 128), lambda e: (e, 0, 0))


def taken_spec(seq):
    return pl.BlockSpec((1, seq, D), lambda e: (e, 0, 0))


def block_shapes(experts, capacity):
    return [shaped((experts, SLOTS, D), LOWTYPE)] * (capacity // SLOTS)


def block_specs(capacity):
    return [pl.BlockSpec((1, SLOTS, D), lambda e: (e, 0, 0))] * (capacity // SLOTS)


def moe_up(loads, c16, router, table, place, w_in, capacity):
    seq, experts = table.shape
    hidden = w_in.shape[1] * w_in.shape[3]
    per = lambda width: pl.BlockSpec((capacity, width), lambda e: (e, 0))
    return gridded(
        moe_up_kernel,
        experts,
        [SCALARS, whole((seq, D)), whole((D, experts)), whole((seq, experts))]
        + [pl.BlockSpec((1, 1, seq), lambda e: (e, 0, 0)), in_spec(w_in)],
        [
            shaped((seq, experts), FULLTYPE),
            shaped((experts, seq, 128), FULLTYPE),
            shaped((experts, seq, 128), FULLTYPE),
            shaped((experts * capacity, hidden), LOWTYPE),
            shaped((experts * capacity, hidden), FULLTYPE),
        ]
        + block_shapes(experts, capacity),
        [whole((seq, experts)), spread_spec(seq), spread_spec(seq), per(hidden), per(hidden)]
        + block_specs(capacity),
        [loads, c16, router, table, place, w_in],
        2 * experts * capacity * D * (hidden + seq),
    )


def moe_down(loads, mid, spread_place, spread_gate, act, w_out):
    seq, experts = (mid.shape[0], w_out.shape[0])
    capacity, hidden = (act.shape[0] // experts, act.shape[1])
    per = lambda width: pl.BlockSpec((capacity, width), lambda e: (e, 0))
    return gridded(
        moe_down_kernel,
        experts,
        [SCALARS, whole((seq, D)), spread_spec(seq), spread_spec(seq), per(hidden), out_spec(w_out)],
        [shaped((seq, D), FULLTYPE), shaped((experts, seq, D), LOWTYPE)],
        [whole((seq, D)), taken_spec(seq)],
        [loads, mid, spread_place, spread_gate, act, w_out],
        2 * experts * capacity * D * (hidden + seq),
        [pltpu.VMEM((capacity, D), LOWTYPE)],
    )


def moe_gate_backward(loads, grad, c16, router, gates, place, spread_gate, taken, capacity):
    seq, experts = gates.shape
    return gridded(
        moe_gate_kernel,
        experts,
        [SCALARS, whole((seq, D)), whole((seq, D)), whole((D, experts)), whole((seq, experts))]
        + [pl.BlockSpec((1, 1, seq), lambda e: (e, 0, 0)), spread_spec(seq), taken_spec(seq)],
        [
            shaped((D, experts), FULLTYPE),
            shaped((seq, D), FULLTYPE),
        ]
        + block_shapes(experts, capacity),
        [whole((D, experts)), whole((seq, D))] + block_specs(capacity),
        [loads, grad, c16, router, gates, place, spread_gate, taken],
        4 * experts * capacity * D * seq,
        [
            pltpu.VMEM((seq, D), LOWTYPE),
            pltpu.VMEM((seq, experts), LOWTYPE),
            pltpu.VMEM((seq, experts), FULLTYPE),
        ],
    )


def moe_backward(loads, start, spread_place, w_in, w_out, dy, slope):
    seq, experts = (start.shape[0], w_out.shape[0])
    capacity, hidden = (slope.shape[0] // experts, w_out.shape[1])
    per = lambda width: pl.BlockSpec((capacity, width), lambda e: (e, 0))
    return gridded(
        moe_backward_kernel,
        experts,
        [SCALARS, whole((seq, D)), spread_spec(seq), in_spec(w_in), out_spec(w_out)]
        + [per(hidden)]
        + block_specs(capacity),
        [shaped((seq, D), FULLTYPE)],
        [whole((seq, D))],
        [loads, start, spread_place, w_in, w_out, slope, *dy],
        2 * experts * capacity * D * (2 * hidden + seq),
        [pltpu.VMEM((capacity, D), LOWTYPE)],
    )[0]


def moe_weight_backward(rows, dy, w_in, w_out):
    count, width = (rows[0].shape[0], w_in.shape[1])
    step = 512
    per = pl.BlockSpec((step, D), lambda i: (i, 0))
    return gridded(
        functools.partial(moe_weight_kernel, len(rows)),
        count // step,
        [per] * (2 * len(rows)) + [whole((D, width)), whole((width, D))],
        [shaped((D, width), FULLTYPE), shaped((width, D), FULLTYPE)],
        [whole((D, width)), whole((width, D))],
        [*rows, *dy, w_in, w_out],
        10 * count * len(rows) * D * width,
    )


def flat_plan(experts):
    shapes = [(PIX, D)] + [(D, 3 * D)] * 3 + [(D, D)] * 3 + [(D, FF)] * 2 + [(FF, D)] * 2
    plan, start = [], 0
    for height, width in shapes:
        plan.append((start, height, width // 128))
        start += height * width // 128
    return (plan, start)


def owner_rows(shard, parts):
    return -(-((shard + 127 + 127) // 128) // (16 * parts)) * 16 * parts


def chunk_of(rows, most=128):
    return max(c for c in range(16, most + 1, 16) if rows % c == 0)


def unpack_kernel(plan, shard, owners, orders, place_ref, *refs):
    chains = len(orders)
    own, other = (refs[:chains], refs[chains : 2 * chains])
    refs = refs[2 * chains :]
    outs, rest, flat = (refs[: len(plan)], refs[len(plan)], refs[len(plan) + 1])
    sizes = [ref.shape[0] // owners for ref in own]
    mine, core = (place_ref[0], place_ref[1])

    def collect(owner, carry):
        first = shard * owner // 128
        last = flat[pl.ds(jnp.maximum(first, 0), 1), :]
        shared = jnp.where(lax.rem(shard * owner, 128) == 0, 0.0, 1.0)
        for half in (0, 1):
            for chain, order in enumerate(orders):
                away = jnp.bitwise_xor(mine, owner)
                slot = sum(
                    jnp.bitwise_and(away // bit, 1) * 2**k for k, bit in enumerate(order)
                )
                size, before = (sizes[chain], half * sum(sizes) + sum(sizes[:chain]))
                source = pl.ds(pl.multiple_of(slot * size, 16), size)
                target = pl.ds(first + before, size)
                for ref, wanted in ((own[chain], core == half), (other[chain], core != half)):

                    @pl.when(wanted)
                    def _(ref=ref, source=source, target=target):
                        flat[target, :] = ref[source, :].astype(FULLTYPE)

        flat[pl.ds(first, 1), :] += last * shared
        return carry

    flat[0:8, :] = jnp.zeros((8, 128), FULLTYPE)
    lax.fori_loop(0, owners, collect, 0)
    spread_flat(plan, flat, outs, rest)


def unpack_parts_kernel(plan, shard, parts_ref, *refs):
    outs, rest, flat = (refs[: len(plan)], refs[len(plan)], refs[len(plan) + 1])
    owners, rows = parts_ref.shape[:2]
    chunk = chunk_of(rows)
    for owner in range(owners):
        first = shard * owner // 128
        if owner:
            last = flat[pl.ds(first, 1), :]

        def copy(i, carry, owner=owner, first=first):
            flat[pl.ds(first + i * chunk, chunk), :] = parts_ref[
                owner, pl.ds(pl.multiple_of(i * chunk, chunk), chunk), :
            ].astype(FULLTYPE)
            return carry

        lax.fori_loop(0, rows // chunk, copy, 0)
        if owner and shard * owner % 128:
            flat[pl.ds(first, 1), :] += last
    spread_flat(plan, flat, outs, rest)


def spread_flat(plan, flat, outs, rest):
    for (start, height, across), out in zip(plan, outs):

        def place(i, carry, start=start, across=across, out=out):
            for c in range(across):
                taken = flat[pl.ds(start + i * 128 * across + c, 128, stride=across), :]
                out[rows_of(i, 128), pl.ds(c * 128, 128)] = taken.astype(LOWTYPE)
            return carry

        lax.fori_loop(0, height // 128, place, 0)
    start = plan[-1][0] + plan[-1][1] * plan[-1][2]
    rest[...] = flat[pl.ds(start, rest.shape[0]), :]


ORDERS = ((4, 8, 1, 2), (4, 8, 2, 1))


def chain_sizes(rows):
    units = rows // 16
    return [16 * (units // 2), 16 * (units - units // 2)]


def gather_weights(part, shard, ep_place, dp_place, experts, beside):
    plan, start = flat_plan(experts)
    owners, groups = (lax.axis_size("ep"), lax.axis_size("dp"))
    rows = owner_rows(shard, groups)
    outs = [shaped((height, across * 128), LOWTYPE) for _, height, across in plan]
    outs.append(shaped((shard * owners // 128 - start, 128), FULLTYPE))
    flat = pltpu.VMEM((-(-(shard * (owners - 1) // 128 + rows) // 8) * 8, 128), FULLTYPE)
    if (owners, groups) != (16, 2) or part.shape[0] < 32:
        parts = lax.all_gather(part, ("ep", "dp")).reshape(owners, rows, 128)
        kernel, args = (functools.partial(unpack_parts_kernel, plan, shard), [parts])
        return (local_call(kernel, outs, args, 0, [flat]), beside[0](*beside[1]))
    sizes = chain_sizes(part.shape[0])
    chains = [part[sum(sizes[:c]) : sum(sizes[: c + 1])] for c in range(len(ORDERS))]
    work, inputs = beside
    for step in range(len(ORDERS[0])):
        got = [
            lax.ppermute(v, "ep", [(i, i ^ order[step]) for i in range(owners)])
            for v, order in zip(chains, ORDERS)
        ]
        if step == len(ORDERS[0]) - 2:
            got, inputs = lax.optimization_barrier((got, inputs))
        elif step == len(ORDERS[0]) - 1:
            got, results = lax.optimization_barrier((got, work(*inputs)))
        else:
            got = lax.optimization_barrier(got)
        chains = [jnp.concatenate([v, g]) for v, g in zip(chains, got)]
    args = [jnp.stack([ep_place, dp_place]).astype(jnp.int32), *chains, *map(swap_dp, chains)]
    moved = sum(math.prod(a.shape) * a.dtype.itemsize for a in (*args, *outs))
    mats = pl.pallas_call(
        functools.partial(unpack_kernel, plan, shard, owners, ORDERS),
        out_shape=outs,
        in_specs=[SCALARS] + in_vmem(len(args) - 1),
        out_specs=in_vmem(len(outs)),
        scratch_shapes=[flat],
        compiler_params=pltpu.CompilerParams(vmem_limit_bytes=VMEM_LIMIT),
        cost_estimate=pl.CostEstimate(flops=0, bytes_accessed=moved, transcendentals=0),
    )(*args)
    return (mats, results)


def pack_kernel(plan, shard, select, place_ref, *refs):
    count = len(plan)
    mats, rest, norms = (refs[:count], refs[count], refs[count + 1 : count + 5])
    outs, flat = (refs[count + 5 : -1], refs[-1])
    for (start, height, across), mat in zip(plan, mats):

        def place(i, carry, start=start, across=across, mat=mat):
            for c in range(across):
                flat[pl.ds(start + i * 128 * across + c, 128, stride=across), :] = mat[
                    rows_of(i, 128), pl.ds(c * 128, 128)
                ]
            return carry

        lax.fori_loop(0, height // 128, place, 0)
    start = plan[-1][0] + plan[-1][1] * plan[-1][2]
    flat[pl.ds(start, rest.shape[0]), :] = rest[...]
    start += rest.shape[0]
    for kind in (0, 1):
        for layer, norm in enumerate(norms):
            for k in range(2 if layer < 3 else 1):
                for c in range(D // 128):
                    row = start + ((7 * kind + 2 * layer + k) * D) // 128 + c
                    flat[row : row + 1, :] = norm[2 * k + kind : 2 * k + kind + 1, c * 128 : c * 128 + 128]
    for out, which in zip(outs, select):
        groups, owners, rows = out.shape[:3]
        chunk = chunk_of(rows)
        for group in range(groups):
            for owner in range(owners):
                member = which(place_ref[0], group)
                first = shard * owner // 128 + member * rows

                def copy(i, carry, out=out, group=group, owner=owner, first=first):
                    out[group, owner, pl.ds(pl.multiple_of(i * chunk, chunk), chunk), :] = flat[
                        pl.ds(first + i * chunk, chunk), :
                    ].astype(out.dtype)
                    return carry

                lax.fori_loop(0, rows // chunk, copy, 0)


def pack_gradients(mats, rest, norms, shard, owners, groups, place, experts):
    plan, _ = flat_plan(experts)
    rows = owner_rows(shard, groups)
    part = rows // groups
    if groups == 2:
        outs = [shaped((1, owners, part, 128), t) for t in (FULLTYPE, EXCHANGE)]
        select = [lambda here, g: here, lambda here, g: 1 - here]
    else:
        outs = [shaped((groups, owners, part, 128), FULLTYPE)]
        select = [lambda here, g: g]
    flat = pltpu.VMEM((-(-(shard * (owners - 1) // 128 + rows) // 8) * 8, 128), FULLTYPE)
    args = [place.reshape(1), *mats, rest, *norms]
    moved = sum(math.prod(a.shape) * a.dtype.itemsize for a in (*args, *outs))
    return pl.pallas_call(
        functools.partial(pack_kernel, plan, shard, select),
        out_shape=outs,
        in_specs=[SCALARS] + in_vmem(len(args) - 1),
        out_specs=in_vmem(len(outs)),
        scratch_shapes=[flat],
        compiler_params=pltpu.CompilerParams(vmem_limit_bytes=PACK_LIMIT),
        cost_estimate=pl.CostEstimate(flops=0, bytes_accessed=moved, transcendentals=0),
    )(*args)


EXCHANGE = jnp.bfloat16
PACK_LIMIT = 60 * 2**20


def swap_dp(value):
    return lax.ppermute(value, "dp", [(0, 1), (1, 0)])


def join_dp(value, place):
    groups = lax.axis_size("dp")
    if groups != 2:
        return lax.all_gather(value, "dp")
    other = swap_dp(value)
    first = place == 0
    return jnp.stack([jnp.where(first, value, other), jnp.where(first, other, value)])


def sum_scatter_dp(parts, place):
    groups = lax.axis_size("dp")
    if groups != 2:
        return lax.psum_scatter(parts, "dp", scatter_dimension=0, tiled=True)[0]
    first = place == 0
    mine = jnp.where(first, parts[0], parts[1])
    return mine + swap_dp(jnp.where(first, parts[1], parts[0]))


def sum_all(value):
    for axis in ("dp", "ep"):
        count = lax.axis_size(axis)
        step = 1
        while step < count:
            value = value + lax.ppermute(value, axis, [(i, i ^ step) for i in range(count)])
            step *= 2
    return value


def to_experts(buffer):
    return lax.all_to_all(buffer, "ep", split_axis=0, concat_axis=0, tiled=True)


def per_device(
    patches,
    labels,
    pixel_mask,
    patch_valid,
    tasks,
    routes,
    dense_weight,
    dense_first,
    dense_second,
    dense_average,
    expert_in,
    in_first,
    in_second,
    in_average,
    expert_out,
    out_first,
    out_second,
    out_average,
):
    ep_count = lax.axis_size("ep")
    experts = min(16, ep_count)
    copies = ep_count // experts
    groups = lax.axis_size("dp")
    ep_place = lax.axis_index("ep")
    dp_place = lax.axis_index("dp")
    own_expert = ep_place // copies
    seq = patches.shape[0]
    capacity = 3 * seq * TOP // (2 * experts)
    shard = dense_weight.shape[0]
    piece = shard // groups
    edges = segment_edges(experts)
    block_count = len(edges) + 1 + 2 * experts
    span, firsts = owner_blocks(edges, shard, ep_count)
    first_block = firsts[ep_place]
    starts = [
        jnp.take(jnp.array([0] + edges + [shard * ep_count] * span, jnp.int32), first_block + k)
        - ep_place * shard
        for k in range(span + 1)
    ]

    def placed(value, at, count):
        return jnp.where(jnp.arange(count) == at, value, 0.0)

    def block_sums(dense_vals, in_vals, out_vals):
        part = lax.dynamic_slice_in_dim(dense_vals, dp_place * piece, piece)
        square = part * part
        index = dp_place * piece + jnp.arange(piece, dtype=jnp.int32)
        listed = placed(jnp.sum(in_vals * in_vals), len(edges) + 1 + own_expert, block_count)
        listed += placed(
            jnp.sum(out_vals * out_vals), len(edges) + 1 + experts + own_expert, block_count
        )
        for k in range(span):
            inside = (index >= starts[k]) & (index < starts[k + 1])
            listed += placed(jnp.sum(jnp.where(inside, square, 0.0)), first_block + k, block_count)
        return listed

    rows = owner_rows(shard, groups)
    offset = lax.rem(ep_place * (shard % 128), 128)
    spread = lax.dynamic_update_slice(
        jnp.zeros((rows * 128,), LOWTYPE), dense_weight.astype(LOWTYPE), (offset,)
    )
    own_part = lax.dynamic_index_in_dim(
        spread.reshape(groups, rows // groups, 128), dp_place, 0, keepdims=False
    )
    low_in, low_out = (expert_in[0].astype(LOWTYPE), expert_out[0].astype(LOWTYPE))
    all_in = lax.all_gather(low_in, ("ep", "dp"))
    all_out = lax.all_gather(low_out, ("ep", "dp"))
    width = low_in.shape[1]
    w_out = all_out.reshape(experts, copies * groups * width, D)

    together = lax.optimization_barrier

    def prepare(labels, pixel_mask, patch_valid, routes, weights):
        named = jnp.sum(
            (routes[:, :, None] == jnp.arange(experts, dtype=jnp.int32)[None, None, :]).astype(FULLTYPE),
            1,
        )
        earlier = jnp.arange(seq)[:, None] > jnp.arange(seq)[None, :]
        table = jnp.where(named > 0, plain(earlier.astype(LOWTYPE), named.astype(LOWTYPE)), -1.0)
        weight_pix = (pixel_mask * patch_valid[:, None]).astype(FULLTYPE)
        class_hot = labels[:, :, None] == jnp.arange(C, dtype=jnp.int32)[None, None, :]
        return (
            table,
            table.T.reshape(experts, 1, seq),
            jnp.sum(named, 0).astype(jnp.int32),
            jnp.where(patch_valid > 0, 0.0, NEG).astype(FULLTYPE).reshape(seq, 1),
            jnp.sum(weight_pix, 1),
            jnp.sum(jnp.where(class_hot, weight_pix[:, :, None], 0.0), 1),
            block_sums(*weights),
        )

    (*mats, rest), prepared = gather_weights(
        own_part,
        shard,
        ep_place,
        dp_place,
        experts,
        (
            prepare,
            (labels, pixel_mask, patch_valid, routes, (dense_weight, expert_in, expert_out)),
        ),
    )
    table, place, loads, down, count_tok, counts, weight_sums = prepared
    first_block, starts, table = together((first_block, starts, table))
    steps = [(axis, 2**k) for axis in ("dp", "ep") for k in range(lax.axis_size(axis).bit_length() - 1)]
    fourth = -(-len(steps) // 4)

    def add_steps(value, turn):
        for axis, step in steps[turn * fourth : (turn + 1) * fourth]:
            count = lax.axis_size(axis)
            value = value + lax.ppermute(value, axis, [(i, i ^ step) for i in range(count)])
        return value

    total = add_steps(jnp.sum(count_tok).reshape(1), 0)
    w_patch, w_qkv, w_attn = (mats[0], mats[1:4], mats[4:7])
    w_up, w_down = (mats[7:9], mats[9:11])
    router_rows, head_rows = (TASKS * D * experts // 128, D * C // 128)
    w_router = rest[:router_rows].reshape(TASKS, D, experts).astype(LOWTYPE)
    w_head = rest[router_rows : router_rows + head_rows].reshape(D, C).astype(LOWTYPE)
    norms = rest[router_rows + head_rows :].reshape(2, 7, D)
    task = tasks[0]
    router = lax.dynamic_index_in_dim(w_router, task, 0, keepdims=False)

    def dispatch(send):
        return to_experts(jnp.repeat(send, copies, axis=0)).reshape(-1, D)

    together = lax.optimization_barrier

    def norm_rows(layer):
        rows = [norms[0, 2 * layer], norms[1, 2 * layer]]
        if layer < 3:
            rows += [norms[0, 2 * layer + 1], norms[1, 2 * layer + 1]]
        return jnp.pad(jnp.stack(rows), ((0, 8 - len(rows)), (0, 0)))

    x0, *kept0, x1, act0, slope0 = layer_forward(
        patches, w_patch, w_qkv[0], w_attn[0], norm_rows(0), down, w_up[0], w_down[0]
    )
    x1, all_in, total = together((x1, all_in, total))
    total = add_steps(total, 1)
    mid1, c16, *kept1 = layer_forward(
        x1, None, w_qkv[1], w_attn[1], norm_rows(1), down, None, None
    )
    c16, total = together((c16, total))
    total = add_steps(total, 2)
    w_in = all_in.reshape(experts, copies * groups, D, width)
    if width % 128:
        w_in = jnp.swapaxes(w_in, 1, 2).reshape(experts, 1, D, copies * groups * width)
    gates, spread_place, spread_gate, act1, slope1, *sent = moe_up(
        loads, c16, router, table, place, w_in, capacity
    )
    x2, taken = moe_down(loads, mid1, spread_place, spread_gate, act1, w_out)
    x2, sent, total = together((x2, sent, total))
    total = add_steps(total, 3)
    rows_a = dispatch(sent[0])
    *kept2, x3, act2, slope2 = layer_forward(
        x2, None, w_qkv[2], w_attn[2], norm_rows(2), down, w_up[1], w_down[1]
    )
    loss_lanes, d_head, d_normf, grad = head_call(
        x3, norm_rows(3), w_head, counts, count_tok, total
    )
    local = loss_lanes[0, 0]
    grad, local, sent, rows_a = together((grad, local, sent, rows_a))
    rows_b = dispatch(sent[1])
    d_qkv2, d_attn2, d_norm2, d_up1, d_down1, grad = layer_backward(
        grad, x2, (*kept2, act2, slope2), w_qkv[2], w_attn[2], norm_rows(2), down,
        (w_up[1], w_down[1]), None, None,
    )
    grad, sent, rows_b = together((grad, sent, rows_b))
    rows_c = dispatch(sent[2])
    d_own_router, d_c, *dy16 = moe_gate_backward(
        loads, grad, c16, router, gates, place, spread_gate, taken, capacity
    )
    d_c, dy16, rows_c = together((d_c, dy16, rows_c))
    dy_a = dispatch(dy16[0])
    d_c = moe_backward(loads, d_c, spread_place, w_in, w_out, dy16, slope1)
    d_c, dy16, dy_a = together((d_c, dy16, dy_a))
    dy_b = dispatch(dy16[1])
    task_hot = (jnp.arange(TASKS, dtype=jnp.int32) == task)[:, None, None]
    d_router = jnp.where(task_hot, d_own_router[None], 0.0)
    d_qkv1, d_attn1, d_norm1, grad = layer_backward(
        grad, x1, (mid1, c16, *kept1), w_qkv[1], w_attn[1], norm_rows(1), down, None, d_c, None
    )
    grad, dy16, dy_b = together((grad, dy16, dy_b))
    dy_c = dispatch(dy16[2])
    d_qkv0, d_attn0, d_norm0, d_up0, d_down0, d_patch = layer_backward(
        grad, x0, (*kept0, act0, slope0), w_qkv[0], w_attn[0], norm_rows(0), down,
        (w_up[0], w_down[0]), None, patches,
    )
    d_patch, dy_c = together((d_patch, dy_c))
    expert_rows, expert_dy = ([rows_a, rows_b, rows_c], [dy_a, dy_b, dy_c])
    d_rest = jnp.concatenate(
        [
            d_router.reshape(router_rows, 128),
            d_head[:, :C].reshape(head_rows, 128),
        ]
    )
    packed = pack_gradients(
        [d_patch, d_qkv0, d_qkv1, d_qkv2, d_attn0, d_attn1, d_attn2, d_up0, d_up1, d_down0, d_down1],
        d_rest, [d_norm0, d_norm1, d_norm2, d_normf], shard, ep_count, groups, dp_place, experts,
    )
    if groups == 2:
        summed = packed[0][0] + swap_dp(packed[1][0]).astype(FULLTYPE)
    else:
        summed = lax.psum_scatter(packed[0], "dp", scatter_dimension=0, tiled=True)[0]
    arrived = to_experts(summed.astype(LOWTYPE))

    own_in = lax.dynamic_index_in_dim(
        all_in.reshape(ep_count, groups, D, width), ep_place, 0, keepdims=False
    )
    own_out = lax.dynamic_index_in_dim(
        all_out.reshape(ep_count, groups, width, D), ep_place, 0, keepdims=False
    )
    if groups == 2:

        def weight_grads(member):
            return moe_weight_backward(
                expert_rows,
                expert_dy,
                lax.dynamic_index_in_dim(own_in, member, 0, keepdims=False),
                lax.dynamic_index_in_dim(own_out, member, 0, keepdims=False),
            )

        theirs = weight_grads(1 - dp_place)
        away = [swap_dp(t.astype(jnp.bfloat16)) for t in theirs]
        mine = weight_grads(dp_place)
        mine, away, arrived = together((mine, away, arrived))
        d_in, d_out = [(m + t.astype(FULLTYPE))[None] for m, t in zip(mine, away)]
    else:
        d_in, d_out = moe_weight_backward(
            expert_rows,
            expert_dy,
            jnp.swapaxes(own_in, 0, 1).reshape(D, groups * width),
            own_out.reshape(groups * width, D),
        )
        d_in, d_out = (
            lax.psum_scatter(
                value[None].astype(jnp.bfloat16), "dp", scatter_dimension=axis, tiled=True
            ).astype(FULLTYPE)
            for value, axis in ((d_in, 2), (d_out, 1))
        )
    own_sum = jnp.sum(arrived.astype(FULLTYPE), 0)
    dense_grad = lax.dynamic_slice_in_dim(
        join_dp(own_sum, dp_place).reshape(-1), offset, shard
    )
    own_grad = lax.dynamic_slice_in_dim(dense_grad, dp_place * piece, piece)
    sums = sum_all(
        together(placed(local, 0, 2 + block_count)
        + placed(jnp.sum(own_grad * own_grad) + jnp.sum(d_in * d_in) + jnp.sum(d_out * d_out), 1, 2 + block_count)
        + jnp.pad(weight_sums, (2, 0)))
    )
    loss, grad_total, weight_total = (sums[0] / total, sums[1], sums[2:])
    grad_norm = jnp.sqrt(grad_total)
    clip = CLIP_NORM / jnp.maximum(grad_norm, CLIP_NORM)

    def moments(weight, first, second, gradient):
        gradient = gradient * clip
        first_new = DECAY_ONE * first + (1.0 - DECAY_ONE) * gradient
        second_new = DECAY_TWO * second + (1.0 - DECAY_TWO) * gradient * gradient
        return (
            first_new,
            second_new,
            first_new / (jnp.sqrt(second_new) + EPS_ADAM) + WEIGHT_DECAY * weight,
        )

    dense_m, dense_v, dense_step = moments(dense_weight, dense_first, dense_second, dense_grad)
    in_m, in_v, in_step = moments(expert_in, in_first, in_second, d_in)
    out_m, out_v, out_step = moments(expert_out, out_first, out_second, d_out)
    update_total = sum_all(together(block_sums(dense_step, in_step, out_step)))
    weight_norm = jnp.sqrt(weight_total)
    update_norm = jnp.sqrt(update_total)
    ratio = weight_norm / (update_norm + EPS_NORM)
    whole_index = jnp.arange(shard, dtype=jnp.int32)
    dense_ratio = jnp.broadcast_to(jnp.take(ratio, first_block), (shard,))
    for k in range(1, span):
        dense_ratio = jnp.where(whole_index >= starts[k], jnp.take(ratio, jnp.minimum(first_block + k, block_count - 1)), dense_ratio)
    in_ratio = lax.dynamic_index_in_dim(ratio, 14 + own_expert, 0, keepdims=False)
    out_ratio = lax.dynamic_index_in_dim(ratio, 14 + experts + own_expert, 0, keepdims=False)

    def finish(weight, average, step, rate):
        new = weight - RATE * rate * step
        return (new, AVERAGE * average + (1.0 - AVERAGE) * new, new.astype(LOWTYPE))

    dense_new, dense_avg, dense_low = finish(dense_weight, dense_average, dense_step, dense_ratio)
    in_new, in_avg, in_low = finish(expert_in, in_average, in_step, in_ratio)
    out_new, out_avg, out_low = finish(expert_out, out_average, out_step, out_ratio)
    block_norms = jnp.stack([weight_norm, update_norm], 1)
    return (
        loss.reshape(1),
        grad_norm.reshape(1),
        block_norms,
        dense_new,
        dense_m,
        dense_v,
        dense_avg,
        dense_low,
        in_new,
        in_m,
        in_v,
        in_avg,
        in_low,
        out_new,
        out_m,
        out_v,
        out_avg,
        out_low,
    )


def solution(mesh):
    in_specs = (
        P(("ep", "dp"), None),
        P(("ep", "dp"), None),
        P(("ep", "dp"), None),
        P(("ep", "dp")),
        P(("ep", "dp")),
        P(("ep", "dp"), None),
        P("ep"),
        P("ep"),
        P("ep"),
        P("ep"),
        P("ep", None, "dp"),
        P("ep", None, "dp"),
        P("ep", None, "dp"),
        P("ep", None, "dp"),
        P("ep", "dp", None),
        P("ep", "dp", None),
        P("ep", "dp", None),
        P("ep", "dp", None),
    )
    out_specs = (
        P(),
        P(),
        P(),
        P("ep"),
        P("ep"),
        P("ep"),
        P("ep"),
        P("ep"),
        P("ep", None, "dp"),
        P("ep", None, "dp"),
        P("ep", None, "dp"),
        P("ep", None, "dp"),
        P("ep", None, "dp"),
        P("ep", "dp", None),
        P("ep", "dp", None),
        P("ep", "dp", None),
        P("ep", "dp", None),
        P("ep", "dp", None),
    )
    return jax.shard_map(
        per_device, mesh=mesh, in_specs=in_specs, out_specs=out_specs, check_vma=False
    )
```

```python
import functools
import math

import jax
import jax.numpy as jnp
from jax import lax
from jax.experimental import pallas as pl
from jax.experimental.pallas import tpu as pltpu
from jax.sharding import PartitionSpec as P

D = 384
HEADS = 6
HD = 64
FF = 1536
TOP = 4
C = 40
PIX = 768
TASKS = 4


EPS_NORM = 1e-05
CLIP_NORM = 0.002
RATE = 0.3
DECAY_ONE = 0.5
DECAY_TWO = 0.5
WEIGHT_DECAY = 0.01
EPS_ADAM = 1e-09
AVERAGE = 0.9
SCALE = 0.125
LOWTYPE = jnp.bfloat16
FULLTYPE = jnp.float32


def plain(left, right):
    return jnp.dot(left, right, preferred_element_type=FULLTYPE)


def left_t(left, right):
    return lax.dot_general(left, right, (((0,), (0,)), ((), ())), preferred_element_type=FULLTYPE)


def right_t(left, right):
    return lax.dot_general(left, right, (((1,), (1,)), ((), ())), preferred_element_type=FULLTYPE)


def segment_sizes(experts):
    return (
        [PIX * D]
        + [3 * D * D] * 3
        + [D * D] * 3
        + [D * FF] * 2
        + [FF * D] * 2
        + [TASKS * D * experts, D * C, 14 * D]
    )


def owner_blocks(edges, shard, owners):
    firsts = [sum(edge <= shard * i for edge in edges) for i in range(owners)]
    lasts = [sum(edge < shard * (i + 1) for edge in edges) for i in range(owners)]
    span = max(b - a + 1 for a, b in zip(firsts, lasts))
    return (span, jnp.array(firsts, jnp.int32))


def segment_edges(experts):
    edges, edge = [], 0
    for size in segment_sizes(experts)[:-1]:
        edge += size
        edges.append(edge)
    return edges


VMEM_LIMIT = 56 * 2**20
ROWS = 512
TILE = 32
KEYS = 64
QUERIES = 512
NEG = -1e30


def rows_of(index, size=ROWS):
    return pl.ds(pl.multiple_of(index * size, size), size)


def norm_parts(x):
    cent = x - jnp.mean(x, -1, keepdims=True)
    scale = lax.rsqrt(jnp.mean(cent * cent, -1, keepdims=True) + EPS_NORM)
    return (cent * scale, scale)


def norm_low(x, gain, bias):
    return (norm_parts(x)[0] * gain + bias).astype(LOWTYPE)


def norm_pull(x, gain, grad):
    unit, scale = norm_parts(x)
    inner = grad * gain
    d_x = scale * (
        inner
        - jnp.mean(inner, -1, keepdims=True)
        - unit * jnp.mean(inner * unit, -1, keepdims=True)
    )
    return (d_x, jnp.sum(grad * unit, 0, keepdims=True), jnp.sum(grad, 0, keepdims=True))


def gelu_pair(h):
    cdf = 0.5 + 0.5 * lax.erf(h * 0.7071067811865476)
    e = jnp.exp((h * h) * -0.5)
    return (h * cdf, cdf + h * (e * 0.3989422804014327))


def half_masks(scale):
    lane = lax.broadcasted_iota(jnp.int32, (1, 128), 1)
    return [jnp.where((lane < HD) == (h == 0), scale, 0.0).astype(LOWTYPE) for h in (0, 1)]


def beside_head(head, own, extras):
    lane = lax.broadcasted_iota(jnp.int32, own.shape, 1)
    value = own.astype(FULLTYPE) * half_masks(1.0)[head].astype(FULLTYPE)
    for k, extra in enumerate(extras):
        value = jnp.where(lane == HD * (1 - head) + k, extra, value)
    return value.astype(LOWTYPE)


def three_parts(column):
    high = column.astype(LOWTYPE).astype(FULLTYPE)
    middle = (column - high).astype(LOWTYPE).astype(FULLTYPE)
    return [high, middle, column - high - middle]


def attend_rows(qkv_ref, bias_ref, o_ref, aug_ref, keys_ref, s_ref, p_ref):
    seq = qkv_ref.shape[0]
    masks = half_masks(SCALE)
    lane = lax.broadcasted_iota(jnp.int32, (ROWS, 128), 1)

    for pair in range(HEADS // 2):
        cols = pl.ds(pair * 128, 128)

        def prepare(i, carry, pair=pair):
            rows = rows_of(i)
            keys = qkv_ref[rows, pl.ds(D + pair * 128, 128)]
            for h in (0, 1):
                keys_ref[h, rows, :] = beside_head(h, keys, [bias_ref[rows, :]])
            return carry

        lax.fori_loop(0, seq // ROWS, prepare, 0)

        def body(i, carry, pair=pair, cols=cols):
            rows = rows_of(i)
            query = qkv_ref[rows, cols]
            values = qkv_ref[:, pl.ds(2 * D + pair * 128, 128)]
            outs = []
            for h in (0, 1):
                s_ref[h] = right_t(beside_head(h, query * masks[h], [1.0]), keys_ref[h])
            for h in (0, 1):
                for first in range(0, ROWS, TILE):
                    s = s_ref[h, first : first + TILE, :]
                    top = jnp.max(s, -1, keepdims=True)
                    e = jnp.exp(s - top)
                    total = jnp.sum(e, -1, keepdims=True)
                    p_ref[h, first : first + TILE, :] = (e * (1.0 / total)).astype(LOWTYPE)
                    at = pl.ds(pl.multiple_of(i * ROWS + first, TILE), TILE)
                    aug_ref[at, pl.ds((2 * pair + h) * 128, 128)] = beside_head(
                        h,
                        query[first : first + TILE] * masks[h],
                        [1.0] + three_parts(-(top + jnp.log(total))),
                    )
            for h in (0, 1):
                outs.append(plain(p_ref[h], values))
            o_ref[rows, cols] = jnp.where(lane < HD, outs[0], outs[1]).astype(LOWTYPE)
            return carry

        lax.fori_loop(0, seq // ROWS, body, 0)


def forward_kernel(has_patch, has_ff, *refs):
    refs = list(refs)
    x_in = refs.pop(0)
    if has_patch:
        w_patch = refs.pop(0)
    w_qkv, w_attn, norms, bias = refs[:4]
    refs = refs[4:]
    if has_ff:
        w_up, w_down = refs[:2]
        refs = refs[2:]
    if has_patch:
        x_ref = refs.pop(0)
    else:
        x_ref = x_in
    mid_ref, c_ref, qkv_ref, o_ref, aug_ref = refs[:5]
    refs = refs[5:]
    if has_ff:
        next_ref, act_ref, slope_ref = refs[:3]
    keys_ref, s_ref, p_ref = refs[-3:]
    seq = x_ref.shape[0]

    def project(i, carry):
        rows = rows_of(i)
        if has_patch:
            x_ref[rows, :] = plain(x_in[rows, :], w_patch[...])
        a16 = norm_low(x_ref[rows, :], norms[0:1, :], norms[1:2, :])
        qkv_ref[rows, :] = plain(a16, w_qkv[...]).astype(LOWTYPE)
        return carry

    lax.fori_loop(0, seq // ROWS, project, 0)
    attend_rows(qkv_ref, bias, o_ref, aug_ref, keys_ref, s_ref, p_ref)

    def finish(i, carry):
        rows = rows_of(i)
        mid = x_ref[rows, :] + plain(o_ref[rows, :], w_attn[...])
        mid_ref[rows, :] = mid
        c16 = norm_low(mid, norms[2:3, :], norms[3:4, :])
        c_ref[rows, :] = c16
        if has_ff:
            act, slope = gelu_pair(plain(c16, w_up[...]))
            act16 = act.astype(LOWTYPE)
            act_ref[rows, :] = act16
            slope_ref[rows, :] = slope
            next_ref[rows, :] = mid + plain(act16, w_down[...])
        return carry

    lax.fori_loop(0, seq // ROWS, finish, 0)


def in_vmem(count):
    return [pl.BlockSpec(memory_space=pltpu.VMEM)] * count


def local_call(kernel, outs, args, flops, scratch=()):
    moved = sum(math.prod(a.shape) * a.dtype.itemsize for a in (*args, *outs))
    return pl.pallas_call(
        kernel,
        out_shape=outs,
        in_specs=in_vmem(len(args)),
        out_specs=in_vmem(len(outs)),
        scratch_shapes=scratch,
        compiler_params=pltpu.CompilerParams(vmem_limit_bytes=VMEM_LIMIT),
        cost_estimate=pl.CostEstimate(flops=flops, bytes_accessed=moved, transcendentals=0),
    )(*args)


def shaped(shape, dtype):
    return jax.ShapeDtypeStruct(shape, dtype)


def layer_forward(x, w_patch, w_qkv, w_attn, norms, bias, w_up, w_down):
    seq = x.shape[0]
    has_patch, has_ff = (w_patch is not None, w_up is not None)
    args = [x] + [w_patch] * has_patch + [w_qkv, w_attn, norms, bias] + [w_up, w_down] * has_ff
    outs = [shaped((seq, D), FULLTYPE)] * has_patch
    outs += [
        shaped((seq, D), FULLTYPE),
        shaped((seq, D), LOWTYPE),
        shaped((seq, 3 * D), LOWTYPE),
        shaped((seq, D), LOWTYPE),
        shaped((seq, 128 * HEADS), LOWTYPE),
    ]
    if has_ff:
        outs += [
            shaped((seq, D), FULLTYPE),
            shaped((seq, FF), LOWTYPE),
            shaped((seq, FF), FULLTYPE),
        ]
    flops = 2 * seq * D * (4 * D + 4 * seq + 2 * FF * has_ff)
    kernel = functools.partial(forward_kernel, has_patch, has_ff)
    scratch = [
        pltpu.VMEM((2, seq, 128), LOWTYPE),
        pltpu.VMEM((2, ROWS, seq), FULLTYPE),
        pltpu.VMEM((2, ROWS, seq), LOWTYPE),
    ]
    return local_call(kernel, outs, args, flops, scratch)


def attend_pull(qkv_ref, o_ref, do_ref, aug_ref, valid_ref, dqkv_ref, dk_ref, dv_ref, sides):
    seq = qkv_ref.shape[0]
    keys_ref, values_ref, across_ref, s_ref, dp_ref, p_ref, ds_ref = sides
    ones = half_masks(1.0)

    for pair in range(HEADS // 2):
        cols = pl.ds(pair * 128, 128)
        dk_ref[...] = jnp.zeros_like(dk_ref)
        dv_ref[...] = jnp.zeros_like(dv_ref)

        def prepare(i, carry, pair=pair):
            rows = rows_of(i)
            keys = qkv_ref[rows, pl.ds(D + pair * 128, 128)]
            values = qkv_ref[rows, pl.ds(2 * D + pair * 128, 128)]
            across_ref[:, rows] = keys.astype(FULLTYPE).T.astype(LOWTYPE)
            for h in (0, 1):
                keys_ref[h, rows, :] = beside_head(h, keys, [valid_ref[rows, :], 1.0, 1.0, 1.0])
                values_ref[h, rows, :] = beside_head(h, values, [1.0, 1.0, 1.0])
            return carry

        lax.fori_loop(0, seq // ROWS, prepare, 0)

        def body(i, carry, pair=pair, cols=cols):
            rows = rows_of(i, QUERIES)
            d_out = do_ref[rows, cols]
            both = d_out.astype(FULLTYPE) * o_ref[rows, cols].astype(FULLTYPE)
            d_query = []
            for h in (0, 1):
                own_q = aug_ref[rows, pl.ds((2 * pair + h) * 128, 128)]
                s_ref[h] = right_t(keys_ref[h], own_q)
                delta = jnp.sum(both * ones[h].astype(FULLTYPE), -1, keepdims=True)
                own_d = beside_head(h, d_out, three_parts(-delta))
                dp_ref[h] = right_t(values_ref[h], own_d)
            for h in (0, 1):
                for first in range(0, seq, KEYS):
                    at, side = (pl.ds(first, KEYS), pl.ds(h * QUERIES, QUERIES))
                    probs = jnp.exp(s_ref[h, at, :])
                    p_ref[at, side] = probs.astype(LOWTYPE)
                    ds_ref[at, side] = (probs * dp_ref[h, at, :]).astype(LOWTYPE)
            own = [
                aug_ref[rows, pl.ds((2 * pair + h) * 128, 128)] * ones[h] for h in (0, 1)
            ]
            dv_ref[...] += plain(p_ref[...], jnp.concatenate([d_out * ones[h] for h in (0, 1)]))
            dk_ref[...] += plain(ds_ref[...], jnp.concatenate(own))
            for h in (0, 1):
                d_query.append(
                    plain(across_ref[pl.ds(h * HD, HD), :], ds_ref[:, pl.ds(h * QUERIES, QUERIES)])
                )
            turned = jnp.concatenate(d_query).T * SCALE
            dqkv_ref[rows, cols] = turned.astype(LOWTYPE)
            return carry

        lax.fori_loop(0, seq // QUERIES, body, 0)
        dqkv_ref[:, pl.ds(D + pair * 128, 128)] = dk_ref[...].astype(LOWTYPE)
        dqkv_ref[:, pl.ds(2 * D + pair * 128, 128)] = dv_ref[...].astype(LOWTYPE)


def weight_pull(left_ref, right_ref, out_ref, tile=384):
    def body(j, carry):
        cols = rows_of(j, tile)
        out_ref[cols, :] = left_t(left_ref[:, cols], right_ref[...])
        return carry

    lax.fori_loop(0, left_ref.shape[1] // tile, body, 0)


def backward_kernel(has_patch, has_ff, *refs):
    refs = list(refs)
    grad, x_ref, mid_ref, qkv, o_ref, aug, w_qkv, w_attn, norms, valid = refs[:10]
    refs = refs[10:]
    if has_ff:
        c_ref, act, slope, w_up, w_down = refs[:5]
        refs = refs[5:]
    else:
        d_c_ref = refs.pop(0)
    if has_patch:
        patches = refs.pop(0)
    d_qkvw, d_attn, d_norms = refs[:3]
    refs = refs[3:]
    if has_ff:
        d_up, d_down = refs[:2]
        refs = refs[2:]
    if has_patch:
        d_patch = refs.pop(0)
    else:
        dx_ref = refs.pop(0)
    gmid, low, do_ref, dqkv, dk, dv = refs[:6]
    sides, refs = (refs[6:13], refs[13:])
    if has_ff:
        dh_ref = refs.pop(0)
    seq = grad.shape[0]
    blocks_count = seq // ROWS
    d_norms[...] = jnp.zeros_like(d_norms)

    def feed(i, carry):
        rows = rows_of(i)
        g = grad[rows, :]
        if has_ff:
            g16 = g.astype(LOWTYPE)
            low[rows, :] = g16
            dh16 = (right_t(g16, w_down[...]) * slope[rows, :]).astype(LOWTYPE)
            dh_ref[rows, :] = dh16
            d_c = right_t(dh16, w_up[...])
        else:
            d_c = d_c_ref[rows, :]
        d_x, d_gain, d_bias = norm_pull(mid_ref[rows, :], norms[2:3, :], d_c)
        gmid[rows, :] = g + d_x
        d_norms[2:3, :] += d_gain
        d_norms[3:4, :] += d_bias
        return carry

    lax.fori_loop(0, blocks_count, feed, 0)
    if has_ff:
        weight_pull(act, low, d_down)
        weight_pull(c_ref, dh_ref, d_up)

    def out_pull(i, carry):
        rows = rows_of(i)
        g16 = gmid[rows, :].astype(LOWTYPE)
        low[rows, :] = g16
        do_ref[rows, :] = right_t(g16, w_attn[...]).astype(LOWTYPE)
        return carry

    lax.fori_loop(0, blocks_count, out_pull, 0)
    weight_pull(o_ref, low, d_attn)
    attend_pull(qkv, o_ref, do_ref, aug, valid, dqkv, dk, dv, sides)

    def in_pull(i, carry):
        rows = rows_of(i)
        d_a = right_t(dqkv[rows, :], w_qkv[...])
        x = x_ref[rows, :]
        d_x, d_gain, d_bias = norm_pull(x, norms[0:1, :], d_a)
        total = gmid[rows, :] + d_x
        if has_patch:
            gmid[rows, :] = total
        else:
            dx_ref[rows, :] = total
        low[rows, :] = norm_low(x, norms[0:1, :], norms[1:2, :])
        d_norms[0:1, :] += d_gain
        d_norms[1:2, :] += d_bias
        return carry

    lax.fori_loop(0, blocks_count, in_pull, 0)
    weight_pull(low, dqkv, d_qkvw)
    if has_patch:

        def lower(i, carry):
            rows = rows_of(i)
            low[rows, :] = gmid[rows, :].astype(LOWTYPE)
            return carry

        lax.fori_loop(0, blocks_count, lower, 0)
        weight_pull(patches, low, d_patch)


def layer_backward(grad, x, kept, w_qkv, w_attn, norms, valid, ff, d_c, patches):
    seq = grad.shape[0]
    mid, c16, qkv16, o16, aug = kept[:5]
    has_ff, has_patch = (ff is not None, patches is not None)
    args = [grad, x, mid, qkv16, o16, aug, w_qkv, w_attn, norms, valid]
    args += [c16, *kept[5:], *ff] if has_ff else [d_c]
    args += [patches] * has_patch
    outs = [
        shaped((D, 3 * D), FULLTYPE),
        shaped((D, D), FULLTYPE),
        shaped((8, D), FULLTYPE),
    ]
    if has_ff:
        outs += [shaped((D, FF), FULLTYPE), shaped((FF, D), FULLTYPE)]
    outs += [shaped((PIX, D), FULLTYPE) if has_patch else shaped((seq, D), FULLTYPE)]
    scratch = [
        pltpu.VMEM((seq, D), FULLTYPE),
        pltpu.VMEM((seq, D), LOWTYPE),
        pltpu.VMEM((seq, D), LOWTYPE),
        pltpu.VMEM((seq, 3 * D), LOWTYPE),
        pltpu.VMEM((seq, 128), FULLTYPE),
        pltpu.VMEM((seq, 128), FULLTYPE),
        pltpu.VMEM((2, seq, 128), LOWTYPE),
        pltpu.VMEM((2, seq, 128), LOWTYPE),
        pltpu.VMEM((128, seq), LOWTYPE),
        pltpu.VMEM((2, seq, QUERIES), FULLTYPE),
        pltpu.VMEM((2, seq, QUERIES), FULLTYPE),
        pltpu.VMEM((seq, 2 * QUERIES), LOWTYPE),
        pltpu.VMEM((seq, 2 * QUERIES), LOWTYPE),
    ] + [pltpu.VMEM((seq, FF), LOWTYPE)] * has_ff
    flops = 2 * seq * D * (8 * D + 10 * seq + 4 * FF * has_ff + PIX * has_patch)
    return local_call(
        functools.partial(backward_kernel, has_patch, has_ff), outs, args, flops, scratch
    )


def head_kernel(x_ref, norms, w_head, counts, count, total, loss, d_head, d_norms, grad, f_ref, dl_ref):
    seq = x_ref.shape[0]
    d_norms[...] = jnp.zeros_like(d_norms)
    loss[...] = jnp.zeros_like(loss)
    real = lax.broadcasted_iota(jnp.int32, (1, 128), 1) < C

    def body(i, carry):
        rows = rows_of(i)
        x = x_ref[rows, :]
        f16 = norm_low(x, norms[0:1, :], norms[1:2, :])
        f_ref[rows, :] = f16
        logits = plain(f16, w_head[...])
        shown = jnp.where(real, logits, NEG)
        top = jnp.max(shown, -1, keepdims=True)
        e = jnp.exp(shown - top)
        under = jnp.sum(e, -1, keepdims=True)
        weight = count[rows, :]
        classes = counts[rows, :]
        part = weight * (top + jnp.log(under)) - jnp.sum(classes * logits, -1, keepdims=True)
        loss[...] += jnp.broadcast_to(jnp.sum(part, 0, keepdims=True), loss.shape)
        d_logits = ((weight * (e * (1.0 / under)) - classes) / total[...]).astype(LOWTYPE)
        dl_ref[rows, :] = d_logits
        d_x, d_gain, d_bias = norm_pull(x, norms[0:1, :], right_t(d_logits, w_head[...]))
        grad[rows, :] = d_x
        d_norms[0:1, :] += d_gain
        d_norms[1:2, :] += d_bias
        return carry

    lax.fori_loop(0, seq // ROWS, body, 0)
    weight_pull(f_ref, dl_ref, d_head)


def head_call(x, norms, w_head, counts, count, total):
    seq = x.shape[0]
    outs = [
        shaped((1, 128), FULLTYPE),
        shaped((D, 128), FULLTYPE),
        shaped((8, D), FULLTYPE),
        shaped((seq, D), FULLTYPE),
    ]
    args = [
        x,
        norms,
        jnp.pad(w_head, ((0, 0), (0, 128 - C))),
        jnp.pad(counts, ((0, 0), (0, 128 - C))),
        count.reshape(seq, 1),
        total.reshape(1, 1),
    ]
    scratch = [pltpu.VMEM((seq, D), LOWTYPE), pltpu.VMEM((seq, 128), LOWTYPE)]
    return local_call(head_kernel, outs, args, 6 * seq * D * 128, scratch)


SLOTS = 128
WIDE = 1024


def by_load(load, capacity, work):
    for count in range(SLOTS, capacity + 1, SLOTS):
        inside = load > count - SLOTS if count > SLOTS else load >= 0
        if count < capacity:
            inside = inside & (load <= count)
        pl.when(inside)(functools.partial(work, count))


def slot_select(place, count):
    row = lax.broadcasted_iota(jnp.int32, (count, place.shape[1]), 0).astype(FULLTYPE)
    return jnp.where(place == row, 1.0, 0.0).astype(LOWTYPE)


def put_blocks(refs, rows):
    for block, ref in enumerate(refs):
        if block * SLOTS < rows.shape[0]:
            ref[0] = rows[block * SLOTS : (block + 1) * SLOTS]
        else:
            ref[0] = jnp.zeros(ref.shape[1:], ref.dtype)


def column_of(table, expert):
    lane = lax.broadcasted_iota(jnp.int32, table.shape, 1)
    return jnp.sum(jnp.where(lane == expert, table, 0.0), -1, keepdims=True)


def patch_select(spread, count):
    lane = lax.broadcasted_iota(jnp.int32, (1, 128), 1).astype(FULLTYPE)
    return jnp.concatenate(
        [
            jnp.where(spread == lane + first, 1.0, 0.0).astype(LOWTYPE)
            for first in range(0, count, 128)
        ],
        1,
    )


def moe_up_kernel(
    loads, c_ref, router, table, place, w_in,
    gates_ref, spread_place, spread_gate, act_ref, slope_ref, *rows_refs,
):
    expert = pl.program_id(0)
    seq, capacity, parts = (c_ref.shape[0], act_ref.shape[0], w_in.shape[1])
    width = w_in.shape[3]

    @pl.when(expert == 0)
    def _():
        def start(i, carry):
            rows = rows_of(i, WIDE)
            z = plain(c_ref[rows, :], router[...])
            named = table[rows, :] >= 0
            shown = jnp.where(named, z, NEG)
            e = jnp.where(named, jnp.exp(shown - jnp.max(shown, -1, keepdims=True)), 0.0)
            gates_ref[rows, :] = e / jnp.sum(e, -1, keepdims=True)
            return carry

        lax.fori_loop(0, seq // WIDE, start, 0)

    def fan(i, carry):
        rows = rows_of(i, WIDE)
        for source, out in ((table, spread_place), (gates_ref, spread_gate)):
            out[0, rows, :] = jnp.broadcast_to(column_of(source[rows, :], expert), (WIDE, 128))
        return carry

    lax.fori_loop(0, seq // WIDE, fan, 0)

    def work(count):
        at = pl.ds(0, count)
        rows = plain(slot_select(place[0], count), c_ref[...]).astype(LOWTYPE)
        put_blocks(rows_refs, rows)
        for part in range(parts):
            step = width // 3 if width % 384 == 0 else width
            for first in range(0, width, step):
                act, slope = gelu_pair(plain(rows, w_in[0, part, :, pl.ds(first, step)]))
                units = pl.ds(part * width + first, step)
                slope_ref[at, units] = slope
                act_ref[at, units] = act.astype(LOWTYPE)

    by_load(loads[expert], capacity, work)


def moe_down_kernel(loads, mid_ref, spread_place, spread_gate, act_ref, w_out, next_ref, taken_ref, y_ref):
    expert = pl.program_id(0)
    seq, capacity = (mid_ref.shape[0], act_ref.shape[0])

    @pl.when(expert == 0)
    def _():
        next_ref[...] = mid_ref[...]

    def work(count):
        at = pl.ds(0, count)
        y_ref[at, :] = plain(act_ref[at, :], w_out[0]).astype(LOWTYPE)

        def add(i, carry):
            rows = rows_of(i, WIDE)
            taken = plain(patch_select(spread_place[0, rows, :], count), y_ref[at, :])
            taken_ref[0, rows, :] = taken.astype(LOWTYPE)
            for first in range(0, D, 128):
                lanes = pl.ds(first, 128)
                next_ref[rows, lanes] += spread_gate[0, rows, :] * taken[:, first : first + 128]
            return carry

        lax.fori_loop(0, seq // WIDE, add, 0)

    by_load(loads[expert], capacity, work)


def moe_gate_kernel(
    loads, grad_ref, c_ref, router, gates, place, spread_gate, taken_ref,
    d_router, d_c, *refs,
):
    dy_refs, (low_ref, dz_ref, d_gates) = (refs[:-3], refs[-3:])
    expert = pl.program_id(0)
    seq, capacity = (grad_ref.shape[0], SLOTS * len(dy_refs))
    lane = lax.broadcasted_iota(jnp.int32, (WIDE, d_gates.shape[1]), 1)

    @pl.when(expert == 0)
    def _():
        d_gates[...] = jnp.zeros_like(d_gates)

    def work(count):
        def one(i, carry):
            rows = rows_of(i, WIDE)
            grad = grad_ref[rows, :]
            gate = spread_gate[0, rows, :]
            taken = taken_ref[0, rows, :].astype(FULLTYPE)
            d_gate = jnp.sum(grad * taken, -1, keepdims=True)
            d_gates[rows, :] += jnp.where(lane == expert, d_gate, 0.0)
            for first in range(0, D, 128):
                lanes = pl.ds(first, 128)
                low_ref[rows, lanes] = (gate * grad[:, first : first + 128]).astype(LOWTYPE)
            return carry

        lax.fori_loop(0, seq // WIDE, one, 0)
        put_blocks(dy_refs, plain(slot_select(place[0], count), low_ref[...]).astype(LOWTYPE))

    by_load(loads[expert], capacity, work)

    @pl.when(expert == pl.num_programs(0) - 1)
    def _():
        def last(i, carry):
            rows = rows_of(i, WIDE)
            gate = gates[rows, :]
            d_gate = d_gates[rows, :]
            d_z = gate * (d_gate - jnp.sum(gate * d_gate, -1, keepdims=True))
            dz_ref[rows, :] = d_z.astype(LOWTYPE)
            d_c[rows, :] = right_t(dz_ref[rows, :], router[...])
            return carry

        lax.fori_loop(0, seq // WIDE, last, 0)
        d_router[...] = left_t(c_ref[...], dz_ref[...])


def moe_backward_kernel(loads, start_ref, spread_place, w_in, w_out, slope_ref, *refs):
    dy_refs, (d_c, back_ref) = (refs[:-2], refs[-2:])
    expert = pl.program_id(0)
    seq, capacity, parts = (d_c.shape[0], slope_ref.shape[0], w_in.shape[1])
    width = w_in.shape[3]

    @pl.when(expert == 0)
    def _():
        d_c[...] = start_ref[...]

    def work(count):
        at = pl.ds(0, count)
        d_y = jnp.concatenate([ref[0] for ref in dy_refs[: count // SLOTS]])
        back = jnp.zeros((count, D), FULLTYPE)
        for part in range(parts):
            units = pl.ds(part * width, width)
            d_act = right_t(d_y, w_out[0, units, :])
            d_h = (d_act * slope_ref[at, units]).astype(LOWTYPE)
            back += right_t(d_h, w_in[0, part])
        back_ref[at, :] = back.astype(LOWTYPE)

        def add(i, carry):
            rows = rows_of(i, WIDE)
            d_c[rows, :] += plain(patch_select(spread_place[0, rows, :], count), back_ref[at, :])
            return carry

        lax.fori_loop(0, seq // WIDE, add, 0)

    by_load(loads[expert], capacity, work)


def moe_weight_kernel(count, *refs):
    rows_refs, dy_refs = (refs[:count], refs[count : 2 * count])
    w_in, w_out, d_in, d_out = refs[2 * count :]

    @pl.when(pl.program_id(0) == 0)
    def _():
        d_in[...] = jnp.zeros_like(d_in)
        d_out[...] = jnp.zeros_like(d_out)

    width = w_in.shape[1]
    step = 384 if width % 384 == 0 else width
    for rows_ref, dy_ref in zip(rows_refs, dy_refs):
        rows, d_y = (rows_ref[...], dy_ref[...])
        for first in range(0, width, step):
            units = pl.ds(first, step)
            act, slope = gelu_pair(plain(rows, w_in[:, units]))
            d_h = (right_t(d_y, w_out[units, :]) * slope).astype(LOWTYPE)
            d_out[units, :] += left_t(act.astype(LOWTYPE), d_y)
            d_in[:, units] += left_t(rows, d_h)


def whole(shape):
    return pl.BlockSpec(shape, lambda e: (0,) * len(shape))


def gridded(kernel, steps, in_specs, outs, out_specs, args, flops, scratch=()):
    moved = sum(math.prod(a.shape) * a.dtype.itemsize for a in (*args, *outs))
    return pl.pallas_call(
        kernel,
        grid=(steps,),
        out_shape=outs,
        in_specs=in_specs,
        out_specs=out_specs,
        scratch_shapes=scratch,
        compiler_params=pltpu.CompilerParams(vmem_limit_bytes=VMEM_LIMIT),
        cost_estimate=pl.CostEstimate(flops=flops, bytes_accessed=moved, transcendentals=0),
    )(*args)


SCALARS = pl.BlockSpec(memory_space=pltpu.SMEM)


def in_spec(w_in):
    return pl.BlockSpec((1,) + w_in.shape[1:], lambda e: (e, 0, 0, 0))


def out_spec(w_out):
    return pl.BlockSpec((1,) + w_out.shape[1:], lambda e: (e, 0, 0))


def spread_spec(seq):
    return pl.BlockSpec((1, seq, 128), lambda e: (e, 0, 0))


def taken_spec(seq):
    return pl.BlockSpec((1, seq, D), lambda e: (e, 0, 0))


def block_shapes(experts, capacity):
    return [shaped((experts, SLOTS, D), LOWTYPE)] * (capacity // SLOTS)


def block_specs(capacity):
    return [pl.BlockSpec((1, SLOTS, D), lambda e: (e, 0, 0))] * (capacity // SLOTS)


def moe_up(loads, c16, router, table, place, w_in, capacity):
    seq, experts = table.shape
    hidden = w_in.shape[1] * w_in.shape[3]
    per = lambda width: pl.BlockSpec((capacity, width), lambda e: (e, 0))
    return gridded(
        moe_up_kernel,
        experts,
        [SCALARS, whole((seq, D)), whole((D, experts)), whole((seq, experts))]
        + [pl.BlockSpec((1, 1, seq), lambda e: (e, 0, 0)), in_spec(w_in)],
        [
            shaped((seq, experts), FULLTYPE),
            shaped((experts, seq, 128), FULLTYPE),
            shaped((experts, seq, 128), FULLTYPE),
            shaped((experts * capacity, hidden), LOWTYPE),
            shaped((experts * capacity, hidden), FULLTYPE),
        ]
        + block_shapes(experts, capacity),
        [whole((seq, experts)), spread_spec(seq), spread_spec(seq), per(hidden), per(hidden)]
        + block_specs(capacity),
        [loads, c16, router, table, place, w_in],
        2 * experts * capacity * D * (hidden + seq),
    )


def moe_down(loads, mid, spread_place, spread_gate, act, w_out):
    seq, experts = (mid.shape[0], w_out.shape[0])
    capacity, hidden = (act.shape[0] // experts, act.shape[1])
    per = lambda width: pl.BlockSpec((capacity, width), lambda e: (e, 0))
    return gridded(
        moe_down_kernel,
        experts,
        [SCALARS, whole((seq, D)), spread_spec(seq), spread_spec(seq), per(hidden), out_spec(w_out)],
        [shaped((seq, D), FULLTYPE), shaped((experts, seq, D), LOWTYPE)],
        [whole((seq, D)), taken_spec(seq)],
        [loads, mid, spread_place, spread_gate, act, w_out],
        2 * experts * capacity * D * (hidden + seq),
        [pltpu.VMEM((capacity, D), LOWTYPE)],
    )


def moe_gate_backward(loads, grad, c16, router, gates, place, spread_gate, taken, capacity):
    seq, experts = gates.shape
    return gridded(
        moe_gate_kernel,
        experts,
        [SCALARS, whole((seq, D)), whole((seq, D)), whole((D, experts)), whole((seq, experts))]
        + [pl.BlockSpec((1, 1, seq), lambda e: (e, 0, 0)), spread_spec(seq), taken_spec(seq)],
        [
            shaped((D, experts), FULLTYPE),
            shaped((seq, D), FULLTYPE),
        ]
        + block_shapes(experts, capacity),
        [whole((D, experts)), whole((seq, D))] + block_specs(capacity),
        [loads, grad, c16, router, gates, place, spread_gate, taken],
        4 * experts * capacity * D * seq,
        [
            pltpu.VMEM((seq, D), LOWTYPE),
            pltpu.VMEM((seq, experts), LOWTYPE),
            pltpu.VMEM((seq, experts), FULLTYPE),
        ],
    )


def moe_backward(loads, start, spread_place, w_in, w_out, dy, slope):
    seq, experts = (start.shape[0], w_out.shape[0])
    capacity, hidden = (slope.shape[0] // experts, w_out.shape[1])
    per = lambda width: pl.BlockSpec((capacity, width), lambda e: (e, 0))
    return gridded(
        moe_backward_kernel,
        experts,
        [SCALARS, whole((seq, D)), spread_spec(seq), in_spec(w_in), out_spec(w_out)]
        + [per(hidden)]
        + block_specs(capacity),
        [shaped((seq, D), FULLTYPE)],
        [whole((seq, D))],
        [loads, start, spread_place, w_in, w_out, slope, *dy],
        2 * experts * capacity * D * (2 * hidden + seq),
        [pltpu.VMEM((capacity, D), LOWTYPE)],
    )[0]


def moe_weight_backward(rows, dy, w_in, w_out):
    count, width = (rows[0].shape[0], w_in.shape[1])
    step = 512
    per = pl.BlockSpec((step, D), lambda i: (i, 0))
    return gridded(
        functools.partial(moe_weight_kernel, len(rows)),
        count // step,
        [per] * (2 * len(rows)) + [whole((D, width)), whole((width, D))],
        [shaped((D, width), FULLTYPE), shaped((width, D), FULLTYPE)],
        [whole((D, width)), whole((width, D))],
        [*rows, *dy, w_in, w_out],
        10 * count * len(rows) * D * width,
    )


def flat_plan(experts):
    shapes = [(PIX, D)] + [(D, 3 * D)] * 3 + [(D, D)] * 3 + [(D, FF)] * 2 + [(FF, D)] * 2
    plan, start = [], 0
    for height, width in shapes:
        plan.append((start, height, width // 128))
        start += height * width // 128
    return (plan, start)


def owner_rows(shard, parts):
    return -(-((shard + 127 + 127) // 128) // (16 * parts)) * 16 * parts


def chunk_of(rows, most=128):
    return max(c for c in range(16, most + 1, 16) if rows % c == 0)


def unpack_kernel(plan, shard, owners, orders, place_ref, *refs):
    chains = len(orders)
    own, other = (refs[:chains], refs[chains : 2 * chains])
    refs = refs[2 * chains :]
    outs, rest, flat = (refs[: len(plan)], refs[len(plan)], refs[len(plan) + 1])
    sizes = [ref.shape[0] // owners for ref in own]
    mine, core = (place_ref[0], place_ref[1])

    def collect(owner, carry):
        first = shard * owner // 128
        last = flat[pl.ds(jnp.maximum(first, 0), 1), :]
        shared = jnp.where(lax.rem(shard * owner, 128) == 0, 0.0, 1.0)
        for half in (0, 1):
            for chain, order in enumerate(orders):
                away = jnp.bitwise_xor(mine, owner)
                slot = sum(
                    jnp.bitwise_and(away // bit, 1) * 2**k for k, bit in enumerate(order)
                )
                size, before = (sizes[chain], half * sum(sizes) + sum(sizes[:chain]))
                source = pl.ds(pl.multiple_of(slot * size, 16), size)
                target = pl.ds(first + before, size)
                for ref, wanted in ((own[chain], core == half), (other[chain], core != half)):

                    @pl.when(wanted)
                    def _(ref=ref, source=source, target=target):
                        flat[target, :] = ref[source, :].astype(FULLTYPE)

        flat[pl.ds(first, 1), :] += last * shared
        return carry

    flat[0:8, :] = jnp.zeros((8, 128), FULLTYPE)
    lax.fori_loop(0, owners, collect, 0)
    spread_flat(plan, flat, outs, rest)


def unpack_parts_kernel(plan, shard, parts_ref, *refs):
    outs, rest, flat = (refs[: len(plan)], refs[len(plan)], refs[len(plan) + 1])
    owners, rows = parts_ref.shape[:2]
    chunk = chunk_of(rows)
    for owner in range(owners):
        first = shard * owner // 128
        if owner:
            last = flat[pl.ds(first, 1), :]

        def copy(i, carry, owner=owner, first=first):
            flat[pl.ds(first + i * chunk, chunk), :] = parts_ref[
                owner, pl.ds(pl.multiple_of(i * chunk, chunk), chunk), :
            ].astype(FULLTYPE)
            return carry

        lax.fori_loop(0, rows // chunk, copy, 0)
        if owner and shard * owner % 128:
            flat[pl.ds(first, 1), :] += last
    spread_flat(plan, flat, outs, rest)


def spread_flat(plan, flat, outs, rest):
    for (start, height, across), out in zip(plan, outs):

        def place(i, carry, start=start, across=across, out=out):
            for c in range(across):
                taken = flat[pl.ds(start + i * 128 * across + c, 128, stride=across), :]
                out[rows_of(i, 128), pl.ds(c * 128, 128)] = taken.astype(LOWTYPE)
            return carry

        lax.fori_loop(0, height // 128, place, 0)
    start = plan[-1][0] + plan[-1][1] * plan[-1][2]
    rest[...] = flat[pl.ds(start, rest.shape[0]), :]


ORDERS = ((4, 8, 1, 2), (4, 8, 2, 1))


def chain_sizes(rows):
    units = rows // 16
    return [16 * (units // 2), 16 * (units - units // 2)]


def gather_weights(part, shard, ep_place, dp_place, experts, beside):
    plan, start = flat_plan(experts)
    owners, groups = (lax.axis_size("ep"), lax.axis_size("dp"))
    rows = owner_rows(shard, groups)
    outs = [shaped((height, across * 128), LOWTYPE) for _, height, across in plan]
    outs.append(shaped((shard * owners // 128 - start, 128), FULLTYPE))
    flat = pltpu.VMEM((-(-(shard * (owners - 1) // 128 + rows) // 8) * 8, 128), FULLTYPE)
    if (owners, groups) != (16, 2) or part.shape[0] < 32:
        parts = lax.all_gather(part, ("ep", "dp")).reshape(owners, rows, 128)
        kernel, args = (functools.partial(unpack_parts_kernel, plan, shard), [parts])
        return (local_call(kernel, outs, args, 0, [flat]), beside[0](*beside[1]))
    sizes = chain_sizes(part.shape[0])
    chains = [part[sum(sizes[:c]) : sum(sizes[: c + 1])] for c in range(len(ORDERS))]
    work, inputs = beside
    for step in range(len(ORDERS[0])):
        got = [
            lax.ppermute(v, "ep", [(i, i ^ order[step]) for i in range(owners)])
            for v, order in zip(chains, ORDERS)
        ]
        if step == len(ORDERS[0]) - 2:
            got, inputs = lax.optimization_barrier((got, inputs))
        elif step == len(ORDERS[0]) - 1:
            got, results = lax.optimization_barrier((got, work(*inputs)))
        else:
            got = lax.optimization_barrier(got)
        chains = [jnp.concatenate([v, g]) for v, g in zip(chains, got)]
    args = [jnp.stack([ep_place, dp_place]).astype(jnp.int32), *chains, *map(swap_dp, chains)]
    moved = sum(math.prod(a.shape) * a.dtype.itemsize for a in (*args, *outs))
    mats = pl.pallas_call(
        functools.partial(unpack_kernel, plan, shard, owners, ORDERS),
        out_shape=outs,
        in_specs=[SCALARS] + in_vmem(len(args) - 1),
        out_specs=in_vmem(len(outs)),
        scratch_shapes=[flat],
        compiler_params=pltpu.CompilerParams(vmem_limit_bytes=VMEM_LIMIT),
        cost_estimate=pl.CostEstimate(flops=0, bytes_accessed=moved, transcendentals=0),
    )(*args)
    return (mats, results)


def pack_kernel(plan, shard, select, place_ref, *refs):
    count = len(plan)
    mats, rest, norms = (refs[:count], refs[count], refs[count + 1 : count + 5])
    outs, flat = (refs[count + 5 : -1], refs[-1])
    for (start, height, across), mat in zip(plan, mats):

        def place(i, carry, start=start, across=across, mat=mat):
            for c in range(across):
                flat[pl.ds(start + i * 128 * across + c, 128, stride=across), :] = mat[
                    rows_of(i, 128), pl.ds(c * 128, 128)
                ]
            return carry

        lax.fori_loop(0, height // 128, place, 0)
    start = plan[-1][0] + plan[-1][1] * plan[-1][2]
    flat[pl.ds(start, rest.shape[0]), :] = rest[...]
    start += rest.shape[0]
    for kind in (0, 1):
        for layer, norm in enumerate(norms):
            for k in range(2 if layer < 3 else 1):
                for c in range(D // 128):
                    row = start + ((7 * kind + 2 * layer + k) * D) // 128 + c
                    flat[row : row + 1, :] = norm[2 * k + kind : 2 * k + kind + 1, c * 128 : c * 128 + 128]
    for out, which in zip(outs, select):
        groups, owners, rows = out.shape[:3]
        chunk = chunk_of(rows)
        for group in range(groups):
            for owner in range(owners):
                member = which(place_ref[0], group)
                first = shard * owner // 128 + member * rows

                def copy(i, carry, out=out, group=group, owner=owner, first=first):
                    out[group, owner, pl.ds(pl.multiple_of(i * chunk, chunk), chunk), :] = flat[
                        pl.ds(first + i * chunk, chunk), :
                    ].astype(out.dtype)
                    return carry

                lax.fori_loop(0, rows // chunk, copy, 0)


def pack_gradients(mats, rest, norms, shard, owners, groups, place, experts):
    plan, _ = flat_plan(experts)
    rows = owner_rows(shard, groups)
    part = rows // groups
    if groups == 2:
        outs = [shaped((1, owners, part, 128), t) for t in (FULLTYPE, EXCHANGE)]
        select = [lambda here, g: here, lambda here, g: 1 - here]
    else:
        outs = [shaped((groups, owners, part, 128), FULLTYPE)]
        select = [lambda here, g: g]
    flat = pltpu.VMEM((-(-(shard * (owners - 1) // 128 + rows) // 8) * 8, 128), FULLTYPE)
    args = [place.reshape(1), *mats, rest, *norms]
    moved = sum(math.prod(a.shape) * a.dtype.itemsize for a in (*args, *outs))
    return pl.pallas_call(
        functools.partial(pack_kernel, plan, shard, select),
        out_shape=outs,
        in_specs=[SCALARS] + in_vmem(len(args) - 1),
        out_specs=in_vmem(len(outs)),
        scratch_shapes=[flat],
        compiler_params=pltpu.CompilerParams(vmem_limit_bytes=PACK_LIMIT),
        cost_estimate=pl.CostEstimate(flops=0, bytes_accessed=moved, transcendentals=0),
    )(*args)


EXCHANGE = jnp.bfloat16
PACK_LIMIT = 60 * 2**20


def swap_dp(value):
    return lax.ppermute(value, "dp", [(0, 1), (1, 0)])


def join_dp(value, place):
    groups = lax.axis_size("dp")
    if groups != 2:
        return lax.all_gather(value, "dp")
    other = swap_dp(value)
    first = place == 0
    return jnp.stack([jnp.where(first, value, other), jnp.where(first, other, value)])


def sum_scatter_dp(parts, place):
    groups = lax.axis_size("dp")
    if groups != 2:
        return lax.psum_scatter(parts, "dp", scatter_dimension=0, tiled=True)[0]
    first = place == 0
    mine = jnp.where(first, parts[0], parts[1])
    return mine + swap_dp(jnp.where(first, parts[1], parts[0]))


def sum_all(value):
    for axis in ("dp", "ep"):
        count = lax.axis_size(axis)
        step = 1
        while step < count:
            value = value + lax.ppermute(value, axis, [(i, i ^ step) for i in range(count)])
            step *= 2
    return value


def to_experts(buffer):
    return lax.all_to_all(buffer, "ep", split_axis=0, concat_axis=0, tiled=True)


def per_device(
    patches,
    labels,
    pixel_mask,
    patch_valid,
    tasks,
    routes,
    dense_weight,
    dense_first,
    dense_second,
    dense_average,
    expert_in,
    in_first,
    in_second,
    in_average,
    expert_out,
    out_first,
    out_second,
    out_average,
):
    ep_count = lax.axis_size("ep")
    experts = min(16, ep_count)
    copies = ep_count // experts
    groups = lax.axis_size("dp")
    ep_place = lax.axis_index("ep")
    dp_place = lax.axis_index("dp")
    own_expert = ep_place // copies
    seq = patches.shape[0]
    capacity = 3 * seq * TOP // (2 * experts)
    shard = dense_weight.shape[0]
    piece = shard // groups
    edges = segment_edges(experts)
    block_count = len(edges) + 1 + 2 * experts
    span, firsts = owner_blocks(edges, shard, ep_count)
    first_block = firsts[ep_place]
    starts = [
        jnp.take(jnp.array([0] + edges + [shard * ep_count] * span, jnp.int32), first_block + k)
        - ep_place * shard
        for k in range(span + 1)
    ]

    def placed(value, at, count):
        return jnp.where(jnp.arange(count) == at, value, 0.0)

    def block_sums(dense_vals, in_vals, out_vals):
        part = lax.dynamic_slice_in_dim(dense_vals, dp_place * piece, piece)
        square = part * part
        index = dp_place * piece + jnp.arange(piece, dtype=jnp.int32)
        listed = placed(jnp.sum(in_vals * in_vals), len(edges) + 1 + own_expert, block_count)
        listed += placed(
            jnp.sum(out_vals * out_vals), len(edges) + 1 + experts + own_expert, block_count
        )
        for k in range(span):
            inside = (index >= starts[k]) & (index < starts[k + 1])
            listed += placed(jnp.sum(jnp.where(inside, square, 0.0)), first_block + k, block_count)
        return listed

    rows = owner_rows(shard, groups)
    offset = lax.rem(ep_place * (shard % 128), 128)
    spread = lax.dynamic_update_slice(
        jnp.zeros((rows * 128,), LOWTYPE), dense_weight.astype(LOWTYPE), (offset,)
    )
    own_part = lax.dynamic_index_in_dim(
        spread.reshape(groups, rows // groups, 128), dp_place, 0, keepdims=False
    )
    low_in, low_out = (expert_in[0].astype(LOWTYPE), expert_out[0].astype(LOWTYPE))
    all_in = lax.all_gather(low_in, ("ep", "dp"))
    all_out = lax.all_gather(low_out, ("ep", "dp"))
    width = low_in.shape[1]
    w_out = all_out.reshape(experts, copies * groups * width, D)

    together = lax.optimization_barrier

    def prepare(labels, pixel_mask, patch_valid, routes, weights):
        named = jnp.sum(
            (routes[:, :, None] == jnp.arange(experts, dtype=jnp.int32)[None, None, :]).astype(FULLTYPE),
            1,
        )
        earlier = jnp.arange(seq)[:, None] > jnp.arange(seq)[None, :]
        table = jnp.where(named > 0, plain(earlier.astype(LOWTYPE), named.astype(LOWTYPE)), -1.0)
        weight_pix = (pixel_mask * patch_valid[:, None]).astype(FULLTYPE)
        class_hot = labels[:, :, None] == jnp.arange(C, dtype=jnp.int32)[None, None, :]
        return (
            table,
            table.T.reshape(experts, 1, seq),
            jnp.sum(named, 0).astype(jnp.int32),
            jnp.where(patch_valid > 0, 0.0, NEG).astype(FULLTYPE).reshape(seq, 1),
            jnp.sum(weight_pix, 1),
            jnp.sum(jnp.where(class_hot, weight_pix[:, :, None], 0.0), 1),
            block_sums(*weights),
        )

    (*mats, rest), prepared = gather_weights(
        own_part,
        shard,
        ep_place,
        dp_place,
        experts,
        (
            prepare,
            (labels, pixel_mask, patch_valid, routes, (dense_weight, expert_in, expert_out)),
        ),
    )
    table, place, loads, down, count_tok, counts, weight_sums = prepared
    first_block, starts, table = together((first_block, starts, table))
    steps = [(axis, 2**k) for axis in ("dp", "ep") for k in range(lax.axis_size(axis).bit_length() - 1)]
    fourth = -(-len(steps) // 4)

    def add_steps(value, turn):
        for axis, step in steps[turn * fourth : (turn + 1) * fourth]:
            count = lax.axis_size(axis)
            value = value + lax.ppermute(value, axis, [(i, i ^ step) for i in range(count)])
        return value

    total = add_steps(jnp.sum(count_tok).reshape(1), 0)
    w_patch, w_qkv, w_attn = (mats[0], mats[1:4], mats[4:7])
    w_up, w_down = (mats[7:9], mats[9:11])
    router_rows, head_rows = (TASKS * D * experts // 128, D * C // 128)
    w_router = rest[:router_rows].reshape(TASKS, D, experts).astype(LOWTYPE)
    w_head = rest[router_rows : router_rows + head_rows].reshape(D, C).astype(LOWTYPE)
    norms = rest[router_rows + head_rows :].reshape(2, 7, D)
    task = tasks[0]
    router = lax.dynamic_index_in_dim(w_router, task, 0, keepdims=False)

    def dispatch(send):
        return to_experts(jnp.repeat(send, copies, axis=0)).reshape(-1, D)

    together = lax.optimization_barrier

    def norm_rows(layer):
        rows = [norms[0, 2 * layer], norms[1, 2 * layer]]
        if layer < 3:
            rows += [norms[0, 2 * layer + 1], norms[1, 2 * layer + 1]]
        return jnp.pad(jnp.stack(rows), ((0, 8 - len(rows)), (0, 0)))

    x0, *kept0, x1, act0, slope0 = layer_forward(
        patches, w_patch, w_qkv[0], w_attn[0], norm_rows(0), down, w_up[0], w_down[0]
    )
    x1, all_in, total = together((x1, all_in, total))
    total = add_steps(total, 1)
    mid1, c16, *kept1 = layer_forward(
        x1, None, w_qkv[1], w_attn[1], norm_rows(1), down, None, None
    )
    c16, total = together((c16, total))
    total = add_steps(total, 2)
    w_in = all_in.reshape(experts, copies * groups, D, width)
    if width % 128:
        w_in = jnp.swapaxes(w_in, 1, 2).reshape(experts, 1, D, copies * groups * width)
    gates, spread_place, spread_gate, act1, slope1, *sent = moe_up(
        loads, c16, router, table, place, w_in, capacity
    )
    x2, taken = moe_down(loads, mid1, spread_place, spread_gate, act1, w_out)
    x2, sent, total = together((x2, sent, total))
    total = add_steps(total, 3)
    rows_a = dispatch(sent[0])
    *kept2, x3, act2, slope2 = layer_forward(
        x2, None, w_qkv[2], w_attn[2], norm_rows(2), down, w_up[1], w_down[1]
    )
    loss_lanes, d_head, d_normf, grad = head_call(
        x3, norm_rows(3), w_head, counts, count_tok, total
    )
    local = loss_lanes[0, 0]
    grad, local, sent, rows_a = together((grad, local, sent, rows_a))
    rows_b = dispatch(sent[1])
    d_qkv2, d_attn2, d_norm2, d_up1, d_down1, grad = layer_backward(
        grad, x2, (*kept2, act2, slope2), w_qkv[2], w_attn[2], norm_rows(2), down,
        (w_up[1], w_down[1]), None, None,
    )
    grad, sent, rows_b = together((grad, sent, rows_b))
    rows_c = dispatch(sent[2])
    d_own_router, d_c, *dy16 = moe_gate_backward(
        loads, grad, c16, router, gates, place, spread_gate, taken, capacity
    )
    d_c, dy16, rows_c = together((d_c, dy16, rows_c))
    dy_a = dispatch(dy16[0])
    d_c = moe_backward(loads, d_c, spread_place, w_in, w_out, dy16, slope1)
    d_c, dy16, dy_a = together((d_c, dy16, dy_a))
    dy_b = dispatch(dy16[1])
    task_hot = (jnp.arange(TASKS, dtype=jnp.int32) == task)[:, None, None]
    d_router = jnp.where(task_hot, d_own_router[None], 0.0)
    d_qkv1, d_attn1, d_norm1, grad = layer_backward(
        grad, x1, (mid1, c16, *kept1), w_qkv[1], w_attn[1], norm_rows(1), down, None, d_c, None
    )
    grad, dy16, dy_b = together((grad, dy16, dy_b))
    dy_c = dispatch(dy16[2])
    d_qkv0, d_attn0, d_norm0, d_up0, d_down0, d_patch = layer_backward(
        grad, x0, (*kept0, act0, slope0), w_qkv[0], w_attn[0], norm_rows(0), down,
        (w_up[0], w_down[0]), None, patches,
    )
    d_patch, dy_c = together((d_patch, dy_c))
    expert_rows, expert_dy = ([rows_a, rows_b, rows_c], [dy_a, dy_b, dy_c])
    d_rest = jnp.concatenate(
        [
            d_router.reshape(router_rows, 128),
            d_head[:, :C].reshape(head_rows, 128),
        ]
    )
    packed = pack_gradients(
        [d_patch, d_qkv0, d_qkv1, d_qkv2, d_attn0, d_attn1, d_attn2, d_up0, d_up1, d_down0, d_down1],
        d_rest, [d_norm0, d_norm1, d_norm2, d_normf], shard, ep_count, groups, dp_place, experts,
    )
    if groups == 2:
        summed = packed[0][0] + swap_dp(packed[1][0]).astype(FULLTYPE)
    else:
        summed = lax.psum_scatter(packed[0], "dp", scatter_dimension=0, tiled=True)[0]
    arrived = to_experts(summed.astype(LOWTYPE))

    own_in = lax.dynamic_index_in_dim(
        all_in.reshape(ep_count, groups, D, width), ep_place, 0, keepdims=False
    )
    own_out = lax.dynamic_index_in_dim(
        all_out.reshape(ep_count, groups, width, D), ep_place, 0, keepdims=False
    )
    if groups == 2:

        def weight_grads(member):
            return moe_weight_backward(
                expert_rows,
                expert_dy,
                lax.dynamic_index_in_dim(own_in, member, 0, keepdims=False),
                lax.dynamic_index_in_dim(own_out, member, 0, keepdims=False),
            )

        theirs = weight_grads(1 - dp_place)
        away = [swap_dp(t.astype(jnp.bfloat16)) for t in theirs]
        mine = weight_grads(dp_place)
        mine, away, arrived = together((mine, away, arrived))
        d_in, d_out = [(m + t.astype(FULLTYPE))[None] for m, t in zip(mine, away)]
    else:
        d_in, d_out = moe_weight_backward(
            expert_rows,
            expert_dy,
            jnp.swapaxes(own_in, 0, 1).reshape(D, groups * width),
            own_out.reshape(groups * width, D),
        )
        d_in, d_out = (
            lax.psum_scatter(
                value[None].astype(jnp.bfloat16), "dp", scatter_dimension=axis, tiled=True
            ).astype(FULLTYPE)
            for value, axis in ((d_in, 2), (d_out, 1))
        )
    own_sum = jnp.sum(arrived.astype(FULLTYPE), 0)
    dense_grad = lax.dynamic_slice_in_dim(
        join_dp(own_sum, dp_place).reshape(-1), offset, shard
    )
    own_grad = lax.dynamic_slice_in_dim(dense_grad, dp_place * piece, piece)
    sums = sum_all(
        together(placed(local, 0, 2 + block_count)
        + placed(jnp.sum(own_grad * own_grad) + jnp.sum(d_in * d_in) + jnp.sum(d_out * d_out), 1, 2 + block_count)
        + jnp.pad(weight_sums, (2, 0)))
    )
    loss, grad_total, weight_total = (sums[0] / total, sums[1], sums[2:])
    grad_norm = jnp.sqrt(grad_total)
    clip = CLIP_NORM / jnp.maximum(grad_norm, CLIP_NORM)

    def moments(weight, first, second, gradient):
        gradient = gradient * clip
        first_new = DECAY_ONE * first + (1.0 - DECAY_ONE) * gradient
        second_new = DECAY_TWO * second + (1.0 - DECAY_TWO) * gradient * gradient
        return (
            first_new,
            second_new,
            first_new / (jnp.sqrt(second_new) + EPS_ADAM) + WEIGHT_DECAY * weight,
        )

    dense_m, dense_v, dense_step = moments(dense_weight, dense_first, dense_second, dense_grad)
    in_m, in_v, in_step = moments(expert_in, in_first, in_second, d_in)
    out_m, out_v, out_step = moments(expert_out, out_first, out_second, d_out)
    update_total = sum_all(together(block_sums(dense_step, in_step, out_step)))
    weight_norm = jnp.sqrt(weight_total)
    update_norm = jnp.sqrt(update_total)
    ratio = weight_norm / (update_norm + EPS_NORM)
    whole_index = jnp.arange(shard, dtype=jnp.int32)
    dense_ratio = jnp.broadcast_to(jnp.take(ratio, first_block), (shard,))
    for k in range(1, span):
        dense_ratio = jnp.where(whole_index >= starts[k], jnp.take(ratio, jnp.minimum(first_block + k, block_count - 1)), dense_ratio)
    in_ratio = lax.dynamic_index_in_dim(ratio, 14 + own_expert, 0, keepdims=False)
    out_ratio = lax.dynamic_index_in_dim(ratio, 14 + experts + own_expert, 0, keepdims=False)

    def finish(weight, average, step, rate):
        new = weight - RATE * rate * step
        return (new, AVERAGE * average + (1.0 - AVERAGE) * new, new.astype(LOWTYPE))

    dense_new, dense_avg, dense_low = finish(dense_weight, dense_average, dense_step, dense_ratio)
    in_new, in_avg, in_low = finish(expert_in, in_average, in_step, in_ratio)
    out_new, out_avg, out_low = finish(expert_out, out_average, out_step, out_ratio)
    block_norms = jnp.stack([weight_norm, update_norm], 1)
    return (
        loss.reshape(1),
        grad_norm.reshape(1),
        block_norms,
        dense_new,
        dense_m,
        dense_v,
        dense_avg,
        dense_low,
        in_new,
        in_m,
        in_v,
        in_avg,
        in_low,
        out_new,
        out_m,
        out_v,
        out_avg,
        out_low,
    )


def solution(mesh):
    in_specs = (
        P(("ep", "dp"), None),
        P(("ep", "dp"), None),
        P(("ep", "dp"), None),
        P(("ep", "dp")),
        P(("ep", "dp")),
        P(("ep", "dp"), None),
        P("ep"),
        P("ep"),
        P("ep"),
        P("ep"),
        P("ep", None, "dp"),
        P("ep", None, "dp"),
        P("ep", None, "dp"),
        P("ep", None, "dp"),
        P("ep", "dp", None),
        P("ep", "dp", None),
        P("ep", "dp", None),
        P("ep", "dp", None),
    )
    out_specs = (
        P(),
        P(),
        P(),
        P("ep"),
        P("ep"),
        P("ep"),
        P("ep"),
        P("ep"),
        P("ep", None, "dp"),
        P("ep", None, "dp"),
        P("ep", None, "dp"),
        P("ep", None, "dp"),
        P("ep", None, "dp"),
        P("ep", "dp", None),
        P("ep", "dp", None),
        P("ep", "dp", None),
        P("ep", "dp", None),
        P("ep", "dp", None),
    )
    return jax.shard_map(
        per_device, mesh=mesh, in_specs=in_specs, out_specs=out_specs, check_vma=False
    )
```
